128 devices in a mesh: section: 4 (over y_lo, core), tensor: 8 (over y_hi, z), dp: 4 (over x).
Axes of the slice: x: 4, y: 4 (y_hi: 2, y_lo: 2; y = y_hi * 2 + y_lo), z: 4, core: 2. Of those that a mesh axis runs over, the one named last changes fastest.
Arguments:
- tokens: int32 [16, 1025], P('dp'), may hold values from 0 to 50303
- groups: int32 [16], replicated, may hold values from 0 to 7
- counts: int32 [4], replicated, may hold values from 1 to 4, as said below
- domain: float32 [8], replicated, may hold values from 0.25 to 4
- w_in: float32 [4, 512, 3584], P('section', None, 'tensor'), may hold values from -0.25 to 0.25
- w_back: float32 [4, 2560, 512], P('section', 'tensor'), may hold values from -0.375 to 0.375
- tables: float32 [2, 50304, 512], P(None, ('section', 'tensor'), 'dp')
- b_in: float32 [4, 3584], P('section', 'tensor'), may hold values from -1.5 to 1.5
- vecs: float32 [4, 6, 512], P('section')
- final_norm: float32 [2, 512], replicated
- w_in_mom: float32 [4, 512, 3584], P('section', None, 'tensor'), may hold values from -0.0012207031 to 0.0012207031
- w_back_mom: float32 [4, 2560, 512], P('section', 'tensor'), may hold values from -0.0012207031 to 0.0012207031
- tables_mom: float32 [2, 50304, 512], P(None, ('section', 'tensor'), 'dp'), may hold values from -1.5258789e-05 to 1.5258789e-05
- b_in_mom: float32 [4, 3584], P('section', 'tensor'), may hold values from -0.0012207031 to 0.0012207031
- vecs_mom: float32 [4, 6, 512], P('section'), may hold values from -0.0012207031 to 0.0012207031
- final_mom: float32 [2, 512], replicated, may hold values from -0.0012207031 to 0.0012207031
- w_in_ema: float32 [4, 512, 3584], P('section', None, 'tensor'), may hold values from -0.25 to 0.25
- w_back_ema: float32 [4, 2560, 512], P('section', 'tensor'), may hold values from -0.375 to 0.375
- tables_ema: float32 [2, 50304, 512], P(None, ('section', 'tensor'), 'dp'), may hold values from -4 to 4
- b_in_ema: float32 [4, 3584], P('section', 'tensor'), may hold values from -1.5 to 1.5
- vecs_ema: float32 [4, 6, 512], P('section')
- final_ema: float32 [2, 512], replicated
- w_in_err: float32 [4, 4, 512, 3584], P('dp', 'section', None, 'tensor'), may hold values from -0.01171875 to 0.01171875
- w_back_err: float32 [4, 4, 2560, 512], P('dp', 'section', 'tensor'), may hold values from -0.01171875 to 0.01171875
- tables_err: float32 [4, 2, 50304, 512], P('dp', None, ('section', 'tensor')), may hold values from -0.00010681152 to 0.00010681152
- w_in_fac: float32 [4, 3584, 8], P('section', 'tensor'), may hold values from -6 to 6
- w_back_fac: float32 [4, 2560, 8], P('section', 'tensor'), may hold values from -6 to 6
- tables_fac: float32 [2, 50304, 8], P(None, ('section', 'tensor')), may hold values from -6 to 6
Outputs:
- loss_sum: float32 [], replicated
- weight_total: float32 [], replicated
- w_in_new: float32 [4, 512, 3584], P('section', None, 'tensor')
- w_back_new: float32 [4, 2560, 512], P('section', 'tensor')
- tables_new: float32 [2, 50304, 512], P(None, ('section', 'tensor'), 'dp')
- b_in_new: float32 [4, 3584], P('section', 'tensor')
- vecs_new: float32 [4, 6, 512], P('section')
- final_new: float32 [2, 512], replicated
- w_in_mom_new: float32 [4, 512, 3584], P('section', None, 'tensor')
- w_back_mom_new: float32 [4, 2560, 512], P('section', 'tensor')
- tables_mom_new: float32 [2, 50304, 512], P(None, ('section', 'tensor'), 'dp')
- b_in_mom_new: float32 [4, 3584], P('section', 'tensor')
- vecs_mom_new: float32 [4, 6, 512], P('section')
- final_mom_new: float32 [2, 512], replicated
- w_in_ema_new: float32 [4, 512, 3584], P('section', None, 'tensor')
- w_back_ema_new: float32 [4, 2560, 512], P('section', 'tensor')
- tables_ema_new: float32 [2, 50304, 512], P(None, ('section', 'tensor'), 'dp')
- b_in_ema_new: float32 [4, 3584], P('section', 'tensor')
- vecs_ema_new: float32 [4, 6, 512], P('section')
- final_ema_new: float32 [2, 512], replicated
- w_in_err_new: float32 [4, 4, 512, 3584], P('dp', 'section', None, 'tensor')
- w_back_err_new: float32 [4, 4, 2560, 512], P('dp', 'section', 'tensor')
- tables_err_new: float32 [4, 2, 50304, 512], P('dp', None, ('section', 'tensor'))
- w_in_fac_new: float32 [4, 3584, 8], P('section', 'tensor')
- w_back_fac_new: float32 [4, 2560, 8], P('section', 'tensor')
- embed_fac_new: float32 [50304, 8], P(('section', 'tensor'))
- head_fac_new: float32 [50304, 8], P(('section', 'tensor'))
The draws below stay inside these ranges and needn't reach their ends.
Inputs may be any that keep to these rules, and one draw needn't show every extreme that they name: Replica r trains on its first counts[r] sequences; the last replica trains on all 4, the first on at most 2.
All inputs are finite; a program needn't handle non-finite values.
Results may differ from the reference program's by a relative error of at most 0.035.
Values may be sent and summed in bfloat16 or wider, within the bound.
A program may use at most 384 MiB of HBM per device.

```python
import math
import jax
import jax.numpy as jnp
from jax import lax

D = 512
HEADS = 8
HEAD = 64
ROT = 16
FF = 2048
VOCAB = 50304
LAYERS = 4
LENGTH = 1024
SEQ_REP = 4
RANK = 8
GROUPS = 8
STEP = 5
SEQS = 16
NIN = 3584
NBACK = 2560
N_SECTION = 4
N_TENSOR = 8
N_DP = 4


def draw_counts(key, part):
    middle = jax.random.randint(key, (N_DP,), 1, SEQ_REP + 1)
    first_count = jax.random.randint(jax.random.fold_in(key, 1), (), 1, SEQ_REP // 3 + 2)
    middle = middle.at[0].set(first_count).at[N_DP - 1].set(SEQ_REP)
    return middle.astype(jnp.int32)


def draw_tables(key, part):
    first_key, second_key = jax.random.split(jax.random.fold_in(key, 7))
    position = jnp.arange(VOCAB, dtype=jnp.float32)[:, None] / (VOCAB - 1)
    embed = jax.random.normal(first_key, (1, VOCAB, D), jnp.float32)
    head = jax.random.normal(second_key, (VOCAB, D), jnp.float32) * (1.0 + 2.0 * position)
    return jnp.concatenate([embed, (head / math.sqrt(D))[None]], 0)


def gain_rows(key, lead, pattern):
    gain_key, shift_key = jax.random.split(key)
    gains = jax.random.uniform(gain_key, (lead, len(pattern), D), jnp.float32, 0.7, 1.3)
    shifts = 0.3 * jax.random.normal(shift_key, (lead, len(pattern), D), jnp.float32)
    chooser = jnp.array(pattern, jnp.float32)[None, :, None]
    return chooser * gains + (1.0 - chooser) * shifts


def draw_vecs(key, part):
    return gain_rows(jax.random.fold_in(key, 11), LAYERS, [1, 0, 1, 0, 0, 0])


def draw_final_norm(key, part):
    return gain_rows(jax.random.fold_in(key, 13), 1, [1, 0])[0]


def draw_vecs_ema(key, part):
    return gain_rows(jax.random.fold_in(key, 17), LAYERS, [1, 0, 1, 0, 0, 0])


def draw_final_ema(key, part):
    return gain_rows(jax.random.fold_in(key, 19), 1, [1, 0])[0]


def touch_ends(values, rng, smallest, largest):
    dims = values.shape
    spot = [jax.random.randint(jax.random.fold_in(rng, axis), (), 0, dims[axis]) for axis in range(len(dims))]
    values = values.at[tuple(spot)].set(smallest)
    longest = dims.index(max(dims))
    spot[longest] = (spot[longest] + 1) % dims[longest]
    return values.at[tuple(spot)].set(largest)


def level_of(rng, extent, cuts, least, largest):
    level = 1.0
    for axis_at, shards_of in cuts:
        steps = jax.random.uniform(jax.random.fold_in(jax.random.fold_in(rng, 6), axis_at), (shards_of,), jnp.float32, least / len(cuts), largest / len(cuts))
        level = level * jnp.repeat(jnp.exp(steps), extent[axis_at] // shards_of).reshape((-1,) + (1,) * (len(extent) - 1 - axis_at))
    return level


def noise(rng, dims, width, most, cuts=(), kind=jnp.bfloat16):
    level = level_of(rng, dims, cuts, -0.22, 0.18) if cuts else 1.0
    values = jax.random.normal(rng, dims, jnp.float32) * width * level
    return jnp.minimum(jnp.maximum(values, -most), most).astype(kind)


def setup_inputs(seed: int = 0) -> dict:
    key_of = jax.random.split(jax.random.key(seed), 29)
    return {
        "tokens": touch_ends(jax.random.randint(key_of[0], (SEQS, LENGTH + 1), 0, VOCAB), jax.random.fold_in(key_of[0], 1), 0, VOCAB - 1).astype(jnp.int32),
        "groups": touch_ends(jax.random.randint(key_of[1], (SEQS,), 0, GROUPS), jax.random.fold_in(key_of[1], 1), 0, GROUPS - 1).astype(jnp.int32),
        "counts": draw_counts(jax.random.fold_in(key_of[28], 71), 0),
        "domain": jnp.clip(jnp.exp(jax.random.uniform(key_of[3], (GROUPS,), jnp.float32, math.log(0.25), math.log(4.0))), 0.25, 4.0),
        "w_in": noise(key_of[4], (LAYERS, D, NIN), D ** -0.5, 0.25, ((0, 4), (2, 8)), jnp.float32),
        "w_back": noise(key_of[5], (LAYERS, NBACK, D), (D // 2) ** -0.5, 0.375, ((0, 4), (1, 8)), jnp.float32),
        "tables": draw_tables(jax.random.fold_in(key_of[28], 71), 0),
        "b_in": noise(key_of[7], (LAYERS, NIN), 0.3, 1.5, ((0, 4), (1, 8)), jnp.float32),
        "vecs": draw_vecs(jax.random.fold_in(key_of[28], 71), 0),
        "final_norm": draw_final_norm(jax.random.fold_in(key_of[28], 71), 0),
        "w_in_mom": noise(key_of[10], (LAYERS, D, NIN), (0.011 / (N_DP * SEQ_REP * LENGTH) ** 0.5), 0.0012207031, ((0, 4), (2, 8)), jnp.float32),
        "w_back_mom": noise(key_of[11], (LAYERS, NBACK, D), (0.011 / (N_DP * SEQ_REP * LENGTH) ** 0.5), 0.0012207031, ((0, 4), (1, 8)), jnp.float32),
        "tables_mom": noise(key_of[12], (2, VOCAB, D), (0.03 / (N_DP * SEQ_REP * LENGTH * VOCAB) ** 0.5), 1.52587890625e-05, ((1, 32), (2, 4)), jnp.float32),
        "b_in_mom": noise(key_of[13], (LAYERS, NIN), (0.011 / (N_DP * SEQ_REP * LENGTH) ** 0.5), 0.0012207031, ((0, 4), (1, 8)), jnp.float32),
        "vecs_mom": noise(key_of[14], (LAYERS, 6, D), (0.011 / (N_DP * SEQ_REP * LENGTH) ** 0.5), 0.0012207031, ((0, 4),), jnp.float32),
        "final_mom": noise(key_of[15], (2, D), (0.011 / (N_DP * SEQ_REP * LENGTH) ** 0.5), 0.0012207031, (), jnp.float32),
        "w_in_ema": noise(key_of[16], (LAYERS, D, NIN), D ** -0.5, 0.25, ((0, 4), (2, 8)), jnp.float32),
        "w_back_ema": noise(key_of[17], (LAYERS, NBACK, D), (D // 2) ** -0.5, 0.375, ((0, 4), (1, 8)), jnp.float32),
        "tables_ema": noise(key_of[18], (2, VOCAB, D), 0.5, 4.0, ((1, 32), (2, 4)), jnp.float32),
        "b_in_ema": noise(key_of[19], (LAYERS, NIN), 0.3, 1.5, ((0, 4), (1, 8)), jnp.float32),
        "vecs_ema": draw_vecs_ema(jax.random.fold_in(key_of[28], 71), 0),
        "final_ema": draw_final_ema(jax.random.fold_in(key_of[28], 71), 0),
        "w_in_err": noise(key_of[22], (N_DP, LAYERS, D, NIN), (0.1 / (N_DP * SEQ_REP * LENGTH) ** 0.5), 0.01171875, ((0, 4), (1, 4), (3, 8)), jnp.float32),
        "w_back_err": noise(key_of[23], (N_DP, LAYERS, NBACK, D), (0.1 / (N_DP * SEQ_REP * LENGTH) ** 0.5), 0.01171875, ((0, 4), (1, 4), (2, 8)), jnp.float32),
        "tables_err": noise(key_of[24], (N_DP, 2, VOCAB, D), (0.2 / (N_DP * SEQ_REP * LENGTH * VOCAB) ** 0.5), 0.00010681152, ((0, 4), (2, 32)), jnp.float32),
        "w_in_fac": noise(key_of[25], (LAYERS, NIN, RANK), 1.0, 6.0, ((0, 4), (1, 8)), jnp.float32),
        "w_back_fac": noise(key_of[26], (LAYERS, NBACK, RANK), 1.0, 6.0, ((0, 4), (1, 8)), jnp.float32),
        "tables_fac": noise(key_of[27], (2, VOCAB, RANK), 1.0, 6.0, ((1, 32),), jnp.float32),
    }


@jax.custom_vjp
def low(v):
    return lax.optimization_barrier(v.astype(jnp.bfloat16)).astype(jnp.float32)

@jax.custom_vjp
def low_back(v):
    return v

def low_keep(v):
    return (low(v), None)

def low_pass(kept, grad):
    return (grad,)

def back_keep(v):
    return (v, None)

def back_low(kept, grad):
    return (low(grad),)
low.defvjp(low_keep, low_pass)
low_back.defvjp(back_keep, back_low)
EPS_NORM = 1e-05
MOMENTUM = 0.9
NEG_BIG = -1e+30
HIGH = lax.Precision.HIGHEST

def ema_decay():
    return min(0.999, (1.0 + STEP) / (10.0 + STEP))

def layer_norm(values, gain, shift):
    center = values - lax.optimization_barrier(jnp.mean(values, -1, keepdims=True))
    spread = lax.optimization_barrier(jnp.mean(center * center, -1, keepdims=True))
    return center * lax.rsqrt(spread + EPS_NORM) * gain + shift

def rotary_tables():
    half_rot = ROT // 2
    inverse = 10000.0 ** (-jnp.arange(half_rot, dtype=jnp.float32) * (2.0 / ROT))
    angles = jnp.arange(LENGTH, dtype=jnp.float32)[:, None] * inverse[None, :]
    return (jnp.cos(angles), jnp.sin(angles))

def rotate(heads, cosine, sine):
    half_rot = ROT // 2
    first = heads[..., :half_rot]
    second = heads[..., half_rot:ROT]
    return jnp.concatenate([first * cosine - second * sine, second * cosine + first * sine, heads[..., ROT:]], -1)

def causal(start, block):
    row_ids = start + jnp.arange(block, dtype=jnp.int32)
    return row_ids[:, None] >= jnp.arange(LENGTH, dtype=jnp.int32)[None, :]

def attend(query, key_in, value_in):
    block = min(512, LENGTH)
    scale = HEAD ** (-0.5)

    def one_block(start):
        query_block = lax.dynamic_slice_in_dim(query, start, block, 1)
        scores = low_back(jnp.einsum('hqd,hkd->hqk', query_block, key_in, precision=HIGH) * scale)
        scores = jnp.where(causal(start, block)[None], scores, NEG_BIG)
        probs = jax.nn.softmax(scores, -1)
        return jnp.einsum('hqk,hkd->hqd', low(probs), value_in, precision=HIGH)
    starts = jnp.arange(0, LENGTH, block, dtype=jnp.int32)
    outputs = lax.map(jax.checkpoint(one_block), starts)
    return jnp.transpose(outputs, (1, 0, 2, 3)).reshape(query.shape)

def layer(resid, w_one, w_two, bias, vector, cosine, sine):
    groups_t = N_TENSOR
    heads_g = HEADS // groups_t
    hidden_g = FF // groups_t
    query_cols = 3 * heads_g * HEAD
    att_rows = heads_g * HEAD
    row_count = resid.shape[0]
    seq_count = row_count // LENGTH
    first_in = low(layer_norm(resid, vector[0], vector[1]))
    second_in = low(layer_norm(resid, vector[2], vector[3]))
    w_cols = low(w_one).reshape(D, groups_t, query_cols + hidden_g)
    w_rows = low(w_two).reshape(groups_t, att_rows + hidden_g, D)
    bias_g = bias.reshape(groups_t, query_cols + hidden_g)
    qkv = low_back(jnp.einsum('td,dgc->tgc', first_in, w_cols[:, :, :query_cols], precision=HIGH) + bias_g[:, :query_cols])
    up_val = low_back(jnp.einsum('td,dgc->tgc', second_in, w_cols[:, :, query_cols:], precision=HIGH) + bias_g[:, query_cols:])
    parts = jnp.transpose(qkv.reshape(seq_count, LENGTH, HEADS, 3, HEAD), (3, 0, 2, 1, 4))
    q_rot = low(rotate(parts[0], cosine, sine))
    k_rot = low(rotate(parts[1], cosine, sine))
    v_val = low(parts[2])
    attended = lax.map(lambda item: attend(item[0], item[1], item[2]), (q_rot, k_rot, v_val))
    attended = low_back(low(attended))
    attended = jnp.transpose(attended, (0, 2, 1, 3)).reshape(row_count, groups_t, att_rows)
    hidden = low(jax.nn.gelu(up_val, approximate=False))
    branch = jnp.einsum('tgc,gcd->tgd', attended, w_rows[:, :att_rows], precision=HIGH)
    branch = branch + jnp.einsum('tgc,gcd->tgd', hidden, w_rows[:, att_rows:], precision=HIGH)
    branch = low_back(low(branch))
    return resid + lax.optimization_barrier(jnp.sum(branch, 1)) + vector[4] + vector[5]

def sequence_loss(normed, target_row, table):
    logits = low_back(jnp.dot(normed, table.T, precision=HIGH, preferred_element_type=jnp.float32))
    total_lse = jax.nn.logsumexp(logits, -1)
    picked = jnp.take_along_axis(logits, target_row[:, None], 1)[:, 0]
    return jnp.mean(total_lse - picked)

def replica_loss(params, token_ids, target_ids, weight_seq, cosine, sine):
    w_one, w_two, table_pair, bias, vector, final_gain = params
    resid = low(table_pair[0])[token_ids]
    for index in range(LAYERS):
        resid = layer(resid, w_one[index], w_two[index], bias[index], vector[index], cosine, sine)
    normed = low(layer_norm(resid, final_gain[0], final_gain[1])).reshape(SEQ_REP, LENGTH, D)
    table = low(table_pair[1])
    losses = lax.map(jax.checkpoint(lambda item: sequence_loss(item[0], item[1], table)), (normed, target_ids))
    return jnp.sum(weight_seq * losses)

def orthonormal(matrix):
    columns = []
    for index in range(RANK):
        column = matrix[..., index]
        for done in columns:
            column = column - lax.optimization_barrier(jnp.sum(done * column, -1, keepdims=True)) * done
        columns.append(column * lax.rsqrt(lax.optimization_barrier(jnp.sum(column * column, -1, keepdims=True)) + 1e-30))
    return jnp.stack(columns, -1)

def power_round(full_list, factor):
    summed = sum((jnp.einsum('...dn,...nr->...dr', item, factor, precision=HIGH) for item in full_list))
    basis = orthonormal(summed)
    pieces = [jnp.einsum('...dn,...dr->...nr', item, basis, precision=HIGH) for item in full_list]
    new_factor = sum(pieces)
    reduced = jnp.einsum('...dr,...nr->...dn', basis, new_factor, precision=HIGH)
    errors = [item - jnp.einsum('...dr,...nr->...dn', basis, piece, precision=HIGH) for item, piece in zip(full_list, pieces)]
    return (reduced, errors, new_factor)

def momentum_step(weight, moment, average, grad, rate):
    decay = ema_decay()
    new_moment = MOMENTUM * moment + (1.0 - MOMENTUM) * grad
    new_weight = weight - rate * new_moment
    return (new_weight, new_moment, decay * average + (1.0 - decay) * new_weight)

def reference(tokens, groups, counts, domain, w_in, w_back, tables, b_in, vecs, final_norm, w_in_mom, w_back_mom, tables_mom, b_in_mom, vecs_mom, final_mom, w_in_ema, w_back_ema, tables_ema, b_in_ema, vecs_ema, final_ema, w_in_err, w_back_err, tables_err, w_in_fac, w_back_fac, tables_fac):
    cosine, sine = rotary_tables()
    seq_index = jnp.arange(SEQ_REP * N_DP, dtype=jnp.int32)
    live = seq_index % SEQ_REP < counts[seq_index // SEQ_REP]
    seq_weight = jnp.where(live, domain[groups], 0.0)
    weight_total = jnp.sum(seq_weight)
    params = (w_in, w_back, tables, b_in, vecs, final_norm)
    loss_sum = jnp.zeros((), jnp.float32)
    grads = []
    for replica in range(N_DP):
        rows_here = tokens[replica * SEQ_REP:(replica + 1) * SEQ_REP]
        token_ids = rows_here[:, :LENGTH].reshape(-1)
        target_ids = rows_here[:, 1:]
        weight_seq = seq_weight[replica * SEQ_REP:(replica + 1) * SEQ_REP]
        value, pullback = jax.vjp(lambda p: replica_loss(p, token_ids, target_ids, weight_seq, cosine, sine), params)
        loss_sum = loss_sum + value
        grads.append(pullback(1.0 / weight_total)[0])
    groups_t = N_TENSOR
    shards = N_SECTION * N_TENSOR
    cols_g = NIN // groups_t
    rows_g = NBACK // groups_t
    vocab_shard = VOCAB // shards

    def in_blocks(item):
        return jnp.transpose(item.reshape(LAYERS, D, groups_t, cols_g), (0, 2, 1, 3))

    def in_whole(item):
        return jnp.transpose(item, (0, 2, 1, 3)).reshape(LAYERS, D, NIN)

    def back_blocks(item):
        return jnp.swapaxes(item.reshape(LAYERS, groups_t, rows_g, D), 2, 3)

    def back_whole(item):
        return jnp.swapaxes(item, 2, 3).reshape(LAYERS, NBACK, D)

    def table_blocks(item):
        return jnp.swapaxes(item.reshape(2, shards, vocab_shard, D), 2, 3)

    def table_whole(item):
        return jnp.swapaxes(item, 2, 3).reshape(2, VOCAB, D)
    red_in, errs_in, fac_in = power_round([in_blocks(grads[r][0] + w_in_err[r]) for r in range(N_DP)], w_in_fac.reshape(LAYERS, groups_t, cols_g, RANK))
    red_back, errs_back, fac_back = power_round([back_blocks(grads[r][1] + w_back_err[r]) for r in range(N_DP)], w_back_fac.reshape(LAYERS, groups_t, rows_g, RANK))
    red_tab, errs_tab, fac_tab = power_round([table_blocks(grads[r][2] + tables_err[r]) for r in range(N_DP)], tables_fac.reshape(2, shards, vocab_shard, RANK))
    red_bias = sum((grads[r][3] for r in range(N_DP)))
    red_vecs = sum((grads[r][4] for r in range(N_DP)))
    red_final = sum((grads[r][5] for r in range(N_DP)))
    token_count = N_DP * SEQ_REP * LENGTH
    rate_layer = 2.0 * math.sqrt(token_count)
    rate_vector = 6.0 * math.sqrt(token_count)
    rate_table = jnp.array([50.0, 0.5], jnp.float32).reshape(2, 1, 1) * math.sqrt(token_count * VOCAB)
    in_w, in_m, in_e = momentum_step(w_in, w_in_mom, w_in_ema, in_whole(red_in), rate_layer)
    back_w, back_m, back_e = momentum_step(w_back, w_back_mom, w_back_ema, back_whole(red_back), rate_layer)
    tab_w, tab_m, tab_e = momentum_step(tables, tables_mom, tables_ema, table_whole(red_tab), rate_table)
    bias_w, bias_m, bias_e = momentum_step(b_in, b_in_mom, b_in_ema, red_bias, rate_layer)
    vec_w, vec_m, vec_e = momentum_step(vecs, vecs_mom, vecs_ema, red_vecs, rate_vector)
    fin_w, fin_m, fin_e = momentum_step(final_norm, final_mom, final_ema, red_final, rate_layer)
    err_in_new = jnp.stack([in_whole(item) for item in errs_in])
    err_back_new = jnp.stack([back_whole(item) for item in errs_back])
    err_tab_new = jnp.stack([table_whole(item) for item in errs_tab])
    fac_tab_whole = fac_tab.reshape(2, VOCAB, RANK)
    return (loss_sum, weight_total, in_w, back_w, tab_w, bias_w, vec_w, fin_w, in_m, back_m, tab_m, bias_m, vec_m, fin_m, in_e, back_e, tab_e, bias_e, vec_e, fin_e, err_in_new, err_back_new, err_tab_new, fac_in.reshape(LAYERS, NIN, RANK), fac_back.reshape(LAYERS, NBACK, RANK), fac_tab_whole[0], fac_tab_whole[1])
```

```python
import functools
import math

import jax
import jax.numpy as jnp
import numpy as np
from jax import lax
from jax.experimental import pallas as pl
from jax.experimental.pallas import tpu as pltpu
from jax.sharding import Mesh
from jax.sharding import PartitionSpec as P

D = 512
HEAD = 64
ROT = 16
VOCAB = 50304
LAYERS = 4
LENGTH = 1024
RANK = 8
STEP = 5
BLOCK = 128

EPS_NORM = 1e-05
MOMENTUM = 0.9
NEG_BIG = -1e30
HIGH = lax.Precision.HIGHEST
BF = jnp.bfloat16
F32 = jnp.float32
MESH_ID = pl.DeviceIdType.MESH
FAR = (2, 1, 3)
PLANE = [(2, 2), (2, 1), (2, 3), (1, 2), (3, 2), (2, 0), (0, 2), (1, 1), (1, 3), (3, 1), (3, 3), (1, 0), (3, 0), (0, 1), (0, 3)]


def where_am_i():
    core, z = lax.axis_index("co"), lax.axis_index("zz")
    y = lax.axis_index("yh") * 2 + lax.axis_index("yl")
    return y, core, z


def at_chip(y, z):
    return {"yh": y // 2, "yl": lax.rem(y, 2), "zz": z}


def send(src, dst, sems, at, device):
    copy = pltpu.make_async_remote_copy(
        src_ref=src,
        dst_ref=dst,
        send_sem=sems[0].at[at],
        recv_sem=sems[1].at[at],
        device_id=device,
        device_id_type=MESH_ID,
    )
    copy.start()
    return copy


def greet(devices):
    barrier = pltpu.get_barrier_semaphore()
    for device in devices:
        pl.semaphore_signal(barrier, inc=1, device_id=device, device_id_type=MESH_ID)
    pl.semaphore_wait(barrier, len(devices))


def sem_pairs(*counts):
    return [pltpu.SemaphoreType.DMA((n,)) for n in counts for _ in range(2)]


VMEM_SPEC = pl.BlockSpec(memory_space=pltpu.VMEM)


def kernel_call(body, out_shape, args, scratch, cid=None, limit=48):
    many = isinstance(out_shape, (list, tuple))
    return pl.pallas_call(
        body,
        out_shape=out_shape,
        in_specs=[VMEM_SPEC] * len(args),
        out_specs=[VMEM_SPEC] * len(out_shape) if many else VMEM_SPEC,
        scratch_shapes=scratch,
        compiler_params=pltpu.CompilerParams(
            collective_id=cid, has_side_effects=cid is not None, vmem_limit_bytes=limit * 2**20
        ),
    )(*args)


def normed_rows(values):
    center = values - jnp.mean(values, -1, keepdims=True)
    spread = jnp.mean(center * center, -1, keepdims=True)
    scale = lax.rsqrt(spread + EPS_NORM)
    return center * scale, scale


def norm_back(values, grad):
    hat, scale = normed_rows(values)
    return scale * (
        grad
        - jnp.mean(grad, -1, keepdims=True)
        - hat * jnp.mean(grad * hat, -1, keepdims=True)
    )


def row_sum(part, r1, s, r2, sems1, sems2):
    y, core, z = where_am_i()
    first = []
    for i, k in enumerate(FAR + (0,)):
        zz = lax.rem(z + k, 4)
        first.append(send(part.at[(1 - core) * 4 + zz], r1.at[i], sems1, i, {"co": 1 - core}))
    second = []
    for i, k in enumerate(FAR):
        zz = lax.rem(z + k, 4)
        first[i].wait_recv()
        s[i] = (part[core * 4 + zz].astype(F32) + r1[i].astype(F32)).astype(BF)
        second.append(send(s.at[i], r2.at[i], sems2, i, {"zz": zz}))
    first[3].wait_recv()
    total = part[core * 4 + z].astype(F32) + r1[3].astype(F32)
    for i in range(3):
        second[i].wait_recv()
        total = total + r2[i].astype(F32)
    for copy in first + second:
        copy.wait_send()
    return total


def row_gather(everyone, sems3, sems4):
    y, core, z = where_am_i()
    own = everyone.at[core * 4 + z]
    third = [
        send(own, own, sems3, i, {"zz": lax.rem(z + k, 4)}) for i, k in enumerate(FAR)
    ]
    fourth = [send(own, own, sems4, 3, {"co": 1 - core})]
    for i, k in enumerate(FAR):
        third[i].wait_recv()
        came = everyone.at[core * 4 + lax.rem(z + 4 - k, 4)]
        fourth.append(send(came, came, sems4, i, {"co": 1 - core}))
    for copy in third:
        copy.wait_send()
    for copy in fourth:
        copy.wait()


def row_peers():
    y, core, z = where_am_i()
    return [{"co": 1 - core}] + [{"zz": lax.rem(z + k, 4)} for k in FAR]


SUM_SCRATCH = [
    pltpu.VMEM((4, BLOCK, D), BF),
    pltpu.VMEM((3, BLOCK, D), BF),
    pltpu.VMEM((3, BLOCK, D), BF),
] + sem_pairs(4, 3)
GATHER_SCRATCH = sem_pairs(3, 4)


def first_body(x, everyone, a, b, c, d):
    y, core, z = where_am_i()
    greet(row_peers())
    everyone[core * 4 + z] = normed_rows(x[...])[0].astype(BF)
    row_gather(everyone, (a, b), (c, d))


def first_hat(x):
    return kernel_call(
        first_body, jax.ShapeDtypeStruct((8, BLOCK, D), BF), (x,), GATHER_SCRATCH, 1
    )


def forward_body(part, x, shift, everyone, x_new, r1, s, r2, e, f, g, h, a, b, c, d):
    y, core, z = where_am_i()
    greet(row_peers())
    after = x[...] + row_sum(part, r1, s, r2, (e, f), (g, h)) + shift[0:1]
    x_new[...] = after
    everyone[core * 4 + z] = normed_rows(after)[0].astype(BF)
    row_gather(everyone, (a, b), (c, d))


def next_hat(part, x, shift):
    return kernel_call(
        forward_body,
        [jax.ShapeDtypeStruct((8, BLOCK, D), BF), jax.ShapeDtypeStruct((BLOCK, D), F32)],
        (part, x, shift),
        SUM_SCRATCH + GATHER_SCRATCH,
        2,
    )


def last_body(part, x, shift, gains, x_new, normed, r1, s, r2, e, f, g, h):
    greet(row_peers())
    after = x[...] + row_sum(part, r1, s, r2, (e, f), (g, h)) + shift[0:1]
    x_new[...] = after
    normed[...] = (normed_rows(after)[0] * gains[0:1] + gains[1:2]).astype(BF)


def last_normed(part, x, shift, gains):
    return kernel_call(
        last_body,
        [jax.ShapeDtypeStruct((BLOCK, D), F32), jax.ShapeDtypeStruct((BLOCK, D), BF)],
        (part, x, shift, gains),
        SUM_SCRATCH,
        3,
    )


def spread_body(grad, everyone, a, b, c, d):
    y, core, z = where_am_i()
    greet(row_peers())
    everyone[core * 4 + z] = grad[...].astype(BF)
    row_gather(everyone, (a, b), (c, d))


def spread_grad(grad):
    return kernel_call(
        spread_body, jax.ShapeDtypeStruct((8, BLOCK, D), BF), (grad,), GATHER_SCRATCH, 4
    )


def backward_body(part, x, grad, everyone, g_new, r1, s, r2, e, f, g, h, a, b, c, d):
    y, core, z = where_am_i()
    greet(row_peers())
    after = grad[...] + norm_back(x[...], row_sum(part, r1, s, r2, (e, f), (g, h)))
    g_new[...] = after
    everyone[core * 4 + z] = after.astype(BF)
    row_gather(everyone, (a, b), (c, d))


def next_grad(part, x, grad):
    return kernel_call(
        backward_body,
        [jax.ShapeDtypeStruct((8, BLOCK, D), BF), jax.ShapeDtypeStruct((BLOCK, D), F32)],
        (part, x, grad),
        SUM_SCRATCH + GATHER_SCRATCH,
        5,
    )


def lowest_body(part, x, grad, low, r1, s, r2, e, f, g, h):
    greet(row_peers())
    after = grad[...] + norm_back(x[...], row_sum(part, r1, s, r2, (e, f), (g, h)))
    low[...] = after.astype(BF)


def lowest_grad(part, x, grad):
    return kernel_call(
        lowest_body, jax.ShapeDtypeStruct((BLOCK, D), BF), (part, x, grad), SUM_SCRATCH, 6
    )


def plane_peers():
    y, core, z = where_am_i()
    return [{"co": 1 - core}] + [
        at_chip(lax.rem(y + dy, 4), lax.rem(z + dz, 4)) for dy, dz in PLANE
    ]


def plane_sum_body(part, out, r1, s, r2, a, b, c, d):
    y, core, z = where_am_i()
    greet(plane_peers())
    first = []
    for i, (dy, dz) in enumerate(PLANE + [(0, 0)]):
        at = lax.rem(y + dy, 4) * 8 + lax.rem(z + dz, 4)
        first.append(send(part.at[at + 4 * (1 - core)], r1.at[i], (a, b), i, {"co": 1 - core}))
    second = []
    for i, (dy, dz) in enumerate(PLANE):
        yy, zz = lax.rem(y + dy, 4), lax.rem(z + dz, 4)
        first[i].wait_recv()
        s[i] = (part[yy * 8 + core * 4 + zz].astype(F32) + r1[i].astype(F32)).astype(BF)
        second.append(send(s.at[i], r2.at[i], (c, d), i, at_chip(yy, zz)))
    first[15].wait_recv()
    total = part[y * 8 + core * 4 + z].astype(F32) + r1[15].astype(F32)
    for i in range(15):
        second[i].wait_recv()
        total = total + r2[i].astype(F32)
    for copy in first + second:
        copy.wait_send()
    out[...] = total


def plane_sum(part):
    return kernel_call(
        plane_sum_body,
        jax.ShapeDtypeStruct((BLOCK, D), F32),
        (part,),
        [
            pltpu.VMEM((16, BLOCK, D), BF),
            pltpu.VMEM((15, BLOCK, D), BF),
            pltpu.VMEM((15, BLOCK, D), BF),
        ]
        + sem_pairs(16, 15),
        7,
    )


def plane_gather_body(block, everyone, a, b, c, d):
    y, core, z = where_am_i()
    greet(plane_peers())
    own = everyone.at[y * 8 + core * 4 + z]
    everyone[y * 8 + core * 4 + z] = block[...]
    first = [
        send(own, own, (a, b), i, at_chip(lax.rem(y + dy, 4), lax.rem(z + dz, 4)))
        for i, (dy, dz) in enumerate(PLANE)
    ]
    second = [send(own, own, (c, d), 15, {"co": 1 - core})]
    for i, (dy, dz) in reversed(list(enumerate(PLANE))):
        first[i].wait_recv()
        came = everyone.at[lax.rem(y + 4 - dy, 4) * 8 + core * 4 + lax.rem(z + 4 - dz, 4)]
        second.append(send(came, came, (c, d), i, {"co": 1 - core}))
    for copy in first:
        copy.wait_send()
    for copy in second:
        copy.wait()


def plane_gather(block):
    return kernel_call(
        plane_gather_body,
        jax.ShapeDtypeStruct((32, BLOCK, D), BF),
        (block,),
        sem_pairs(15, 16),
        8,
    )


def stats_body(stats, result, came, everyone, a, b, c, d):
    y, core, z = where_am_i()
    me = y * 8 + core * 4 + z
    peers = []
    for k in range(1, 32):
        p = lax.rem(me + k, 32)
        peers.append((p, {**at_chip(p // 8, lax.rem(p, 4)), "co": lax.rem(p // 4, 2)}))
    greet([device for _, device in peers])
    copies = [
        send(stats.at[p], came.at[me], (a, b), k, device) for k, (p, device) in enumerate(peers)
    ]
    came[me] = stats[me]
    for copy in copies:
        copy.wait_recv()
    top = jnp.max(came[:, 0, :], 0, keepdims=True)
    total = jnp.sum(came[:, 1, :] * jnp.exp(came[:, 0, :] - top), 0, keepdims=True)
    target = jnp.sum(came[:, 2, :], 0, keepdims=True)
    lse = top + jnp.log(total)
    everyone[me] = jnp.concatenate([lse, lse - target, jnp.zeros((6, BLOCK), F32)], 0)
    own = everyone.at[me]
    for copy in copies:
        copy.wait_send()
    copies = [send(own, own, (c, d), k, device) for k, (_, device) in enumerate(peers)]
    for copy in copies:
        copy.wait()
    result[...] = everyone[...]


def joined_stats(stats):
    return kernel_call(
        stats_body,
        jax.ShapeDtypeStruct((32, 8, BLOCK), F32),
        (stats,),
        [pltpu.VMEM((32, 8, BLOCK), F32), pltpu.VMEM((32, 8, BLOCK), F32)] + sem_pairs(31, 31),
        9,
    )


def column_peers():
    y, core, z = where_am_i()
    return [{"co": 1 - core}] + [
        {**at_chip(lax.rem(y + dy, 4), z), "co": c} for dy in FAR for c in (0, 1)
    ]


def weights_body(cols, rows, all_cols, all_rows, a, b, c, d):
    y, core, z = where_am_i()
    greet(column_peers())
    layer = lax.rem(y, 2) * 2 + core
    home = y // 2 == core
    pairs = ((cols, all_cols, a, b), (rows, all_rows, c, d))

    def out_copy(src, dst, s, r, dy):
        return pltpu.make_async_remote_copy(
            src_ref=src,
            dst_ref=dst.at[layer],
            send_sem=s.at[dy],
            recv_sem=r.at[layer],
            device_id={**at_chip(lax.rem(y + dy, 4), z), "co": y // 2},
            device_id_type=MESH_ID,
        )

    for dy in FAR:
        for src, dst, s, r in pairs:
            out_copy(src, dst, s, r, dy).start()
    for src, dst, s, r in pairs:

        @pl.when(home)
        def _():
            pltpu.make_async_copy(src, dst.at[layer], r.at[layer]).start()

        @pl.when(jnp.logical_not(home))
        def _():
            out_copy(src, dst, s, r, 0).start()
            out_copy(src, dst, s, r, 0).wait_send()

    for dy in FAR:
        for src, dst, s, r in pairs:
            out_copy(src, dst, s, r, dy).wait_send()
    for index in range(LAYERS):
        for src, dst, s, r in pairs:
            pltpu.make_async_copy(src, dst.at[index], r.at[index]).wait()


def gathered_weights(cols, rows):
    return pl.pallas_call(
        weights_body,
        out_shape=[
            jax.ShapeDtypeStruct((LAYERS, *cols.shape), BF),
            jax.ShapeDtypeStruct((LAYERS, *rows.shape), BF),
        ],
        in_specs=[pl.BlockSpec(memory_space=pl.ANY)] * 2,
        out_specs=[pl.BlockSpec(memory_space=pl.ANY)] * 2,
        scratch_shapes=sem_pairs(4, 4),
        compiler_params=pltpu.CompilerParams(collective_id=10, has_side_effects=True),
    )(cols, rows)


def grads_body(count, *refs):
    sources, landed, sems = refs[:count], refs[count : 2 * count], refs[2 * count :]
    y, core, z = where_am_i()
    greet(column_peers())
    own_layer = lax.rem(y, 2) * 2 + core
    home = y // 2 == core

    def out_copy(n, layer):
        return pltpu.make_async_remote_copy(
            src_ref=sources[n].at[layer],
            dst_ref=landed[n].at[y],
            send_sem=sems[2 * n].at[layer],
            recv_sem=sems[2 * n + 1].at[y],
            device_id={**at_chip(core * 2 + layer // 2, z), "co": layer % 2},
            device_id_type=MESH_ID,
        )

    def both(layer, act):
        local = jnp.logical_and(home, own_layer == layer)
        for n in range(count):

            @pl.when(jnp.logical_not(local))
            def _():
                act(out_copy(n, layer))

    for layer in range(LAYERS):
        both(layer, lambda copy: copy.start())
    for n in range(count):

        @pl.when(home)
        def _():
            pltpu.make_async_copy(
                sources[n].at[own_layer], landed[n].at[y], sems[2 * n + 1].at[y]
            ).start()

    for layer in range(LAYERS):
        both(layer, lambda copy: copy.wait_send())
    for index in range(4):
        for n in range(count):
            pltpu.make_async_copy(
                sources[n].at[0], landed[n].at[index], sems[2 * n + 1].at[index]
            ).wait()


def returned_grads(*grads):
    return pl.pallas_call(
        functools.partial(grads_body, len(grads)),
        out_shape=[jax.ShapeDtypeStruct(g.shape, g.dtype) for g in grads],
        in_specs=[pl.BlockSpec(memory_space=pl.ANY)] * len(grads),
        out_specs=[pl.BlockSpec(memory_space=pl.ANY)] * len(grads),
        scratch_shapes=sem_pairs(*[4] * len(grads)),
        compiler_params=pltpu.CompilerParams(collective_id=11, has_side_effects=True),
    )(*grads)


def replicas_peers():
    x = lax.axis_index("xx")
    return [(lax.rem(x + k, 4), {"xx": lax.rem(x + k, 4)}) for k in FAR]


def replicas_exchange(block, everyone, a, b):
    x = lax.axis_index("xx")
    copies = [
        send(block, everyone.at[x], (a, b), i, device)
        for i, (_, device) in enumerate(replicas_peers())
    ]
    return copies


def features_body(block, everyone, a, b, own_sem):
    greet([device for _, device in replicas_peers()])
    copies = replicas_exchange(block, everyone, a, b)
    own = pltpu.make_async_copy(block, everyone.at[lax.axis_index("xx")], own_sem)
    own.start()
    own.wait()
    for copy in copies:
        copy.wait()


def all_features(block):
    return pl.pallas_call(
        features_body,
        out_shape=jax.ShapeDtypeStruct((4, *block.shape), block.dtype),
        in_specs=[pl.BlockSpec(memory_space=pl.ANY)],
        out_specs=pl.BlockSpec(memory_space=pl.ANY),
        scratch_shapes=sem_pairs(3) + [pltpu.SemaphoreType.DMA],
        compiler_params=pltpu.CompilerParams(collective_id=12, has_side_effects=True),
    )(block)


def left_body(left, extra, basis, extra_sum, came, came_extra, work, a, b, c, d):
    x = lax.axis_index("xx")
    greet([device for _, device in replicas_peers()])
    copies = replicas_exchange(left, came, a, b) + replicas_exchange(extra, came_extra, c, d)
    came[x] = left[...]
    came_extra[x] = extra[...]
    for copy in copies:
        copy.wait()
    extra_sum[...] = jnp.sum(came_extra[...], 0)
    work[...] = jnp.sum(came[...], 0)
    rows = lax.broadcasted_iota(jnp.int32, (1, RANK, 1), 1)
    for index in range(RANK):
        columns = work[...]
        one = columns[:, index : index + 1, :]
        one = one * lax.rsqrt(jnp.sum(one * one, -1, keepdims=True) + 1e-30)
        shares = jnp.sum(columns * one, -1, keepdims=True)
        work[...] = jnp.where(rows > index, columns - shares * one, columns)
        basis[:, index : index + 1, :] = one


def orthonormal_sum(left, extra):
    return kernel_call(
        left_body,
        [
            jax.ShapeDtypeStruct(left.shape, F32),
            jax.ShapeDtypeStruct(extra.shape, F32),
        ],
        (left, extra),
        [
            pltpu.VMEM((4, *left.shape), F32),
            pltpu.VMEM((4, *extra.shape), F32),
            pltpu.VMEM(left.shape, F32),
        ]
        + sem_pairs(3, 3),
        13,
    )


def right_body(right, total, came, a, b):
    x = lax.axis_index("xx")
    greet([device for _, device in replicas_peers()])
    copies = replicas_exchange(right, came, a, b)
    came[x] = right[...]
    for copy in copies:
        copy.wait()
    total[...] = jnp.sum(came[...].astype(F32), 0)


def right_sum(right):
    return kernel_call(
        right_body,
        jax.ShapeDtypeStruct(right.shape, F32),
        (right,),
        [pltpu.VMEM((4, *right.shape), BF)] + sem_pairs(3),
        14,
    )


def ema_decay():
    return min(0.999, (1.0 + STEP) / (10.0 + STEP))


def rotary_tables():
    half_rot = ROT // 2
    inverse = 10000.0 ** (-jnp.arange(half_rot, dtype=F32) * (2.0 / ROT))
    angles = jnp.arange(LENGTH, dtype=F32)[:, None] * inverse[None, :]
    return (jnp.cos(angles), jnp.sin(angles))


def rotate(heads, cosine, sine):
    half_rot = ROT // 2
    first = heads[..., :half_rot]
    second = heads[..., half_rot:ROT]
    return jnp.concatenate(
        [first * cosine - second * sine, second * cosine + first * sine, heads[..., ROT:]], -1
    )


def dot_rows(left, right):
    return lax.dot_general(
        left, right, (((0,), (0,)), ((), ())), preferred_element_type=F32
    )


def dot_cols(left, right):
    return lax.dot_general(
        left, right, (((1,), (1,)), ((), ())), preferred_element_type=F32
    )


def dot_plain(left, right):
    return jnp.dot(left, right, preferred_element_type=F32)


ATT_BLOCK = 512


def causal(start, stop):
    rows = start + lax.broadcasted_iota(jnp.int32, (stop - start, stop), 0)
    return rows >= lax.broadcasted_iota(jnp.int32, (stop - start, stop), 1)


def attention_forward(q_rot, k_rot, v_val):
    outputs, all_lse = [], []
    for start in range(0, LENGTH, ATT_BLOCK):
        stop = start + ATT_BLOCK
        scores = dot_cols(q_rot[start:stop], k_rot[:stop]) * HEAD ** (-0.5)
        scores = jnp.where(causal(start, stop), scores, NEG_BIG)
        top = jnp.max(scores, -1, keepdims=True)
        expo = jnp.exp(scores - top)
        total = jnp.sum(expo, -1, keepdims=True)
        probs = (expo / total).astype(BF)
        outputs.append(dot_plain(probs, v_val[:stop]))
        all_lse.append(top + jnp.log(total))
    return (jnp.concatenate(outputs, 0), jnp.concatenate(all_lse, 0))


def attention_backward(q_rot, k_rot, v_val, lse, grad_out):
    scale = HEAD ** (-0.5)
    grad_query, grad_key, grad_value = [], 0.0, 0.0
    for start in range(0, LENGTH, ATT_BLOCK):
        stop = start + ATT_BLOCK
        spare = ((0, LENGTH - stop), (0, 0))
        scores = dot_cols(q_rot[start:stop], k_rot[:stop]) * scale
        probs = jnp.where(causal(start, stop), jnp.exp(scores - lse[start:stop]), 0.0)
        grad_probs = dot_cols(grad_out[start:stop], v_val[:stop])
        grad_scores = (
            probs * (grad_probs - jnp.sum(grad_probs * probs, -1, keepdims=True))
        ).astype(BF)
        grad_query.append(dot_plain(grad_scores, k_rot[:stop]) * scale)
        grad_key = grad_key + jnp.pad(dot_rows(grad_scores, q_rot[start:stop]), spare) * scale
        grad_value = grad_value + jnp.pad(
            dot_rows(probs.astype(BF), grad_out[start:stop]), spare
        )
    return (jnp.concatenate(grad_query, 0), grad_key, grad_value)


def block_forward(hat, weights, cosine, sine):
    w_cols, w_rows, bias, vector = weights
    wide = hat.astype(F32)
    first_in = (wide * vector[0] + vector[1]).astype(BF)
    second_in = (wide * vector[2] + vector[3]).astype(BF)
    qkv = dot_plain(first_in, w_cols[:, : 3 * HEAD]) + bias[: 3 * HEAD]
    up_val = dot_plain(second_in, w_cols[:, 3 * HEAD :]) + bias[3 * HEAD :]
    q_rot = rotate(qkv[:, :HEAD], cosine, sine).astype(BF)
    k_rot = rotate(qkv[:, HEAD : 2 * HEAD], cosine, sine).astype(BF)
    v_val = qkv[:, 2 * HEAD :].astype(BF)
    attended, lse = attention_forward(q_rot, k_rot, v_val)
    attended = attended.astype(BF)
    hidden = jax.nn.gelu(up_val, approximate=False).astype(BF)
    branch = dot_plain(attended, w_rows[:HEAD]) + dot_plain(hidden, w_rows[HEAD:])
    return (
        branch.astype(BF),
        (hat, first_in, second_in, q_rot, k_rot, v_val, lse, attended, up_val, hidden),
    )


def gelu_exact(values):
    return jax.nn.gelu(values, approximate=False)


def block_backward(grad_low, kept, weights, cosine, sine):
    w_cols, w_rows, bias, vector = weights
    hat, first_in, second_in, q_rot, k_rot, v_val, lse, attended, up_val, hidden = kept
    grad_rows = jnp.concatenate([dot_rows(attended, grad_low), dot_rows(hidden, grad_low)], 0)
    grad_att = dot_cols(grad_low, w_rows[:HEAD]).astype(BF)
    grad_hidden = dot_cols(grad_low, w_rows[HEAD:])
    grad_up = jax.vjp(gelu_exact, up_val)[1](grad_hidden)[0].astype(BF)
    grad_query, grad_key, grad_value = attention_backward(q_rot, k_rot, v_val, lse, grad_att)
    grad_query = rotate(grad_query, cosine, -sine)
    grad_key = rotate(grad_key, cosine, -sine)
    grad_qkv = jnp.concatenate([grad_query, grad_key, grad_value], 1).astype(BF)
    grad_cols = jnp.concatenate([dot_rows(first_in, grad_qkv), dot_rows(second_in, grad_up)], 1)
    grad_bias = jnp.concatenate(
        [jnp.sum(grad_qkv.astype(F32), 0), jnp.sum(grad_up.astype(F32), 0)]
    )
    grad_first = dot_cols(grad_qkv, w_cols[:, : 3 * HEAD])
    grad_second = dot_cols(grad_up, w_cols[:, 3 * HEAD :])
    wide = hat.astype(F32)
    grad_norms = jnp.stack(
        [
            jnp.sum(grad_first * wide, 0),
            jnp.sum(grad_first, 0),
            jnp.sum(grad_second * wide, 0),
            jnp.sum(grad_second, 0),
        ]
    )
    grad_hat = grad_first * vector[0] + grad_second * vector[2]
    return (grad_hat.astype(BF), (grad_cols.astype(BF), grad_rows.astype(BF), grad_bias, grad_norms))


def momentum_step(weight, moment, average, grad, rate):
    decay = ema_decay()
    new_moment = MOMENTUM * moment + (1.0 - MOMENTUM) * grad
    new_weight = weight - rate * new_moment
    return (new_weight, new_moment, decay * average + (1.0 - decay) * new_weight)


def on_device(
    tokens,
    groups,
    counts,
    domain,
    w_in,
    w_back,
    tables,
    b_in,
    vecs,
    final_norm,
    w_in_mom,
    w_back_mom,
    tables_mom,
    b_in_mom,
    vecs_mom,
    final_mom,
    w_in_ema,
    w_back_ema,
    tables_ema,
    b_in_ema,
    vecs_ema,
    final_ema,
    w_in_err,
    w_back_err,
    tables_err,
    w_in_fac,
    w_back_fac,
    tables_fac,
):
    y, core, z = where_am_i()
    replica = lax.axis_index("xx")
    section = lax.axis_index("yl") * 2 + core
    vocab_part = section * 8 + lax.axis_index("yh") * 4 + z
    shard = core * 4 + z
    seq_rep = tokens.shape[0]
    row_total = seq_rep * LENGTH
    vocab_shard = tables.shape[1]
    own_cols = tables.shape[2]
    cosine, sine = rotary_tables()

    seq_index = jnp.arange(groups.shape[0], dtype=jnp.int32)
    live = seq_index % seq_rep < counts[seq_index // seq_rep]
    domain_hit = groups[:, None] == jnp.arange(domain.shape[0], dtype=jnp.int32)[None, :]
    seq_weight = jnp.where(live, jnp.sum(jnp.where(domain_hit, domain[None, :], 0.0), 1), 0.0)
    weight_total = jnp.sum(seq_weight)
    own_weight = lax.dynamic_slice_in_dim(seq_weight, replica * seq_rep, seq_rep, 0)
    token_ids = tokens[:, :LENGTH].reshape(-1)
    target_ids = tokens[:, 1:].reshape(-1)
    local_ids = token_ids - vocab_part * vocab_shard
    local_targets = target_ids - vocab_part * vocab_shard

    short = tables.astype(BF)
    spare = -vocab_shard % 16
    embed_low = all_features(jnp.pad(short[0], ((0, spare), (0, 0))))
    embed_low = jnp.transpose(embed_low, (1, 0, 2)).reshape(vocab_shard + spare, D)
    head_low = lax.all_gather(short[1], "xx", axis=1, tiled=True)
    all_cols, all_rows = gathered_weights(w_in[0].astype(BF), w_back[0].astype(BF))
    small = jnp.concatenate([vecs[0].reshape(-1), b_in[0]])
    small = lax.all_gather(small, ("yl", "co", "yh", "zz"), axis=0, tiled=False)
    small = small.reshape(LAYERS, 8, -1)
    all_vecs = small[:, 0, : 6 * D].reshape(LAYERS, 6, D)
    all_bias = lax.dynamic_index_in_dim(small[:, :, 6 * D :], shard, 1, False)

    vocab_ids = jnp.arange(vocab_shard + spare, dtype=jnp.int32)
    looked = dot_plain((local_ids[:, None] == vocab_ids[None, :]).astype(BF), embed_low)
    x = plane_sum(looked.astype(BF).reshape(32, BLOCK, D))
    hat = first_hat(x).reshape(LENGTH, D)

    weights = [
        (all_cols[index], all_rows[index], all_bias[index], all_vecs[index])
        for index in range(LAYERS)
    ]
    shifts = [
        jnp.broadcast_to((all_vecs[index, 4] + all_vecs[index, 5])[None], (8, D))
        for index in range(LAYERS)
    ]
    gains = jnp.pad(final_norm, ((0, 6), (0, 0)))
    kept, before = [], []
    for index in range(LAYERS):
        before.append(x)
        branch, keep = block_forward(hat, weights[index], cosine, sine)
        kept.append(keep)
        branch = branch.reshape(8, BLOCK, D)
        if index + 1 < LAYERS:
            hat, x = next_hat(branch, x, shifts[index])
            hat = hat.reshape(LENGTH, D)
        else:
            x, normed_own = last_normed(branch, x, shifts[index], gains)

    normed = plane_gather(normed_own).reshape(row_total, D)
    logits = dot_cols(normed, head_low)
    target_hit = local_targets[:, None] == jnp.arange(vocab_shard, dtype=jnp.int32)[None, :]
    top_local = jnp.max(logits, 1)
    total_local = jnp.sum(jnp.exp(logits - top_local[:, None]), 1)
    target_local = jnp.sum(jnp.where(target_hit, logits, 0.0), 1)
    stats = jnp.stack([top_local, total_local, target_local]).reshape(3, 32, BLOCK)
    stats = jnp.pad(jnp.transpose(stats, (1, 0, 2)), ((0, 0), (0, 5), (0, 0)))
    joined = joined_stats(stats)
    lse_all = joined[:, 0, :].reshape(-1)
    losses = joined[:, 1, :].reshape(seq_rep, LENGTH)
    loss_part = jnp.sum(own_weight * jnp.mean(losses, 1))
    row_coef = jnp.repeat(own_weight / (weight_total * LENGTH), LENGTH)
    grad_logits = (
        (jnp.exp(logits - lse_all[:, None]) - target_hit.astype(F32)) * row_coef[:, None]
    ).astype(BF)
    grad_normed = plane_sum(dot_plain(grad_logits, head_low).astype(BF).reshape(32, BLOCK, D))
    grad_table = dot_rows(grad_logits, normed)

    hat_own, _ = normed_rows(x)
    grad_gains = jnp.stack([jnp.sum(grad_normed * hat_own, 0), jnp.sum(grad_normed, 0)])
    grad = norm_back(x, grad_normed * final_norm[0])
    grad_all = spread_grad(grad)
    layer_grads = [None] * LAYERS
    grad_outbias = [None] * LAYERS
    for index in reversed(range(LAYERS)):
        grad_outbias[index] = jnp.sum(grad, 0)
        grad_hat, layer_grads[index] = block_backward(
            grad_all.reshape(LENGTH, D), kept[index], weights[index], cosine, sine
        )
        grad_hat = grad_hat.reshape(8, BLOCK, D)
        if index:
            grad_all, grad = next_grad(grad_hat, before[index], grad)
        else:
            grad_low = lowest_grad(grad_hat, before[index], grad)
    grad_embedded = plane_gather(grad_low).reshape(row_total, D)
    grad_embed = dot_rows(
        (local_ids[:, None] == jnp.arange(vocab_shard, dtype=jnp.int32)[None, :]).astype(BF),
        grad_embedded,
    )

    cols_came, rows_came, bias_came = returned_grads(
        jnp.stack([g[0] for g in layer_grads]),
        jnp.stack([g[1] for g in layer_grads]),
        jnp.stack([jnp.pad(g[2].reshape(1, -1), ((0, 7), (0, 64))) for g in layer_grads]),
    )
    bias_part = jnp.sum(bias_came, 0)
    loss_row = jnp.zeros((1, D), F32).at[0, 0].set(jnp.where(shard + y * 8 == 0, loss_part, 0.0))
    vector_parts = jnp.concatenate(
        [
            jnp.concatenate([layer_grads[index][3], grad_outbias[index][None], grad_outbias[index][None]])
            for index in range(LAYERS)
        ]
        + [grad_gains, loss_row],
        0,
    )
    vector_sums = lax.psum(vector_parts, ("yl", "co", "yh", "zz", "xx"))
    vec_sum = lax.dynamic_slice_in_dim(vector_sums, section * 6, 6, 0)
    final_sum = vector_sums[6 * LAYERS : 6 * LAYERS + 2]
    loss_sum = vector_sums[6 * LAYERS + 2, 0]

    full_in = jnp.sum(cols_came.astype(F32), 0) + w_in_err[0, 0]
    full_back = jnp.sum(rows_came.astype(F32), 0) + w_back_err[0, 0]
    full_embed = grad_embed + tables_err[0, 0]
    full_head = grad_table + tables_err[0, 1]
    left = jnp.stack(
        [
            jnp.einsum("dn,nr->rd", full_in, w_in_fac[0], precision=HIGH),
            jnp.einsum("nd,nr->rd", full_back, w_back_fac[0], precision=HIGH),
            jnp.einsum("nd,nr->rd", full_embed, tables_fac[0], precision=HIGH),
            jnp.einsum("nd,nr->rd", full_head, tables_fac[1], precision=HIGH),
        ]
    )
    basis, bias_sum = orthonormal_sum(left, bias_part)
    bias_sum = bias_sum[:1, : b_in.shape[1]]
    right_in = jnp.einsum("dn,rd->rn", full_in, basis[0], precision=HIGH)
    right_back = jnp.einsum("nd,rd->rn", full_back, basis[1], precision=HIGH)
    right_embed = jnp.einsum("nd,rd->rn", full_embed, basis[2], precision=HIGH)
    right_head = jnp.einsum("nd,rd->rn", full_head, basis[3], precision=HIGH)
    rights = [right_in, right_back, right_embed, right_head]
    joint = jnp.concatenate(rights, 1).astype(BF)
    width = joint.shape[1]
    joint = right_sum(jnp.pad(joint, ((0, 8), (0, -width % 128))))[:8]
    sums, at = [], 0
    for right in rights:
        sums.append(joint[:, at : at + right.shape[1]])
        at += right.shape[1]
    sum_in, sum_back, sum_embed, sum_head = sums
    red_in = jnp.einsum("rd,rn->dn", basis[0], sum_in, precision=HIGH)
    red_back = jnp.einsum("rn,rd->nd", sum_back, basis[1], precision=HIGH)
    own_basis = lax.dynamic_slice_in_dim(basis[2:], replica * own_cols, own_cols, 2)
    red_tab = jnp.stack(
        [
            jnp.einsum("rn,rd->nd", sum_embed, own_basis[0], precision=HIGH),
            jnp.einsum("rn,rd->nd", sum_head, own_basis[1], precision=HIGH),
        ]
    )
    err_in_new = full_in - jnp.einsum("rd,rn->dn", basis[0], right_in, precision=HIGH)
    err_back_new = full_back - jnp.einsum("rn,rd->nd", right_back, basis[1], precision=HIGH)
    err_tab_new = jnp.stack(
        [
            full_embed - jnp.einsum("rn,rd->nd", right_embed, basis[2], precision=HIGH),
            full_head - jnp.einsum("rn,rd->nd", right_head, basis[3], precision=HIGH),
        ]
    )
    token_count = lax.axis_size("xx") * seq_rep * LENGTH
    rate_layer = 2.0 * math.sqrt(token_count)
    rate_vector = 6.0 * math.sqrt(token_count)
    rate_table = jnp.array([50.0, 0.5], F32).reshape(2, 1, 1) * math.sqrt(token_count * VOCAB)
    in_w, in_m, in_e = momentum_step(w_in, w_in_mom, w_in_ema, red_in[None], rate_layer)
    back_w, back_m, back_e = momentum_step(
        w_back, w_back_mom, w_back_ema, red_back[None], rate_layer
    )
    tab_w, tab_m, tab_e = momentum_step(tables, tables_mom, tables_ema, red_tab, rate_table)
    bias_w, bias_m, bias_e = momentum_step(b_in, b_in_mom, b_in_ema, bias_sum, rate_layer)
    vec_w, vec_m, vec_e = momentum_step(vecs, vecs_mom, vecs_ema, vec_sum[None], rate_vector)
    fin_w, fin_m, fin_e = momentum_step(final_norm, final_mom, final_ema, final_sum, rate_layer)
    return (
        loss_sum,
        weight_total,
        in_w,
        back_w,
        tab_w,
        bias_w,
        vec_w,
        fin_w,
        in_m,
        back_m,
        tab_m,
        bias_m,
        vec_m,
        fin_m,
        in_e,
        back_e,
        tab_e,
        bias_e,
        vec_e,
        fin_e,
        err_in_new[None, None],
        err_back_new[None, None],
        err_tab_new[None],
        sum_in.T[None],
        sum_back.T[None],
        sum_embed.T,
        sum_head.T,
    )


def solution(mesh):
    fine = Mesh(
        np.asarray(mesh.devices).reshape(2, 2, 2, 4, 4), ("yl", "co", "yh", "zz", "xx")
    )
    names = {"section": ("yl", "co"), "tensor": ("yh", "zz"), "dp": ("xx",)}

    def spec(*axes):
        return P(*[None if a is None else sum((names[n] for n in a.split()), ()) for a in axes])

    layer_in, layer_back = spec("section", None, "tensor"), spec("section", "tensor", None)
    table, bias = spec(None, "section tensor", "dp"), spec("section", "tensor")
    vector = spec("section", None, None)
    params = (layer_in, layer_back, table, bias, vector, P())
    errors = (
        spec("dp", "section", None, "tensor"),
        spec("dp", "section", "tensor", None),
        spec("dp", None, "section tensor", None),
    )
    in_specs = (
        (spec("dp", None), P(), P(), P())
        + params * 3
        + errors
        + (layer_back, layer_back, spec(None, "section tensor", None))
    )
    out_specs = (
        (P(), P())
        + params * 3
        + errors
        + (layer_back, layer_back, spec("section tensor", None), spec("section tensor", None))
    )
    return jax.shard_map(
        on_device, mesh=fine, in_specs=in_specs, out_specs=out_specs, check_vma=False
    )
```

```python
import functools
import math

import jax
import jax.numpy as jnp
import numpy as np
from jax import lax
from jax.experimental import pallas as pl
from jax.experimental.pallas import tpu as pltpu
from jax.sharding import Mesh
from jax.sharding import PartitionSpec as P

D = 512
HEAD = 64
ROT = 16
VOCAB = 50304
LAYERS = 4
LENGTH = 1024
RANK = 8
STEP = 5
BLOCK = 128

EPS_NORM = 1e-05
MOMENTUM = 0.9
NEG_BIG = -1e30
HIGH = lax.Precision.HIGHEST
BF = jnp.bfloat16
F32 = jnp.float32
MESH_ID = pl.DeviceIdType.MESH
FAR = (2, 1, 3)
PLANE = [(2, 2), (2, 1), (2, 3), (1, 2), (3, 2), (2, 0), (0, 2), (1, 1), (1, 3), (3, 1), (3, 3), (1, 0), (3, 0), (0, 1), (0, 3)]


def where_am_i():
    core, z = lax.axis_index("co"), lax.axis_index("zz")
    y = lax.axis_index("yh") * 2 + lax.axis_index("yl")
    return y, core, z


def at_chip(y, z):
    return {"yh": y // 2, "yl": lax.rem(y, 2), "zz": z}


def send(src, dst, sems, at, device):
    copy = pltpu.make_async_remote_copy(
        src_ref=src,
        dst_ref=dst,
        send_sem=sems[0].at[at],
        recv_sem=sems[1].at[at],
        device_id=device,
        device_id_type=MESH_ID,
    )
    copy.start()
    return copy


def greet(devices):
    barrier = pltpu.get_barrier_semaphore()
    for device in devices:
        pl.semaphore_signal(barrier, inc=1, device_id=device, device_id_type=MESH_ID)
    pl.semaphore_wait(barrier, len(devices))


def sem_pairs(*counts):
    return [pltpu.SemaphoreType.DMA((n,)) for n in counts for _ in range(2)]


VMEM_SPEC = pl.BlockSpec(memory_space=pltpu.VMEM)


def kernel_call(body, out_shape, args, scratch, cid=None, limit=48):
    many = isinstance(out_shape, (list, tuple))
    return pl.pallas_call(
        body,
        out_shape=out_shape,
        in_specs=[VMEM_SPEC] * len(args),
        out_specs=[VMEM_SPEC] * len(out_shape) if many else VMEM_SPEC,
        scratch_shapes=scratch,
        compiler_params=pltpu.CompilerParams(
            collective_id=cid, has_side_effects=cid is not None, vmem_limit_bytes=limit * 2**20
        ),
    )(*args)


def normed_rows(values):
    center = values - jnp.mean(values, -1, keepdims=True)
    spread = jnp.mean(center * center, -1, keepdims=True)
    scale = lax.rsqrt(spread + EPS_NORM)
    return center * scale, scale


def norm_back(values, grad):
    hat, scale = normed_rows(values)
    return scale * (
        grad
        - jnp.mean(grad, -1, keepdims=True)
        - hat * jnp.mean(grad * hat, -1, keepdims=True)
    )


def row_sum(part, r1, s, r2, sems1, sems2):
    y, core, z = where_am_i()
    first = []
    for i, k in enumerate(FAR + (0,)):
        zz = lax.rem(z + k, 4)
        first.append(send(part.at[(1 - core) * 4 + zz], r1.at[i], sems1, i, {"co": 1 - core}))
    second = []
    for i, k in enumerate(FAR):
        zz = lax.rem(z + k, 4)
        first[i].wait_recv()
        s[i] = (part[core * 4 + zz].astype(F32) + r1[i].astype(F32)).astype(BF)
        second.append(send(s.at[i], r2.at[i], sems2, i, {"zz": zz}))
    first[3].wait_recv()
    total = part[core * 4 + z].astype(F32) + r1[3].astype(F32)
    for i in range(3):
        second[i].wait_recv()
        total = total + r2[i].astype(F32)
    for copy in first + second:
        copy.wait_send()
    return total


def row_gather(everyone, sems3, sems4):
    y, core, z = where_am_i()
    own = everyone.at[core * 4 + z]
    third = [
        send(own, own, sems3, i, {"zz": lax.rem(z + k, 4)}) for i, k in enumerate(FAR)
    ]
    fourth = [send(own, own, sems4, 3, {"co": 1 - core})]
    for i, k in enumerate(FAR):
        third[i].wait_recv()
        came = everyone.at[core * 4 + lax.rem(z + 4 - k, 4)]
        fourth.append(send(came, came, sems4, i, {"co": 1 - core}))
    for copy in third:
        copy.wait_send()
    for copy in fourth:
        copy.wait()


def row_peers():
    y, core, z = where_am_i()
    return [{"co": 1 - core}] + [{"zz": lax.rem(z + k, 4)} for k in FAR]


SUM_SCRATCH = [
    pltpu.VMEM((4, BLOCK, D), BF),
    pltpu.VMEM((3, BLOCK, D), BF),
    pltpu.VMEM((3, BLOCK, D), BF),
] + sem_pairs(4, 3)
GATHER_SCRATCH = sem_pairs(3, 4)


def pair_peer():
    return [{"co": 1 - lax.axis_index("co")}]


def column_peers():
    y, core, z = where_am_i()
    return [{**at_chip(lax.rem(y + dy, 4), z), "co": c} for dy in FAR for c in (0, 1)]


def home_and_layer():
    y, core, z = where_am_i()
    return y // 2 == core, lax.rem(y, 2) * 2 + core


def take_copies(sources, places, sems, dy):
    y, core, z = where_am_i()
    return [
        pltpu.make_async_remote_copy(
            src_ref=src,
            dst_ref=dst,
            send_sem=sems[2 * n].at[dy],
            recv_sem=sems[2 * n + 1].at[0],
            device_id={**at_chip(lax.rem(y + dy, 4), z), "co": y // 2},
            device_id_type=MESH_ID,
        )
        for n, (src, dst) in enumerate(zip(sources, places))
    ]


def take_local(sources, places, sems):
    return [
        pltpu.make_async_copy(src, dst, sems[2 * n + 1].at[0])
        for n, (src, dst) in enumerate(zip(sources, places))
    ]


def take_start(layer, sources, places, sems):
    home, own = home_and_layer()

    @pl.when(own == layer)
    def _():
        for dy in FAR:
            for copy in take_copies(sources, places, sems, dy):
                copy.start()

    @pl.when(jnp.logical_and(own == layer, home))
    def _():
        for copy in take_local(sources, places, sems):
            copy.start()

    @pl.when(jnp.logical_and(own == layer, jnp.logical_not(home)))
    def _():
        for copy in take_copies(sources, places, sems, 0):
            copy.start()


def take_finish(layer, sources, places, sems):
    home, own = home_and_layer()

    @pl.when(own == layer)
    def _():
        for dy in FAR:
            for copy in take_copies(sources, places, sems, dy):
                copy.wait_send()

    @pl.when(jnp.logical_and(own == layer, jnp.logical_not(home)))
    def _():
        for copy in take_copies(sources, places, sems, 0):
            copy.wait_send()

    for copy in take_local(sources, places, sems):
        copy.wait()


def take_scratch(count):
    return [pltpu.SemaphoreType.DMA((n,)) for _ in range(count) for n in (4, 1)]


def give_copies(layer, sources, landed, sems):
    y, core, z = where_am_i()
    return [
        pltpu.make_async_remote_copy(
            src_ref=src,
            dst_ref=dst.at[y],
            send_sem=sems[2 * n].at[0],
            recv_sem=sems[2 * n + 1].at[y],
            device_id={**at_chip(core * 2 + layer // 2, z), "co": layer % 2},
            device_id_type=MESH_ID,
        )
        for n, (src, dst) in enumerate(zip(sources, landed))
    ]


def give_start(layer, sources, landed, sems):
    y, core, z = where_am_i()
    home, own = home_and_layer()
    local = jnp.logical_and(home, own == layer)

    @pl.when(jnp.logical_not(local))
    def _():
        for copy in give_copies(layer, sources, landed, sems):
            copy.start()

    @pl.when(local)
    def _():
        for n, (src, dst) in enumerate(zip(sources, landed)):
            pltpu.make_async_copy(src, dst.at[y], sems[2 * n + 1].at[y]).start()


def give_finish(layer, sources, landed, sums, sems):
    home, own = home_and_layer()

    @pl.when(own == layer)
    def _():
        for n, (src, dst) in enumerate(zip(sources, landed)):
            for index in range(4):
                pltpu.make_async_copy(src, dst.at[index], sems[2 * n + 1].at[index]).wait()
            total = dst[0].astype(F32)
            for index in range(1, 4):
                total = total + dst[index].astype(F32)
            sums[n][...] = total

    @pl.when(jnp.logical_not(jnp.logical_and(home, own == layer)))
    def _():
        for copy in give_copies(layer, sources, landed, sems):
            copy.wait_send()


def give_scratch(grads):
    return [pltpu.VMEM((4, *g.shape), g.dtype) for g in grads] + [
        pltpu.SemaphoreType.DMA((n,)) for _ in grads for n in (1, 4)
    ]


def first_body(layer, x, *refs):
    sources, everyone, places, sems = refs[:3], refs[3], refs[4:7], refs[7:]
    y, core, z = where_am_i()
    greet(row_peers() + column_peers())
    everyone[core * 4 + z] = normed_rows(x[...])[0].astype(BF)
    take_start(layer, sources, places, sems[4:])
    row_gather(everyone, sems[:2], sems[2:4])
    take_finish(layer, sources, places, sems[4:])


def first_hat(layer, x, sources):
    return kernel_call(
        functools.partial(first_body, layer),
        [jax.ShapeDtypeStruct((8, BLOCK, D), BF)]
        + [jax.ShapeDtypeStruct(a.shape, a.dtype) for a in sources],
        (x, *sources),
        GATHER_SCRATCH + take_scratch(3),
        1,
    )


def forward_body(layer, part, x, shift, *refs):
    sources, refs = (refs[:3], refs[3:]) if layer is not None else ((), refs)
    everyone, x_new, refs = refs[0], refs[1], refs[2:]
    places, refs = (refs[:3], refs[3:]) if layer is not None else ((), refs)
    r1, s, r2, e, f, g, h, a, b, c, d = refs[:11]
    sems = refs[11:]
    y, core, z = where_am_i()
    greet(row_peers() + (column_peers() if layer is not None else []))
    if layer is not None:
        take_start(layer, sources, places, sems)
    after = x[...] + row_sum(part, r1, s, r2, (e, f), (g, h)) + shift[0:1]
    x_new[...] = after
    everyone[core * 4 + z] = normed_rows(after)[0].astype(BF)
    row_gather(everyone, (a, b), (c, d))
    if layer is not None:
        take_finish(layer, sources, places, sems)


def next_hat(part, x, shift, layer=None, sources=()):
    return kernel_call(
        functools.partial(forward_body, layer),
        [jax.ShapeDtypeStruct((8, BLOCK, D), BF), jax.ShapeDtypeStruct((BLOCK, D), F32)]
        + [jax.ShapeDtypeStruct(a.shape, a.dtype) for a in sources],
        (part, x, shift, *sources),
        SUM_SCRATCH + GATHER_SCRATCH + take_scratch(len(sources)),
        10 + (layer or 0),
    )


def last_body(part, x, shift, gains, x_new, normed, r1, s, r2, e, f, g, h):
    greet(row_peers())
    after = x[...] + row_sum(part, r1, s, r2, (e, f), (g, h)) + shift[0:1]
    x_new[...] = after
    normed[...] = (normed_rows(after)[0] * gains[0:1] + gains[1:2]).astype(BF)


def last_normed(part, x, shift, gains):
    return kernel_call(
        last_body,
        [jax.ShapeDtypeStruct((BLOCK, D), F32), jax.ShapeDtypeStruct((BLOCK, D), BF)],
        (part, x, shift, gains),
        SUM_SCRATCH,
        3,
    )


def spread_body(grad, everyone, a, b, c, d):
    y, core, z = where_am_i()
    greet(row_peers())
    everyone[core * 4 + z] = grad[...].astype(BF)
    row_gather(everyone, (a, b), (c, d))


def spread_grad(grad):
    return kernel_call(
        spread_body, jax.ShapeDtypeStruct((8, BLOCK, D), BF), (grad,), GATHER_SCRATCH, 4
    )


def backward_body(layer, part, x, grad, *refs):
    sources, everyone, g_new, sums, landed = refs[:3], refs[3], refs[4], refs[5:8], refs[8:11]
    give_sems = refs[11:17]
    r1, s, r2, e, f, g, h, a, b, c, d = refs[17:]
    y, core, z = where_am_i()
    greet(row_peers() + column_peers())
    give_start(layer, sources, landed, give_sems)
    after = grad[...] + norm_back(x[...], row_sum(part, r1, s, r2, (e, f), (g, h)))
    g_new[...] = after
    everyone[core * 4 + z] = after.astype(BF)
    row_gather(everyone, (a, b), (c, d))
    give_finish(layer, sources, landed, sums, give_sems)


def next_grad(layer, part, x, grad, sources):
    return kernel_call(
        functools.partial(backward_body, layer),
        [jax.ShapeDtypeStruct((8, BLOCK, D), BF), jax.ShapeDtypeStruct((BLOCK, D), F32)]
        + [jax.ShapeDtypeStruct(a.shape, F32) for a in sources],
        (part, x, grad, *sources),
        give_scratch(sources) + SUM_SCRATCH + GATHER_SCRATCH,
        20 + layer,
    )


def lowest_body(layer, part, x, grad, *refs):
    sources, low, sums, landed, give_sems = refs[:3], refs[3], refs[4:7], refs[7:10], refs[10:16]
    r1, s, r2, e, f, g, h = refs[16:]
    greet(row_peers() + column_peers())
    give_start(layer, sources, landed, give_sems)
    after = grad[...] + norm_back(x[...], row_sum(part, r1, s, r2, (e, f), (g, h)))
    low[...] = after.astype(BF)
    give_finish(layer, sources, landed, sums, give_sems)


def lowest_grad(layer, part, x, grad, sources):
    return kernel_call(
        functools.partial(lowest_body, layer),
        [jax.ShapeDtypeStruct((BLOCK, D), BF)]
        + [jax.ShapeDtypeStruct(a.shape, F32) for a in sources],
        (part, x, grad, *sources),
        give_scratch(sources) + SUM_SCRATCH,
        6,
    )


def plane_peers():
    y, core, z = where_am_i()
    return [{"co": 1 - core}] + [
        at_chip(lax.rem(y + dy, 4), lax.rem(z + dz, 4)) for dy, dz in PLANE
    ]


def plane_sum_body(part, out, r1, s, r2, a, b, c, d):
    y, core, z = where_am_i()
    greet(plane_peers())
    first = []
    for i, (dy, dz) in enumerate(PLANE + [(0, 0)]):
        at = lax.rem(y + dy, 4) * 8 + lax.rem(z + dz, 4)
        first.append(send(part.at[at + 4 * (1 - core)], r1.at[i], (a, b), i, {"co": 1 - core}))
    second = []
    for i, (dy, dz) in enumerate(PLANE):
        yy, zz = lax.rem(y + dy, 4), lax.rem(z + dz, 4)
        first[i].wait_recv()
        s[i] = (part[yy * 8 + core * 4 + zz].astype(F32) + r1[i].astype(F32)).astype(BF)
        second.append(send(s.at[i], r2.at[i], (c, d), i, at_chip(yy, zz)))
    first[15].wait_recv()
    total = part[y * 8 + core * 4 + z].astype(F32) + r1[15].astype(F32)
    for i in range(15):
        second[i].wait_recv()
        total = total + r2[i].astype(F32)
    for copy in first + second:
        copy.wait_send()
    out[...] = total


def plane_sum(part):
    return kernel_call(
        plane_sum_body,
        jax.ShapeDtypeStruct((BLOCK, D), F32),
        (part,),
        [
            pltpu.VMEM((16, BLOCK, D), BF),
            pltpu.VMEM((15, BLOCK, D), BF),
            pltpu.VMEM((15, BLOCK, D), BF),
        ]
        + sem_pairs(16, 15),
        7,
    )


def plane_gather_body(block, everyone, a, b, c, d):
    y, core, z = where_am_i()
    greet(plane_peers())
    own = everyone.at[y * 8 + core * 4 + z]
    everyone[y * 8 + core * 4 + z] = block[...]
    first = [
        send(own, own, (a, b), i, at_chip(lax.rem(y + dy, 4), lax.rem(z + dz, 4)))
        for i, (dy, dz) in enumerate(PLANE)
    ]
    second = [send(own, own, (c, d), 15, {"co": 1 - core})]
    for i, (dy, dz) in reversed(list(enumerate(PLANE))):
        first[i].wait_recv()
        came = everyone.at[lax.rem(y + 4 - dy, 4) * 8 + core * 4 + lax.rem(z + 4 - dz, 4)]
        second.append(send(came, came, (c, d), i, {"co": 1 - core}))
    for copy in first:
        copy.wait_send()
    for copy in second:
        copy.wait()


def plane_gather(block):
    return kernel_call(
        plane_gather_body,
        jax.ShapeDtypeStruct((32, BLOCK, D), BF),
        (block,),
        sem_pairs(15, 16),
        8,
    )


def stats_body(stats, result, came, everyone, a, b, c, d):
    y, core, z = where_am_i()
    me = y * 8 + core * 4 + z
    peers = []
    for k in range(1, 32):
        p = lax.rem(me + k, 32)
        peers.append((p, {**at_chip(p // 8, lax.rem(p, 4)), "co": lax.rem(p // 4, 2)}))
    greet([device for _, device in peers])
    copies = [
        send(stats.at[p], came.at[me], (a, b), k, device) for k, (p, device) in enumerate(peers)
    ]
    came[me] = stats[me]
    for copy in copies:
        copy.wait_recv()
    top = jnp.max(came[:, 0, :], 0, keepdims=True)
    total = jnp.sum(came[:, 1, :] * jnp.exp(came[:, 0, :] - top), 0, keepdims=True)
    target = jnp.sum(came[:, 2, :], 0, keepdims=True)
    lse = top + jnp.log(total)
    everyone[me] = jnp.concatenate([lse, lse - target, jnp.zeros((6, BLOCK), F32)], 0)
    own = everyone.at[me]
    for copy in copies:
        copy.wait_send()
    copies = [send(own, own, (c, d), k, device) for k, (_, device) in enumerate(peers)]
    for copy in copies:
        copy.wait()
    result[...] = everyone[...]


def joined_stats(stats):
    return kernel_call(
        stats_body,
        jax.ShapeDtypeStruct((32, 8, BLOCK), F32),
        (stats,),
        [pltpu.VMEM((32, 8, BLOCK), F32), pltpu.VMEM((32, 8, BLOCK), F32)] + sem_pairs(31, 31),
        9,
    )


def replicas_peers():
    x = lax.axis_index("xx")
    return [(lax.rem(x + k, 4), {"xx": lax.rem(x + k, 4)}) for k in FAR]


def replicas_exchange(block, everyone, a, b):
    x = lax.axis_index("xx")
    copies = [
        send(block, everyone.at[x], (a, b), i, device)
        for i, (_, device) in enumerate(replicas_peers())
    ]
    return copies


def features_body(layers, count, block, *refs):
    sources, everyone = refs[:count], refs[count]
    places, sems = refs[count + 1 : -1], refs[-1 - 2 - 2 * count * len(layers) : -1]
    places = places[: count * len(layers)]
    own_sem = refs[-1]
    greet([device for _, device in replicas_peers()] + pair_peer() + column_peers())
    copies = replicas_exchange(block, everyone, *sems[:2])
    own = pltpu.make_async_copy(block, everyone.at[lax.axis_index("xx")], own_sem)
    own.start()
    parts = [
        (layer, sources, places[count * n : count * (n + 1)],
         sems[2 + 2 * count * n : 2 + 2 * count * (n + 1)])
        for n, layer in enumerate(layers)
    ]
    for part in parts:
        take_start(*part)
    own.wait()
    for copy in copies:
        copy.wait()
    for part in parts:
        take_finish(*part)


def all_features(block, layers, sources):
    count = len(sources)
    return pl.pallas_call(
        functools.partial(features_body, layers, count),
        out_shape=[jax.ShapeDtypeStruct((4, *block.shape), block.dtype)]
        + [jax.ShapeDtypeStruct(a.shape, a.dtype) for _ in layers for a in sources],
        in_specs=[pl.BlockSpec(memory_space=pl.ANY)] * (1 + count),
        out_specs=[pl.BlockSpec(memory_space=pl.ANY)] * (1 + count * len(layers)),
        scratch_shapes=sem_pairs(3)
        + take_scratch(count * len(layers))
        + [pltpu.SemaphoreType.DMA],
        compiler_params=pltpu.CompilerParams(collective_id=31, has_side_effects=True),
    )(block, *sources)


CHUNK = 128
TILES = D // 128


def exact_dot(left, right, contract):
    return lax.dot_general(
        left, right, (contract, ((), ())), preferred_element_type=F32, precision=HIGH
    )


def factor_places(cols, rows, vocab):
    def up(n):
        return -(-n // 128) * 128

    half = max(up(cols) + up(vocab), up(rows) + up(vocab))
    return half, ((0, 0, cols), (1, 0, rows), (0, up(cols), vocab), (1, up(rows), vocab))


def compress_body(
    vocab, g_embed, g_head, err, m_in, m_back, q_in, q_back, q_embed, q_head, bias, vectors,
    m_embed, m_head, basis, own, sums, bias_sum, vector_sum,
    left, left_came, bias_came, joint, joint_came, work, vec_came, vec_mine, vec_sums, vec_all,
    *sems,
):
    y, core, z = where_am_i()
    x = lax.axis_index("xx")
    me = y * 8 + core * 4 + z
    peers = []
    for k in range(1, 32):
        p = lax.rem(me + k, 32)
        peers.append((p, {**at_chip(p // 8, lax.rem(p, 4)), "co": lax.rem(p // 4, 2)}))
    greet([device for _, device in peers] + [device for _, device in replicas_peers()])
    pairs = [(sems[2 * n], sems[2 * n + 1]) for n in range(len(sems) // 2)]
    vec_first = [
        send(vectors.at[p], vec_came.at[me], pairs[0], k, device)
        for k, (p, device) in enumerate(peers)
    ]
    vec_came[me] = vectors[me]

    half, places = factor_places(m_in.shape[1], m_back.shape[0], vocab)
    chunks = m_embed.shape[0] // CHUNK
    whole = vocab // CHUNK
    left[...] = jnp.zeros(left.shape, F32)

    def add_rows(start, count):
        for b, (grad, out) in enumerate(((g_embed, m_embed), (g_head, m_head))):
            for tile in range(TILES):
                place = (pl.ds(start, count), pl.ds(tile * 128, 128))
                far = pl.ds(start * (2 * TILES) + 2 * tile + b, count, stride=2 * TILES)
                out[place] = grad[place] + err[far, :]

    @pl.loop(0, whole)
    def _(c):
        add_rows(pl.multiple_of(c * CHUNK, CHUNK), CHUNK)

    m_embed[pl.ds(whole * CHUNK, (chunks - whole) * CHUNK), :] = jnp.zeros(
        ((chunks - whole) * CHUNK, D), F32
    )
    m_head[pl.ds(whole * CHUNK, (chunks - whole) * CHUNK), :] = jnp.zeros(
        ((chunks - whole) * CHUNK, D), F32
    )
    add_rows(whole * CHUNK, vocab - whole * CHUNK)
    left[0] = exact_dot(q_in[...], m_in[...], ((1,), (1,)))
    left[1] = exact_dot(q_back[...], m_back[...], ((1,), (0,)))

    @pl.loop(0, chunks)
    def _(c):
        rows = pl.ds(pl.multiple_of(c * CHUNK, CHUNK), CHUNK)
        left[2] += exact_dot(q_embed[:, rows], m_embed[rows, :], ((1,), (0,)))
        left[3] += exact_dot(q_head[:, rows], m_head[rows, :], ((1,), (0,)))

    for copy in vec_first:
        copy.wait_recv()
    vec_mine[...] = jnp.sum(vec_came[...], 0)
    second = []
    for n, (src, dst) in enumerate(
        ((left, left_came), (bias, bias_came), (vec_mine, vec_sums))
    ):
        second += replicas_exchange(src, dst, *pairs[1 + n])
    left_came[x] = left[...]
    bias_came[x] = bias[...]
    vec_sums[x] = vec_mine[...]
    for copy in second:
        copy.wait()
    bias_sum[...] = jnp.sum(bias_came[...], 0)
    vec_all[me] = jnp.sum(vec_sums[...], 0)
    mine = vec_all.at[me]
    third = [send(mine, mine, pairs[4], k, device) for k, (_, device) in enumerate(peers)]
    work[...] = jnp.sum(left_came[...], 0)
    order = lax.broadcasted_iota(jnp.int32, (1, RANK, 1), 1)
    for index in range(RANK):
        columns = work[...]
        one = columns[:, index : index + 1, :]
        one = one * lax.rsqrt(jnp.sum(one * one, -1, keepdims=True) + 1e-30)
        shares = jnp.sum(columns * one, -1, keepdims=True)
        work[...] = jnp.where(order > index, columns - shares * one, columns)
        basis[:, index : index + 1, :] = one

    own[...] = jnp.zeros(own.shape, F32)
    own[0, :, pl.ds(places[0][1], places[0][2])] = exact_dot(basis[0], m_in[...], ((1,), (0,)))
    own[1, :, pl.ds(places[1][1], places[1][2])] = exact_dot(basis[1], m_back[...], ((1,), (1,)))

    @pl.loop(0, chunks)
    def _(c):
        start = pl.multiple_of(c * CHUNK, CHUNK)
        for b, matrix in ((2, m_embed), (3, m_head)):
            at = pl.ds(pl.multiple_of(places[b][1] + start, 128), CHUNK)
            own[places[b][0], :, at] = exact_dot(
                basis[b], matrix[pl.ds(start, CHUNK), :], ((1,), (1,))
            )

    joint[...] = own[...].reshape(joint.shape).astype(BF)
    fourth = replicas_exchange(joint, joint_came, *pairs[5])
    joint_came[x] = joint[...]
    for copy in fourth:
        copy.wait()
    total = jnp.sum(joint_came[...].astype(F32), 0)
    sums[...] = total.reshape(sums.shape)
    for copy in vec_first:
        copy.wait_send()
    for copy in third:
        copy.wait()
    vector_sum[...] = vec_all[...]


def compressed(vocab, g_embed, g_head, err, m_in, m_back, facs, bias, vectors):
    half, _ = factor_places(m_in.shape[1], m_back.shape[0], vocab)
    tall = g_embed.shape
    return kernel_call(
        functools.partial(compress_body, vocab),
        [
            jax.ShapeDtypeStruct(s, F32)
            for s in (tall, tall, (4, 8, D), (2, 8, half), (2, 8, half), bias.shape, vectors.shape)
        ],
        (g_embed, g_head, err, m_in, m_back, *facs, bias, vectors),
        [
            pltpu.VMEM((4, 8, D), F32),
            pltpu.VMEM((4, 4, 8, D), F32),
            pltpu.VMEM((4, *bias.shape), F32),
            pltpu.VMEM((16, half), BF),
            pltpu.VMEM((4, 16, half), BF),
            pltpu.VMEM((4, 8, D), F32),
            pltpu.VMEM(vectors.shape, F32),
            pltpu.VMEM(vectors.shape[1:], F32),
            pltpu.VMEM((4, *vectors.shape[1:]), F32),
            pltpu.VMEM(vectors.shape, F32),
        ]
        + sem_pairs(31, 3, 3, 3, 31, 3),
        30,
        56,
    )


def ema_decay():
    return min(0.999, (1.0 + STEP) / (10.0 + STEP))


def stepped(rate, weight, moment, average, grad):
    decay = ema_decay()
    new_moment = MOMENTUM * moment + (1.0 - MOMENTUM) * grad
    new_weight = weight - rate * new_moment
    return new_weight, new_moment, decay * average + (1.0 - decay) * new_weight


def update_body(
    vocab, rate_layer, rate_tables, m_embed, m_head, m_in, m_back, basis, own, sums,
    in_w, in_m, in_e, back_w, back_m, back_e, tab_w, tab_m, tab_e,
    err_tab, err_in, err_back, o_in_w, o_in_m, o_in_e, o_back_w, o_back_m, o_back_e,
    o_tab_w, o_tab_m, o_tab_e,
):
    x = lax.axis_index("xx")
    half, places = factor_places(m_in.shape[1], m_back.shape[0], vocab)
    whole = vocab // CHUNK
    own_cols = pl.ds(pl.multiple_of(x * 128, 128), 128)

    def part(ref, b, start, count):
        return ref[places[b][0], :, pl.ds(pl.multiple_of(places[b][1] + start, 128), count)]

    def table_rows(start, count):
        for b, matrix in ((2, m_embed), (3, m_head)):
            span = CHUNK
            product = exact_dot(part(own, b, start, span), basis[b], ((0,), (0,)))
            for tile in range(TILES):
                far = pl.ds(start * (2 * TILES) + 2 * tile + b - 2, count, stride=2 * TILES)
                err_tab[far, :] = (
                    matrix[pl.ds(start, count), pl.ds(tile * 128, 128)]
                    - product[:count, tile * 128 : (tile + 1) * 128]
                )
            reduced = exact_dot(part(sums, b, start, span), basis[b, :, own_cols], ((0,), (0,)))
            near = pl.ds(start * 2 + b - 2, count, stride=2)
            new = stepped(
                rate_tables[b - 2], tab_w[near, :], tab_m[near, :], tab_e[near, :], reduced[:count]
            )
            for out, value in zip((o_tab_w, o_tab_m, o_tab_e), new):
                out[near, :] = value

    @pl.loop(0, whole)
    def _(c):
        table_rows(pl.multiple_of(c * CHUNK, CHUNK), CHUNK)

    if vocab > whole * CHUNK:
        table_rows(whole * CHUNK, vocab - whole * CHUNK)

    cols, rows = places[0][2], places[1][2]

    @pl.loop(0, D // CHUNK)
    def _(c):
        at = pl.ds(pl.multiple_of(c * CHUNK, CHUNK), CHUNK)
        left = basis[0, :, at]
        err_in[at, :] = m_in[at, :] - exact_dot(left, part(own, 0, 0, cols), ((0,), (0,)))
        reduced = exact_dot(left, part(sums, 0, 0, cols), ((0,), (0,)))
        new = stepped(rate_layer, in_w[at, :], in_m[at, :], in_e[at, :], reduced)
        for out, value in zip((o_in_w, o_in_m, o_in_e), new):
            out[at, :] = value

    err_back[...] = m_back[...] - exact_dot(part(own, 1, 0, rows), basis[1], ((0,), (0,)))
    reduced = exact_dot(part(sums, 1, 0, rows), basis[1], ((0,), (0,)))
    new = stepped(rate_layer, back_w[...], back_m[...], back_e[...], reduced)
    for out, value in zip((o_back_w, o_back_m, o_back_e), new):
        out[...] = value


def updated(vocab, rates, m_tables, m_in, m_back, basis, own, sums, params, err):
    outs = [err, m_in, m_back] + list(params)
    return kernel_call(
        functools.partial(update_body, vocab, rates[0], rates[1]),
        [jax.ShapeDtypeStruct(a.shape, F32) for a in outs],
        (*m_tables, m_in, m_back, basis, own, sums, *params),
        [],
        None,
        56,
    )


def rotary_tables():
    half_rot = ROT // 2
    inverse = 10000.0 ** (-jnp.arange(half_rot, dtype=F32) * (2.0 / ROT))
    angles = jnp.arange(LENGTH, dtype=F32)[:, None] * inverse[None, :]
    return (jnp.cos(angles), jnp.sin(angles))


def rotate(heads, cosine, sine):
    half_rot = ROT // 2
    first = heads[..., :half_rot]
    second = heads[..., half_rot:ROT]
    return jnp.concatenate(
        [first * cosine - second * sine, second * cosine + first * sine, heads[..., ROT:]], -1
    )


def dot_rows(left, right):
    return lax.dot_general(
        left, right, (((0,), (0,)), ((), ())), preferred_element_type=F32
    )


def dot_cols(left, right):
    return lax.dot_general(
        left, right, (((1,), (1,)), ((), ())), preferred_element_type=F32
    )


def dot_plain(left, right):
    return jnp.dot(left, right, preferred_element_type=F32)


ATT_BLOCK = 512


def causal(start, stop):
    rows = start + lax.broadcasted_iota(jnp.int32, (stop - start, stop), 0)
    return rows >= lax.broadcasted_iota(jnp.int32, (stop - start, stop), 1)


def attention_forward(q_rot, k_rot, v_val):
    outputs, all_lse = [], []
    for start in range(0, LENGTH, ATT_BLOCK):
        stop = start + ATT_BLOCK
        scores = dot_cols(q_rot[start:stop], k_rot[:stop]) * HEAD ** (-0.5)
        scores = jnp.where(causal(start, stop), scores, NEG_BIG)
        top = jnp.max(scores, -1, keepdims=True)
        expo = jnp.exp(scores - top)
        total = jnp.sum(expo, -1, keepdims=True)
        probs = (expo / total).astype(BF)
        outputs.append(dot_plain(probs, v_val[:stop]))
        all_lse.append(top + jnp.log(total))
    return (jnp.concatenate(outputs, 0), jnp.concatenate(all_lse, 0))


def attention_backward(q_rot, k_rot, v_val, lse, grad_out):
    scale = HEAD ** (-0.5)
    grad_query, grad_key, grad_value = [], 0.0, 0.0
    for start in range(0, LENGTH, ATT_BLOCK):
        stop = start + ATT_BLOCK
        spare = ((0, LENGTH - stop), (0, 0))
        scores = dot_cols(q_rot[start:stop], k_rot[:stop]) * scale
        probs = jnp.where(causal(start, stop), jnp.exp(scores - lse[start:stop]), 0.0)
        grad_probs = dot_cols(grad_out[start:stop], v_val[:stop])
        grad_scores = (
            probs * (grad_probs - jnp.sum(grad_probs * probs, -1, keepdims=True))
        ).astype(BF)
        grad_query.append(dot_plain(grad_scores, k_rot[:stop]) * scale)
        grad_key = grad_key + jnp.pad(dot_rows(grad_scores, q_rot[start:stop]), spare) * scale
        grad_value = grad_value + jnp.pad(
            dot_rows(probs.astype(BF), grad_out[start:stop]), spare
        )
    return (jnp.concatenate(grad_query, 0), grad_key, grad_value)


def block_forward(hat, weights, cosine, sine):
    w_cols, w_rows, bias, vector = weights
    wide = hat.astype(F32)
    first_in = (wide * vector[0] + vector[1]).astype(BF)
    second_in = (wide * vector[2] + vector[3]).astype(BF)
    qkv = dot_plain(first_in, w_cols[:, : 3 * HEAD]) + bias[: 3 * HEAD]
    up_val = dot_plain(second_in, w_cols[:, 3 * HEAD :]) + bias[3 * HEAD :]
    q_rot = rotate(qkv[:, :HEAD], cosine, sine).astype(BF)
    k_rot = rotate(qkv[:, HEAD : 2 * HEAD], cosine, sine).astype(BF)
    v_val = qkv[:, 2 * HEAD :].astype(BF)
    attended, lse = attention_forward(q_rot, k_rot, v_val)
    attended = attended.astype(BF)
    hidden = jax.nn.gelu(up_val, approximate=False).astype(BF)
    branch = dot_plain(attended, w_rows[:HEAD]) + dot_plain(hidden, w_rows[HEAD:])
    return (
        branch.astype(BF),
        (hat, first_in, second_in, q_rot, k_rot, v_val, lse, attended, up_val, hidden),
    )


def gelu_exact(values):
    return jax.nn.gelu(values, approximate=False)


def block_backward(grad_low, kept, weights, cosine, sine):
    w_cols, w_rows, bias, vector = weights
    hat, first_in, second_in, q_rot, k_rot, v_val, lse, attended, up_val, hidden = kept
    grad_rows = jnp.concatenate([dot_rows(attended, grad_low), dot_rows(hidden, grad_low)], 0)
    grad_att = dot_cols(grad_low, w_rows[:HEAD]).astype(BF)
    grad_hidden = dot_cols(grad_low, w_rows[HEAD:])
    grad_up = jax.vjp(gelu_exact, up_val)[1](grad_hidden)[0].astype(BF)
    grad_query, grad_key, grad_value = attention_backward(q_rot, k_rot, v_val, lse, grad_att)
    grad_query = rotate(grad_query, cosine, -sine)
    grad_key = rotate(grad_key, cosine, -sine)
    grad_qkv = jnp.concatenate([grad_query, grad_key, grad_value], 1).astype(BF)
    grad_cols = jnp.concatenate([dot_rows(first_in, grad_qkv), dot_rows(second_in, grad_up)], 1)
    grad_bias = jnp.concatenate(
        [jnp.sum(grad_qkv.astype(F32), 0), jnp.sum(grad_up.astype(F32), 0)]
    )
    grad_first = dot_cols(grad_qkv, w_cols[:, : 3 * HEAD])
    grad_second = dot_cols(grad_up, w_cols[:, 3 * HEAD :])
    wide = hat.astype(F32)
    grad_norms = jnp.stack(
        [
            jnp.sum(grad_first * wide, 0),
            jnp.sum(grad_first, 0),
            jnp.sum(grad_second * wide, 0),
            jnp.sum(grad_second, 0),
        ]
    )
    grad_hat = grad_first * vector[0] + grad_second * vector[2]
    return (grad_hat.astype(BF), (grad_cols.astype(BF), grad_rows.astype(BF), grad_bias, grad_norms))


def on_device(
    tokens,
    groups,
    counts,
    domain,
    w_in,
    w_back,
    tables,
    b_in,
    vecs,
    final_norm,
    w_in_mom,
    w_back_mom,
    tables_mom,
    b_in_mom,
    vecs_mom,
    final_mom,
    w_in_ema,
    w_back_ema,
    tables_ema,
    b_in_ema,
    vecs_ema,
    final_ema,
    w_in_err,
    w_back_err,
    tables_err,
    w_in_fac,
    w_back_fac,
    tables_fac,
):
    y, core, z = where_am_i()
    replica = lax.axis_index("xx")
    section = lax.axis_index("yl") * 2 + core
    vocab_part = section * 8 + lax.axis_index("yh") * 4 + z
    shard = core * 4 + z
    seq_rep = tokens.shape[0]
    row_total = seq_rep * LENGTH
    vocab_shard = tables.shape[1]
    own_cols = tables.shape[2]
    cosine, sine = rotary_tables()

    seq_index = jnp.arange(groups.shape[0], dtype=jnp.int32)
    live = seq_index % seq_rep < counts[seq_index // seq_rep]
    domain_hit = groups[:, None] == jnp.arange(domain.shape[0], dtype=jnp.int32)[None, :]
    seq_weight = jnp.where(live, jnp.sum(jnp.where(domain_hit, domain[None, :], 0.0), 1), 0.0)
    weight_total = jnp.sum(seq_weight)
    own_weight = lax.dynamic_slice_in_dim(seq_weight, replica * seq_rep, seq_rep, 0)
    token_ids = tokens[:, :LENGTH].reshape(-1)
    target_ids = tokens[:, 1:].reshape(-1)
    local_ids = token_ids - vocab_part * vocab_shard
    local_targets = target_ids - vocab_part * vocab_shard

    short = tables.astype(BF)
    spare = -vocab_shard % 16
    small = jnp.concatenate(
        [
            jnp.pad(vecs[0], ((0, 2), (0, 0))),
            jnp.pad(b_in, ((0, 7), (0, D - b_in.shape[1]))),
        ]
    )
    sources = (w_in[0].astype(BF), w_back[0].astype(BF), small)
    embed_low, *taken = all_features(jnp.pad(short[0], ((0, spare), (0, 0))), (0,), sources)
    packs = {0: taken}
    embed_low = jnp.transpose(embed_low, (1, 0, 2)).reshape(vocab_shard + spare, D)
    head_low = lax.all_gather(short[1], "xx", axis=1, tiled=True)

    vocab_ids = jnp.arange(vocab_shard + spare, dtype=jnp.int32)
    looked = dot_plain((local_ids[:, None] == vocab_ids[None, :]).astype(BF), embed_low)
    x = plane_sum(looked.astype(BF).reshape(32, BLOCK, D))
    hat, *packs[1] = first_hat(1, x, sources)

    gains = jnp.pad(final_norm, ((0, 6), (0, 0)))
    weights, kept, before = [], [], []
    for index in range(LAYERS):
        cols, rows, rest = packs[index]
        weights.append((cols, rows, rest[8, : cols.shape[1]], rest))
        shift = jnp.broadcast_to((rest[4] + rest[5])[None], (8, D))
        before.append(x)
        branch, keep = block_forward(hat.reshape(LENGTH, D), weights[index], cosine, sine)
        kept.append(keep)
        branch = branch.reshape(8, BLOCK, D)
        if index + 2 < LAYERS:
            hat, x, *packs[index + 2] = next_hat(branch, x, shift, index + 2, sources)
        elif index + 1 < LAYERS:
            hat, x = next_hat(branch, x, shift)
        else:
            x, normed_own = last_normed(branch, x, shift, gains)

    normed = plane_gather(normed_own).reshape(row_total, D)
    logits = dot_cols(normed, head_low)
    target_hit = local_targets[:, None] == jnp.arange(vocab_shard, dtype=jnp.int32)[None, :]
    top_local = jnp.max(logits, 1)
    total_local = jnp.sum(jnp.exp(logits - top_local[:, None]), 1)
    target_local = jnp.sum(jnp.where(target_hit, logits, 0.0), 1)
    stats = jnp.stack([top_local, total_local, target_local]).reshape(3, 32, BLOCK)
    stats = jnp.pad(jnp.transpose(stats, (1, 0, 2)), ((0, 0), (0, 5), (0, 0)))
    joined = joined_stats(stats)
    lse_all = joined[:, 0, :].reshape(-1)
    losses = joined[:, 1, :].reshape(seq_rep, LENGTH)
    loss_part = jnp.sum(own_weight * jnp.mean(losses, 1))
    row_coef = jnp.repeat(own_weight / (weight_total * LENGTH), LENGTH)
    grad_logits = (
        (jnp.exp(logits - lse_all[:, None]) - target_hit.astype(F32)) * row_coef[:, None]
    ).astype(BF)
    grad_normed = plane_sum(dot_plain(grad_logits, head_low).astype(BF).reshape(32, BLOCK, D))
    grad_table = dot_rows(grad_logits, normed)

    hat_own, _ = normed_rows(x)
    grad_gains = jnp.stack([jnp.sum(grad_normed * hat_own, 0), jnp.sum(grad_normed, 0)])
    grad = norm_back(x, grad_normed * final_norm[0])
    grad_all = spread_grad(grad)
    pad_ids = -vocab_shard % 128
    tall_ids = jnp.arange(vocab_shard + pad_ids, dtype=jnp.int32)
    vector_rows = [None] * LAYERS
    returned = [None] * LAYERS
    for index in reversed(range(LAYERS)):
        outbias = jnp.sum(grad, 0)[None]
        grad_hat, (cols, rows, bias_row, norm_rows) = block_backward(
            grad_all.reshape(LENGTH, D), kept[index], weights[index], cosine, sine
        )
        vector_rows[index] = jnp.concatenate([norm_rows, outbias, outbias], 0)
        given = (cols, rows, jnp.pad(bias_row[None], ((0, 7), (0, D - bias_row.shape[0]))))
        grad_hat = grad_hat.reshape(8, BLOCK, D)
        if index:
            grad_all, grad, *returned[index] = next_grad(
                index, grad_hat, before[index], grad, given
            )
        else:
            grad_low, *returned[index] = lowest_grad(index, grad_hat, before[index], grad, given)
    grad_embedded = plane_gather(grad_low).reshape(row_total, D)
    inside_ids = jnp.where(local_ids < vocab_shard, local_ids, -1)
    grad_embed = dot_rows(
        (inside_ids[:, None] == tall_ids[None, :]).astype(BF), grad_embedded
    )
    grad_table = jnp.pad(grad_table, ((0, pad_ids), (0, 0)))

    def of_own_layer(n):
        picked = returned[LAYERS - 1][n]
        for index in range(LAYERS - 1):
            picked = jnp.where(section == index, returned[index][n], picked)
        return picked

    loss_row = jnp.zeros((1, D), F32).at[0, 0].set(jnp.where(shard + y * 8 == 0, loss_part, 0.0))
    vectors = jnp.concatenate(vector_rows + [grad_gains, loss_row], 0)
    vectors = jnp.pad(vectors, ((0, 32 - vectors.shape[0]), (0, 0))).reshape(32, D // 128, 128)
    vectors = jnp.pad(vectors, ((0, 0), (0, 8 - D // 128), (0, 0)))
    full_in = of_own_layer(0) + w_in_err[0, 0]
    full_back = of_own_layer(1) + w_back_err[0, 0]
    err = jnp.transpose(
        tables_err.reshape(2, vocab_shard, D // 128, 128), (1, 2, 0, 3)
    ).reshape(-1, 128)
    facs = (
        w_in_fac[0].T,
        w_back_fac[0].T,
        jnp.pad(tables_fac[0].T, ((0, 0), (0, pad_ids))),
        jnp.pad(tables_fac[1].T, ((0, 0), (0, pad_ids))),
    )
    m_embed, m_head, basis, own, sums, bias_sum, vector_sums = compressed(
        vocab_shard, grad_embed, grad_table, err, full_in, full_back, facs, of_own_layer(2), vectors
    )
    bias_sum = bias_sum[:1, : b_in.shape[1]]
    vector_sums = vector_sums[:, : D // 128, :].reshape(32, D)
    vec_sum = lax.dynamic_slice_in_dim(vector_sums, section * 6, 6, 0)
    final_sum = vector_sums[6 * LAYERS : 6 * LAYERS + 2]
    loss_sum = vector_sums[6 * LAYERS + 2, 0]

    def of_tables(arrays):
        return [jnp.transpose(a, (1, 0, 2)).reshape(-1, 128) for a in arrays]

    token_count = lax.axis_size("xx") * seq_rep * LENGTH
    rate_layer = 2.0 * math.sqrt(token_count)
    rate_vector = 6.0 * math.sqrt(token_count)
    rate_tables = [rate * math.sqrt(token_count * VOCAB) for rate in (50.0, 0.5)]
    params = (
        [w_in[0], w_in_mom[0], w_in_ema[0], w_back[0], w_back_mom[0], w_back_ema[0]]
        + of_tables((tables, tables_mom, tables_ema))
    )
    err_tab, err_in, err_back, *new = updated(
        vocab_shard, (rate_layer, rate_tables), (m_embed, m_head), full_in, full_back,
        basis, own, sums, params, err,
    )
    err_tab = jnp.transpose(
        err_tab.reshape(vocab_shard, D // 128, 2, 128), (2, 0, 1, 3)
    ).reshape(tables_err.shape)
    in_w, in_m, in_e, back_w, back_m, back_e = [a[None] for a in new[:6]]
    tab_w, tab_m, tab_e = [
        jnp.transpose(a.reshape(vocab_shard, 2, own_cols), (1, 0, 2)) for a in new[6:]
    ]
    _, places = factor_places(full_in.shape[1], full_back.shape[0], vocab_shard)
    fac_in, fac_back, fac_embed, fac_head = [
        sums[half, :, at : at + width].T for half, at, width in places
    ]
    bias_w, bias_m, bias_e = stepped(rate_layer, b_in, b_in_mom, b_in_ema, bias_sum)
    vec_w, vec_m, vec_e = stepped(rate_vector, vecs, vecs_mom, vecs_ema, vec_sum[None])
    fin_w, fin_m, fin_e = stepped(rate_layer, final_norm, final_mom, final_ema, final_sum)
    return (
        loss_sum,
        weight_total,
        in_w,
        back_w,
        tab_w,
        bias_w,
        vec_w,
        fin_w,
        in_m,
        back_m,
        tab_m,
        bias_m,
        vec_m,
        fin_m,
        in_e,
        back_e,
        tab_e,
        bias_e,
        vec_e,
        fin_e,
        err_in[None, None],
        err_back[None, None],
        err_tab,
        fac_in[None],
        fac_back[None],
        fac_embed,
        fac_head,
    )


def solution(mesh):
    fine = Mesh(
        np.asarray(mesh.devices).reshape(2, 2, 2, 4, 4), ("yl", "co", "yh", "zz", "xx")
    )
    names = {"section": ("yl", "co"), "tensor": ("yh", "zz"), "dp": ("xx",)}

    def spec(*axes):
        return P(*[None if a is None else sum((names[n] for n in a.split()), ()) for a in axes])

    layer_in, layer_back = spec("section", None, "tensor"), spec("section", "tensor", None)
    table, bias = spec(None, "section tensor", "dp"), spec("section", "tensor")
    vector = spec("section", None, None)
    params = (layer_in, layer_back, table, bias, vector, P())
    errors = (
        spec("dp", "section", None, "tensor"),
        spec("dp", "section", "tensor", None),
        spec("dp", None, "section tensor", None),
    )
    in_specs = (
        (spec("dp", None), P(), P(), P())
        + params * 3
        + errors
        + (layer_back, layer_back, spec(None, "section tensor", None))
    )
    out_specs = (
        (P(), P())
        + params * 3
        + errors
        + (layer_back, layer_back, spec("section tensor", None), spec("section tensor", None))
    )
    return jax.shard_map(
        on_device, mesh=fine, in_specs=in_specs, out_specs=out_specs, check_vma=False
    )
```

```python
import functools
import math

import jax
import jax.numpy as jnp
import numpy as np
from jax import lax
from jax.experimental import pallas as pl
from jax.experimental.pallas import tpu as pltpu
from jax.sharding import Mesh
from jax.sharding import PartitionSpec as P

D = 512
HEAD = 64
ROT = 16
VOCAB = 50304
LAYERS = 4
LENGTH = 1024
RANK = 8
STEP = 5
BLOCK = 128
CHUNK = 128
TILES = D // 128

EPS_NORM = 1e-05
MOMENTUM = 0.9
NEG_BIG = -1e30
HIGH = lax.Precision.HIGHEST
BF = jnp.bfloat16
F32 = jnp.float32
MESH_ID = pl.DeviceIdType.MESH
FAR = (2, 1, 3)


def where_am_i():
    core, z = lax.axis_index("co"), lax.axis_index("zz")
    y = lax.axis_index("yh") * 2 + lax.axis_index("yl")
    return y, core, z


def at_chip(y, z):
    return {"yh": y // 2, "yl": lax.rem(y, 2), "zz": z}


def send(src, dst, sems, at, device):
    copy = pltpu.make_async_remote_copy(
        src_ref=src,
        dst_ref=dst,
        send_sem=sems[0].at[at],
        recv_sem=sems[1].at[at],
        device_id=device,
        device_id_type=MESH_ID,
    )
    copy.start()
    return copy


def greet(devices):
    barrier = pltpu.get_barrier_semaphore()
    for device in devices:
        pl.semaphore_signal(barrier, inc=1, device_id=device, device_id_type=MESH_ID)
    pl.semaphore_wait(barrier, len(devices))


def sem_pairs(*counts):
    return [pltpu.SemaphoreType.DMA((n,)) for n in counts for _ in range(2)]


VMEM_SPEC = pl.BlockSpec(memory_space=pltpu.VMEM)


def kernel_call(
    body, out_shape, args, scratch, cid=None, limit=48, in_specs=None, out_specs=None
):
    many = isinstance(out_shape, (list, tuple))
    return pl.pallas_call(
        body,
        out_shape=out_shape,
        in_specs=in_specs or [VMEM_SPEC] * len(args),
        out_specs=out_specs or ([VMEM_SPEC] * len(out_shape) if many else VMEM_SPEC),
        scratch_shapes=scratch,
        compiler_params=pltpu.CompilerParams(
            collective_id=cid, has_side_effects=cid is not None, vmem_limit_bytes=limit * 2**20
        ),
    )(*args)


def dot_rows(left, right):
    return lax.dot_general(
        left, right, (((0,), (0,)), ((), ())), preferred_element_type=F32
    )


def dot_cols(left, right):
    return lax.dot_general(
        left, right, (((1,), (1,)), ((), ())), preferred_element_type=F32
    )


def dot_plain(left, right):
    return jnp.dot(left, right, preferred_element_type=F32)


def normed_rows(values):
    center = values - jnp.mean(values, -1, keepdims=True)
    spread = jnp.mean(center * center, -1, keepdims=True)
    scale = lax.rsqrt(spread + EPS_NORM)
    return center * scale, scale


def norm_back(values, grad):
    hat, scale = normed_rows(values)
    return scale * (
        grad
        - jnp.mean(grad, -1, keepdims=True)
        - hat * jnp.mean(grad * hat, -1, keepdims=True)
    )


def row_sum(part, r1, s, r2, sems1, sems2, meanwhile=None):
    y, core, z = where_am_i()
    first = []
    for i, k in enumerate(FAR + (0,)):
        zz = lax.rem(z + k, 4)
        first.append(send(part.at[zz * 2 + 1 - core], r1.at[i], sems1, i, {"co": 1 - core}))
    second = []
    for i, k in enumerate(FAR):
        zz = lax.rem(z + k, 4)
        first[i].wait_recv()
        s[i] = (part[zz * 2 + core].astype(F32) + r1[i].astype(F32)).astype(BF)
        second.append(send(s.at[i], r2.at[i], sems2, i, {"zz": zz}))
    if meanwhile is not None:
        meanwhile()
    first[3].wait_recv()
    total = part[z * 2 + core].astype(F32) + r1[3].astype(F32)
    for i in range(3):
        second[i].wait_recv()
        total = total + r2[i].astype(F32)
    for copy in first + second:
        copy.wait_send()
    return total


def row_gather(everyone, sems3, sems4, meanwhile=None):
    y, core, z = where_am_i()
    own = everyone.at[z * 2 + core]
    third = [
        send(own, own, sems3, i, {"zz": lax.rem(z + k, 4)}) for i, k in enumerate(FAR)
    ]
    fourth = [send(own, own, sems4, 3, {"co": 1 - core})]
    if meanwhile is not None:
        meanwhile()
    for i, k in enumerate(FAR):
        third[i].wait_recv()
        came = everyone.at[lax.rem(z + 4 - k, 4) * 2 + core]
        fourth.append(send(came, came, sems4, i, {"co": 1 - core}))
    for copy in third:
        copy.wait_send()
    for copy in fourth:
        copy.wait()


def row_peers():
    y, core, z = where_am_i()
    return [{"co": 1 - core}] + [{"zz": lax.rem(z + k, 4)} for k in FAR]


SUM_SCRATCH = [
    pltpu.VMEM((4, BLOCK, D), BF),
    pltpu.VMEM((3, BLOCK, D), BF),
    pltpu.VMEM((3, BLOCK, D), BF),
] + sem_pairs(4, 3)
GATHER_SCRATCH = sem_pairs(3, 4)


def pair_peer():
    return [{"co": 1 - lax.axis_index("co")}]


def column_peers():
    y, core, z = where_am_i()
    return [{**at_chip(lax.rem(y + dy, 4), z), "co": c} for dy in FAR for c in (0, 1)]


def column_others():
    y, core, z = where_am_i()
    return [{**at_chip(lax.rem(y + dy, 4), z), "co": 1 - core} for dy in FAR]


def home_and_layer():
    y, core, z = where_am_i()
    return y // 2 == core, lax.rem(y, 2) * 2 + core


def take_copies(sources, places, sems, dy):
    y, core, z = where_am_i()
    return [
        pltpu.make_async_remote_copy(
            src_ref=src,
            dst_ref=dst,
            send_sem=sems[2 * n].at[dy],
            recv_sem=sems[2 * n + 1].at[0],
            device_id={**at_chip(lax.rem(y + dy, 4), z), "co": y // 2},
            device_id_type=MESH_ID,
        )
        for n, (src, dst) in enumerate(zip(sources, places))
    ]


def take_local(sources, places, sems):
    return [
        pltpu.make_async_copy(src, dst, sems[2 * n + 1].at[0])
        for n, (src, dst) in enumerate(zip(sources, places))
    ]


def take_start(layer, sources, places, sems):
    home, own = home_and_layer()

    @pl.when(own == layer)
    def _():
        for dy in FAR:
            for copy in take_copies(sources, places, sems, dy):
                copy.start()

    @pl.when(jnp.logical_and(own == layer, home))
    def _():
        for copy in take_local(sources, places, sems):
            copy.start()

    @pl.when(jnp.logical_and(own == layer, jnp.logical_not(home)))
    def _():
        for copy in take_copies(sources, places, sems, 0):
            copy.start()


def take_finish(layer, sources, places, sems):
    home, own = home_and_layer()

    @pl.when(own == layer)
    def _():
        for dy in FAR:
            for copy in take_copies(sources, places, sems, dy):
                copy.wait_send()

    @pl.when(jnp.logical_and(own == layer, jnp.logical_not(home)))
    def _():
        for copy in take_copies(sources, places, sems, 0):
            copy.wait_send()

    for copy in take_local(sources, places, sems):
        copy.wait()


def take_scratch(count):
    return [pltpu.SemaphoreType.DMA((n,)) for _ in range(count) for n in (4, 1)]


def give_copies(layer, sources, landed, sems):
    y, core, z = where_am_i()
    return [
        pltpu.make_async_remote_copy(
            src_ref=src,
            dst_ref=dst.at[y],
            send_sem=sems[2 * n].at[0],
            recv_sem=sems[2 * n + 1].at[y],
            device_id={**at_chip(core * 2 + layer // 2, z), "co": layer % 2},
            device_id_type=MESH_ID,
        )
        for n, (src, dst) in enumerate(zip(sources, landed))
    ]


def give_start(layer, sources, landed, sems):
    y, core, z = where_am_i()
    home, own = home_and_layer()
    local = jnp.logical_and(home, own == layer)

    @pl.when(jnp.logical_not(local))
    def _():
        for copy in give_copies(layer, sources, landed, sems):
            copy.start()

    @pl.when(local)
    def _():
        for n, (src, dst) in enumerate(zip(sources, landed)):
            pltpu.make_async_copy(src, dst.at[y], sems[2 * n + 1].at[y]).start()


def give_finish(layer, sources, landed, sums, sems):
    home, own = home_and_layer()

    @pl.when(own == layer)
    def _():
        for n, (src, dst) in enumerate(zip(sources, landed)):
            for index in range(4):
                pltpu.make_async_copy(src, dst.at[index], sems[2 * n + 1].at[index]).wait()
            total = dst[0].astype(F32)
            for index in range(1, 4):
                total = total + dst[index].astype(F32)
            sums[n][...] = total

    @pl.when(jnp.logical_not(jnp.logical_and(home, own == layer)))
    def _():
        for copy in give_copies(layer, sources, landed, sems):
            copy.wait_send()


def give_scratch(grads):
    return [pltpu.VMEM((4, *g.shape), g.dtype) for g in grads] + [
        pltpu.SemaphoreType.DMA((n,)) for _ in grads for n in (1, 4)
    ]


def forward_body(layer, part, x, shift, *refs):
    sources, everyone, x_new, places, refs = refs[:2], refs[2], refs[3], refs[4:6], refs[6:]
    r1, s, r2, e, f, g, h, a, b, c, d = refs[:11]
    sems = refs[11:]
    y, core, z = where_am_i()
    greet(row_peers() + column_peers())
    take_start(layer, sources, places, sems)
    after = x[...] + row_sum(part, r1, s, r2, (e, f), (g, h)) + shift[0:1]
    x_new[...] = after
    everyone[z * 2 + core] = normed_rows(after)[0].astype(BF)
    row_gather(everyone, (a, b), (c, d))
    take_finish(layer, sources, places, sems)


def next_hat(part, x, shift, layer, sources):
    return kernel_call(
        functools.partial(forward_body, layer),
        [jax.ShapeDtypeStruct((8, BLOCK, D), BF), jax.ShapeDtypeStruct((BLOCK, D), F32)]
        + [jax.ShapeDtypeStruct(a.shape, a.dtype) for a in sources],
        (part, x, shift, *sources),
        SUM_SCRATCH + GATHER_SCRATCH + take_scratch(len(sources)),
        10 + layer,
    )


def backward_body(layer, table_parts, part, x, grad, *refs):
    sources, refs = refs[:2], refs[2:]
    begun, steep, tokens = (), None, None
    if table_parts:
        steep, tokens, refs = refs[0], refs[1], refs[2:]
        if table_parts[0]:
            begun, refs = refs[:1], refs[1:]
    everyone, g_new, sums, refs = refs[0], refs[1], refs[2:4], refs[4:]
    if table_parts:
        table_grad, refs = refs[0], refs[1:]
    landed, give_sems, refs = refs[:2], refs[2:6], refs[6:]
    r1, s, r2, e, f, g, h, a, b, c, d = refs[:11]
    y, core, z = where_am_i()
    greet(row_peers() + column_peers())
    hooks = [None, None]
    if table_parts:
        slopes, rows, sem_slopes, sem_rows = refs[11:]
        loads = []
        for n, q in enumerate(table_parts):
            loads.append(
                (
                    pltpu.make_async_copy(steep.at[q], slopes.at[n], sem_slopes.at[n]),
                    pltpu.make_async_copy(
                        tokens.at[pl.ds(q * 4, 4)], rows.at[pl.ds(n * 4, 4)], sem_rows.at[n]
                    ),
                )
            )
            for load in loads[n]:
                load.start()

        def table_step(n):
            for load in loads[n]:
                load.wait()
            product = dot_plain(slopes[n], rows[pl.ds(n * 4, 4)].reshape(8 * BLOCK, D))
            if n:
                table_grad[...] += product
            else:
                table_grad[...] = begun[0][...] + product if begun else product

        hooks = [lambda: table_step(0), lambda: table_step(1)]
    give_start(layer, sources, landed, give_sems)
    after = grad[...] + norm_back(x[...], row_sum(part, r1, s, r2, (e, f), (g, h), hooks[0]))
    g_new[...] = after
    everyone[z * 2 + core] = after.astype(BF)
    row_gather(everyone, (a, b), (c, d), hooks[1])
    give_finish(layer, sources, landed, sums, give_sems)


def next_grad(layer, part, x, grad, sources, table_parts=(), steep=None, tokens=None, begun=None):
    args, outs, scratch = [], [], []
    if table_parts:
        args = [steep, tokens] + ([] if begun is None else [begun])
        outs = [jax.ShapeDtypeStruct((steep.shape[1], D), F32)]
        scratch = [
            pltpu.VMEM((2, *steep.shape[1:]), BF),
            pltpu.VMEM((8, *tokens.shape[1:]), BF),
            pltpu.SemaphoreType.DMA((2,)),
            pltpu.SemaphoreType.DMA((2,)),
        ]
    specs = [VMEM_SPEC] * (3 + len(sources)) + [pl.BlockSpec(memory_space=pl.ANY)] * 2 + [VMEM_SPEC]
    return kernel_call(
        functools.partial(backward_body, layer, table_parts),
        [jax.ShapeDtypeStruct((8, BLOCK, D), BF), jax.ShapeDtypeStruct((BLOCK, D), F32)]
        + [jax.ShapeDtypeStruct(a.shape, F32) for a in sources]
        + outs,
        (part, x, grad, *sources, *args),
        give_scratch(sources) + SUM_SCRATCH + GATHER_SCRATCH + scratch,
        20 + layer,
        in_specs=specs[: 3 + len(sources) + len(args)],
    )


def offset(i):
    at = lax.rem(jnp.int32(i) * 5, 16)
    return lax.div(at, 4), lax.rem(at, 4)


def chip(i, sign):
    y, _, z = where_am_i()
    dy, dz = offset(i)
    return lax.rem(y + sign * dy + 4, 4), lax.rem(z + sign * dz + 4, 4)


def plane_peers(both_cores):
    y, core, z = where_am_i()
    found = [{"co": 1 - core}]
    for i in range(1, 16):
        for c in (core, 1 - core) if both_cores else (core,):
            found.append({**at_chip(*chip(i, 1)), "co": c})
    return found


def remote(src, dst, send_sem, recv_sem, device):
    return pltpu.make_async_remote_copy(
        src_ref=src,
        dst_ref=dst,
        send_sem=send_sem,
        recv_sem=recv_sem,
        device_id=device,
        device_id_type=MESH_ID,
    )


def core_rows(core):
    return pl.ds(pl.multiple_of(core * BLOCK, BLOCK), BLOCK)


def plane_collect(everyone, sems, on_chip):
    y, core, z = where_am_i()
    a, b, c, d = sems
    own = everyone.at[y * 4 + z, core_rows(core)]

    def direct(i):
        return remote(own, own, a.at[i], b.at[i], at_chip(*chip(i, 1)))

    def across(i):
        yy, zz = chip(i, -1)
        came = everyone.at[yy * 4 + zz, core_rows(core)]
        return remote(came, came, c.at[i], d.at[i], {"co": 1 - core})

    across(0).start()

    @pl.loop(1, 16)
    def _(i):
        direct(i).start()

    def use(i):
        across(i).wait_recv()
        yy, zz = chip(i, -1)
        on_chip(i, yy * 4 + zz)

    direct(1).wait_recv()
    across(1).start()
    use(0)

    @pl.loop(2, 16)
    def _(i):
        direct(i).wait_recv()
        across(i).start()
        use(i - 1)

    use(15)

    @pl.loop(1, 16)
    def _(i):
        direct(i).wait_send()
        across(i).wait_send()

    across(0).wait_send()


COLLECT_SEMS = sem_pairs(16, 16)


def plane_total(group, between, keep, other, r1, s, r2, sems):
    y, core, z = where_am_i()
    a, b, c, d = sems

    def pair(i):
        return remote(other.at[i], r1.at[i], a.at[i], b.at[i], {"co": 1 - core})

    def away(i):
        return remote(s.at[i], r2.at[i], c.at[i], d.at[i], at_chip(*chip(i, 1)))

    def make(i):
        yy, zz = chip(i, 1)
        part = group(yy * 4 + zz)
        low, high = part[:, :BLOCK], part[:, BLOCK:]
        keep[i] = jnp.where(core == 0, low, high).astype(BF)
        other[i] = jnp.where(core == 0, high, low).astype(BF)
        pair(i).start()

    def forward(i):
        pair(i).wait_recv()
        s[i] = (keep[i].astype(F32) + r1[i].astype(F32)).astype(BF)
        away(i).start()

    make(1)

    @pl.loop(2, 16)
    def _(i):
        make(i)
        forward(i - 1)

    forward(15)
    make(0)
    between()
    pair(0).wait_recv()
    total = keep[0].astype(F32) + r1[0].astype(F32)

    def add(i, total):
        away(i).wait_recv()
        return total + r2[i].astype(F32)

    total = lax.fori_loop(1, 16, add, total)

    @pl.loop(1, 16)
    def _(i):
        pair(i).wait_send()
        away(i).wait_send()

    pair(0).wait_send()
    return total


TOTAL_SCRATCH = [pltpu.VMEM((16, D, BLOCK), BF) for _ in range(5)] + sem_pairs(16, 16)


def vocab_rows(v, rows):
    return v * rows + lax.broadcasted_iota(jnp.int32, (rows, 1), 0)


def onehot_into(place, ids):
    rows = place.shape[0]

    @pl.loop(0, rows // 128)
    def _(v):
        hit = vocab_rows(v, 128) == ids
        place[pl.ds(pl.multiple_of(v * 128, 128), 128), :] = jnp.where(hit, 1.0, 0.0).astype(BF)


def embed_body(table, ids, x, everyone, hot, keep, other, r1, s, r2, e, f, g, h, a, b, c, d):
    y, core, z = where_am_i()
    greet(plane_peers(False))

    def group(c):
        onehot_into(hot, ids[c])
        return jnp.dot(table[...], hot[...], preferred_element_type=F32)

    total = plane_total(group, lambda: None, keep, other, r1, s, r2, (e, f, g, h))
    rows = jnp.transpose(total)
    x[...] = rows
    everyone[z * 2 + core] = normed_rows(rows)[0].astype(BF)
    row_gather(everyone, (a, b), (c, d))


def embedded(table, ids):
    return kernel_call(
        embed_body,
        [jax.ShapeDtypeStruct((BLOCK, D), F32), jax.ShapeDtypeStruct((8, BLOCK, D), BF)],
        (table, ids),
        [pltpu.VMEM((table.shape[1], 2 * BLOCK), BF)] + TOTAL_SCRATCH + GATHER_SCRATCH,
        7,
    )


def lse_body(
    vocab, part, x, shift, gains, head, targets,
    x_new, everyone, probs, stats, joined, logits, came, r1, s, r2, *sems,
):
    y, core, z = where_am_i()
    greet(plane_peers(True))
    here = y * 4 + z
    a, b, c, d = sems[8:]
    after = x[...] + row_sum(part, r1, s, r2, sems[0:2], sems[2:4]) + shift[0:1]
    x_new[...] = after
    everyone[here, core_rows(core)] = (
        normed_rows(after)[0] * gains[0:1] + gains[1:2]
    ).astype(BF)
    tall = head.shape[0]

    def stat_copy(i, flip, where):
        device = {**at_chip(*chip(i, -1)), "co": core if flip == 0 else 1 - core}
        to = core if flip == 0 else 1 - core
        return remote(
            stats.at[where, to], came.at[2 * i + flip], a.at[2 * i + flip], b.at[2 * i + flip], device
        )

    def on_chip(i, where):
        logits[...] = dot_cols(head[...], everyone[where])
        wanted = targets[where]

        def highest(v, top):
            rows = pl.ds(pl.multiple_of(v * 128, 128), 128)
            value = jnp.where(vocab_rows(v, 128) < vocab, logits[rows, :], NEG_BIG)
            logits[rows, :] = value
            return jnp.maximum(top, jnp.max(value.reshape(16, 8, 2 * BLOCK), 0))

        top = lax.fori_loop(0, tall // 128, highest, jnp.full((8, 2 * BLOCK), NEG_BIG, F32))
        top = jnp.max(top, 0, keepdims=True)

        def summed(v, carry):
            rows = pl.ds(pl.multiple_of(v * 128, 128), 128)
            value = logits[rows, :]
            expo = jnp.exp(value - top)
            probs[where, rows, :] = expo.astype(BF)
            hit = jnp.where(vocab_rows(v, 128) == wanted, value, 0.0)
            return (
                carry[0] + jnp.sum(expo.reshape(16, 8, 2 * BLOCK), 0),
                carry[1] + jnp.sum(hit.reshape(16, 8, 2 * BLOCK), 0),
            )

        zero = jnp.zeros((8, 2 * BLOCK), F32)
        total, target = lax.fori_loop(0, tall // 128, summed, (zero, zero))
        found = jnp.concatenate(
            [
                top,
                jnp.sum(total, 0, keepdims=True),
                jnp.sum(target, 0, keepdims=True),
                jnp.zeros((5, 2 * BLOCK), F32),
            ],
            0,
        )
        stats[where, 0] = found[:, :BLOCK]
        stats[where, 1] = found[:, BLOCK:]
        if isinstance(i, int) and i == 0:
            came[0] = stats[where, core]
        else:
            stat_copy(i, 0, where).start()
        stat_copy(i, 1, where).start()

    plane_collect(everyone, sems[4:8], on_chip)

    @pl.loop(1, 16)
    def _(i):
        stat_copy(i, 0, here).wait()
        stat_copy(i, 1, here).wait()

    stat_copy(0, 1, here).wait()
    top = jnp.max(came[:, 0, :], 0, keepdims=True)
    total = jnp.sum(came[:, 1, :] * jnp.exp(came[:, 0, :] - top), 0, keepdims=True)
    target = jnp.sum(came[:, 2, :], 0, keepdims=True)
    lse = top + jnp.log(total)
    joined[here, core] = jnp.concatenate([lse, lse - target, jnp.zeros((6, BLOCK), F32)], 0)
    mine = joined.at[here, core]

    def lse_copy(i, flip):
        device = {**at_chip(*chip(i, 1)), "co": core if flip == 0 else 1 - core}
        return remote(mine, mine, c.at[2 * i + flip], d.at[2 * i + flip], device)

    lse_copy(0, 1).start()

    @pl.loop(1, 16)
    def _(i):
        lse_copy(i, 0).start()
        lse_copy(i, 1).start()

    @pl.loop(1, 16)
    def _(i):
        lse_copy(i, 0).wait()
        lse_copy(i, 1).wait()

    lse_copy(0, 1).wait()


def last_and_lse(vocab, part, x, shift, gains, head, targets):
    tall = head.shape[0]
    return kernel_call(
        functools.partial(lse_body, vocab),
        [
            jax.ShapeDtypeStruct((BLOCK, D), F32),
            jax.ShapeDtypeStruct((16, 2 * BLOCK, D), BF),
            jax.ShapeDtypeStruct((16, tall, 2 * BLOCK), BF),
            jax.ShapeDtypeStruct((16, 2, 8, BLOCK), F32),
            jax.ShapeDtypeStruct((16, 2, 8, BLOCK), F32),
        ],
        (part, x, shift, gains, head, targets),
        [pltpu.VMEM((tall, 2 * BLOCK), F32), pltpu.VMEM((32, 8, BLOCK), F32)]
        + SUM_SCRATCH
        + COLLECT_SEMS
        + sem_pairs(32, 32),
        8,
        56,
    )


def loss_back_body(
    probs, stats, joined, targets, coefs, head_t, x, gains,
    steep, row_all, grad, grad_gains, slopes, keep, other, r1, s, r2, *sems,
):
    y, core, z = where_am_i()
    greet(plane_peers(False))
    tall = head_t.shape[1]
    written = pltpu.make_async_copy(slopes, steep, sems[8])

    def group(c):
        def row(ref):
            return jnp.concatenate([ref[c, 0, 0:1, :], ref[c, 1, 0:1, :]], 1)

        coef, wanted = coefs[c], targets[c]
        scale = jnp.exp(row(stats) - row(joined)) * coef
        lanes = pl.ds(pl.multiple_of(lax.rem(c, 4) * (2 * BLOCK), 2 * BLOCK), 2 * BLOCK)

        @pl.loop(0, tall // 128)
        def _(v):
            rows = pl.ds(pl.multiple_of(v * 128, 128), 128)
            hit = jnp.where(vocab_rows(v, 128) == wanted, coef, 0.0)
            slopes[lax.div(c, 4), rows, lanes] = (
                probs[c, rows, :].astype(F32) * scale - hit
            ).astype(BF)

        return jnp.dot(
            head_t[...], slopes[lax.div(c, 4), :, lanes], preferred_element_type=F32
        )

    total = plane_total(group, lambda: written.start(), keep, other, r1, s, r2, sems[:4])
    normed_grad = jnp.transpose(total)
    hat, _ = normed_rows(x[...])
    grad_gains[...] = jnp.concatenate(
        [
            jnp.sum(normed_grad * hat, 0, keepdims=True),
            jnp.sum(normed_grad, 0, keepdims=True),
            jnp.zeros((6, D), F32),
        ],
        0,
    )
    after = norm_back(x[...], normed_grad * gains[0:1])
    grad[...] = after
    row_all[z * 2 + core] = after.astype(BF)
    row_gather(row_all, sems[4:6], sems[6:8])
    written.wait()


def loss_back(probs, stats, joined, targets, coefs, head_t, x, gains):
    tall = head_t.shape[1]
    return kernel_call(
        loss_back_body,
        [
            jax.ShapeDtypeStruct((4, tall, 8 * BLOCK), BF),
            jax.ShapeDtypeStruct((8, BLOCK, D), BF),
            jax.ShapeDtypeStruct((BLOCK, D), F32),
            jax.ShapeDtypeStruct((8, D), F32),
        ],
        (probs, stats, joined, targets, coefs, head_t, x, gains),
        [pltpu.VMEM((4, tall, 8 * BLOCK), BF)]
        + TOTAL_SCRATCH
        + GATHER_SCRATCH
        + [pltpu.SemaphoreType.DMA],
        9,
        56,
        out_specs=[pl.BlockSpec(memory_space=pl.ANY)] + [VMEM_SPEC] * 3,
    )


def lowest_body(layer, part, x, grad, ids, *refs):
    sources, grad_embed, sums, landed, give_sems = (
        refs[:2], refs[2], refs[3:5], refs[5:7], refs[7:11],
    )
    r1, s, r2, e, f, g, h, everyone, hot = refs[11:20]
    y, core, z = where_am_i()
    greet(plane_peers(False) + column_others())
    give_start(layer, sources, landed, give_sems)
    after = grad[...] + norm_back(x[...], row_sum(part, r1, s, r2, (e, f), (g, h)))
    everyone[y * 4 + z, core_rows(core)] = after.astype(BF)
    grad_embed[...] = jnp.zeros(grad_embed.shape, F32)

    def on_chip(i, where):
        onehot_into(hot, ids[where])
        grad_embed[...] += jnp.dot(hot[...], everyone[where], preferred_element_type=F32)

    plane_collect(everyone, refs[20:], on_chip)
    give_finish(layer, sources, landed, sums, give_sems)


def lowest_grad(layer, part, x, grad, ids, sources, tall):
    return kernel_call(
        functools.partial(lowest_body, layer),
        [jax.ShapeDtypeStruct((tall, D), F32)]
        + [jax.ShapeDtypeStruct(a.shape, F32) for a in sources],
        (part, x, grad, ids, *sources),
        give_scratch(sources)
        + SUM_SCRATCH
        + [pltpu.VMEM((16, 2 * BLOCK, D), BF), pltpu.VMEM((tall, 2 * BLOCK), BF)]
        + COLLECT_SEMS,
        6,
        56,
    )


def replicas_peers():
    x = lax.axis_index("xx")
    return [(lax.rem(x + k, 4), {"xx": lax.rem(x + k, 4)}) for k in FAR]


def replicas_exchange(block, everyone, a, b):
    x = lax.axis_index("xx")
    copies = [
        send(block, everyone.at[x], (a, b), i, device)
        for i, (_, device) in enumerate(replicas_peers())
    ]
    return copies


def features_body(layer, vocab, block, err, *refs):
    sources, everyone, places, ordered = refs[:2], refs[2], refs[3:5], refs[5]
    mixed, own_sem, err_sem, sems = refs[6], refs[7], refs[8], refs[9:]
    load = pltpu.make_async_copy(err, mixed, err_sem)
    load.start()
    greet([device for _, device in replicas_peers()] + pair_peer() + column_peers())
    copies = replicas_exchange(block, everyone, *sems[:2])
    own = pltpu.make_async_copy(block, everyone.at[lax.axis_index("xx")], own_sem)
    own.start()
    take_start(layer, sources, places, sems[2:])
    load.wait()

    def put_rows(start, count):
        for b in range(2):
            for tile in range(TILES):
                far = pl.ds(start * (2 * TILES) + 2 * tile + b, count, stride=2 * TILES)
                ordered[b, pl.ds(start, count), pl.ds(tile * 128, 128)] = mixed[far, :]

    whole = vocab // CHUNK * CHUNK
    ordered[:, pl.ds(whole, ordered.shape[1] - whole), :] = jnp.zeros(
        (2, ordered.shape[1] - whole, D), F32
    )

    @pl.loop(0, vocab // CHUNK)
    def _(c):
        put_rows(pl.multiple_of(c * CHUNK, CHUNK), CHUNK)

    put_rows(whole, vocab - whole)
    own.wait()
    for copy in copies:
        copy.wait()
    take_finish(layer, sources, places, sems[2:])


def all_features(block, layer, sources, err, vocab, tall):
    some = pl.BlockSpec(memory_space=pl.ANY)
    return kernel_call(
        functools.partial(features_body, layer, vocab),
        [jax.ShapeDtypeStruct((4, *block.shape), block.dtype)]
        + [jax.ShapeDtypeStruct(a.shape, a.dtype) for a in sources]
        + [jax.ShapeDtypeStruct((2, tall, D), F32)],
        (block, err, *sources),
        [pltpu.VMEM(err.shape, F32), pltpu.SemaphoreType.DMA, pltpu.SemaphoreType.DMA]
        + sem_pairs(3)
        + take_scratch(2),
        31,
        in_specs=[some] * 4,
        out_specs=[some] * 3 + [VMEM_SPEC],
    )


def halves(values):
    high = values.astype(BF)
    return high, (values - high.astype(F32)).astype(BF)


def short_dot(short, tall, contract):
    high, low = halves(tall)
    both = jnp.concatenate(halves(short), 0)
    first = lax.dot_general(both, high, (contract, ((), ())), preferred_element_type=F32)
    second = lax.dot_general(both, low, (contract, ((), ())), preferred_element_type=F32)
    return first[:RANK] + first[RANK:] + second[:RANK]


def outer_dot(left, right):
    (a, b), (c, d) = halves(left), halves(right)
    return dot_rows(jnp.concatenate([a, b, a], 0), jnp.concatenate([c, c, d], 0))


def factor_places(cols, rows, vocab):
    def up(n):
        return -(-n // 128) * 128

    half = max(up(cols) + up(vocab), up(rows) + up(vocab))
    return half, ((0, 0, cols), (1, 0, rows), (0, up(cols), vocab), (1, up(rows), vocab))


def compress_body(
    vocab, g_embed, g_head, err, m_in, m_back, q_in, q_back, q_embed, q_head, bias, vectors,
    m_embed, m_head, basis, own, sums, bias_sum, vector_sum,
    left, left_came, bias_came, joint, joint_came, work, vec_came, vec_mine, vec_sums, vec_all,
    *sems,
):
    y, core, z = where_am_i()
    x = lax.axis_index("xx")
    me = y * 8 + core * 4 + z
    peers = []
    for k in range(1, 32):
        p = lax.rem(me + k, 32)
        peers.append((p, {**at_chip(p // 8, lax.rem(p, 4)), "co": lax.rem(p // 4, 2)}))
    greet([device for _, device in peers] + [device for _, device in replicas_peers()])
    pairs = [(sems[2 * n], sems[2 * n + 1]) for n in range(len(sems) // 2)]
    vec_first = [
        send(vectors.at[p], vec_came.at[me], pairs[0], k, device)
        for k, (p, device) in enumerate(peers)
    ]
    vec_came[me] = vectors[me]

    half, places = factor_places(m_in.shape[0], m_back.shape[0], vocab)
    m_embed[...] = g_embed[...] + err[0]
    m_head[...] = g_head[...] + err[1]
    blocks = (m_in, m_back, m_embed, m_head)
    for b, (factor, block) in enumerate(zip((q_in, q_back, q_embed, q_head), blocks)):
        left[b] = short_dot(factor[...], block[...], ((1,), (0,)))

    for copy in vec_first:
        copy.wait_recv()
    vec_mine[...] = jnp.sum(vec_came[...], 0)
    second = []
    for n, (src, dst) in enumerate(
        ((left, left_came), (bias, bias_came), (vec_mine, vec_sums))
    ):
        second += replicas_exchange(src, dst, *pairs[1 + n])
    left_came[x] = left[...]
    bias_came[x] = bias[...]
    vec_sums[x] = vec_mine[...]
    for copy in second:
        copy.wait()
    bias_sum[...] = jnp.sum(bias_came[...], 0)
    vec_all[me] = jnp.sum(vec_sums[...], 0)
    mine = vec_all.at[me]
    third = [send(mine, mine, pairs[4], k, device) for k, (_, device) in enumerate(peers)]
    work[...] = jnp.sum(left_came[...], 0)
    order = lax.broadcasted_iota(jnp.int32, (1, RANK, 1), 1)
    for index in range(RANK):
        columns = work[...]
        one = columns[:, index : index + 1, :]
        one = one * lax.rsqrt(jnp.sum(one * one, -1, keepdims=True) + 1e-30)
        shares = jnp.sum(columns * one, -1, keepdims=True)
        work[...] = jnp.where(order > index, columns - shares * one, columns)
        basis[:, index : index + 1, :] = one

    own[...] = jnp.zeros(own.shape, F32)
    for b, block in enumerate(blocks):
        at = pl.ds(places[b][1], block.shape[0])
        own[places[b][0], :, at] = short_dot(basis[b], block[...], ((1,), (1,)))

    joint[...] = own[...].reshape(joint.shape).astype(BF)
    fourth = replicas_exchange(joint, joint_came, *pairs[5])
    joint_came[x] = joint[...]
    for copy in fourth:
        copy.wait()
    total = jnp.sum(joint_came[...].astype(F32), 0)
    sums[...] = total.reshape(sums.shape)
    for copy in vec_first:
        copy.wait_send()
    for copy in third:
        copy.wait()
    vector_sum[...] = vec_all[...]


def compressed(vocab, g_embed, g_head, err, m_in, m_back, facs, bias, vectors):
    half, _ = factor_places(m_in.shape[0], m_back.shape[0], vocab)
    tall = g_embed.shape
    return kernel_call(
        functools.partial(compress_body, vocab),
        [
            jax.ShapeDtypeStruct(s, F32)
            for s in (tall, tall, (4, 8, D), (2, 8, half), (2, 8, half), bias.shape, vectors.shape)
        ],
        (g_embed, g_head, err, m_in, m_back, *facs, bias, vectors),
        [
            pltpu.VMEM((4, 8, D), F32),
            pltpu.VMEM((4, 4, 8, D), F32),
            pltpu.VMEM((4, *bias.shape), F32),
            pltpu.VMEM((16, half), BF),
            pltpu.VMEM((4, 16, half), BF),
            pltpu.VMEM((4, 8, D), F32),
            pltpu.VMEM(vectors.shape, F32),
            pltpu.VMEM(vectors.shape[1:], F32),
            pltpu.VMEM((4, *vectors.shape[1:]), F32),
            pltpu.VMEM(vectors.shape, F32),
        ]
        + sem_pairs(31, 3, 3, 3, 31, 3),
        30,
        56,
    )


def ema_decay():
    return min(0.999, (1.0 + STEP) / (10.0 + STEP))


def stepped(rate, weight, moment, average, grad):
    decay = ema_decay()
    new_moment = MOMENTUM * moment + (1.0 - MOMENTUM) * grad
    new_weight = weight - rate * new_moment
    return new_weight, new_moment, decay * average + (1.0 - decay) * new_weight


def update_body(
    vocab, rate_layer, rate_tables, m_embed, m_head, m_in, m_back, basis, own, sums,
    in_w, in_m, in_e, back_w, back_m, back_e, tab_w, tab_m, tab_e,
    err_tab, err_in, err_back, o_in_w, o_in_m, o_in_e, o_back_w, o_back_m, o_back_e,
    o_tab_w, o_tab_m, o_tab_e,
):
    x = lax.axis_index("xx")
    half, places = factor_places(m_in.shape[0], m_back.shape[0], vocab)
    whole = vocab // CHUNK
    own_cols = pl.ds(pl.multiple_of(x * 128, 128), 128)

    def part(ref, b, start, count):
        return ref[places[b][0], :, pl.ds(pl.multiple_of(places[b][1] + start, 128), count)]

    def table_rows(start, count):
        for b, matrix in ((2, m_embed), (3, m_head)):
            span = CHUNK
            product = outer_dot(part(own, b, start, span), basis[b])
            for tile in range(TILES):
                far = pl.ds(start * (2 * TILES) + 2 * tile + b - 2, count, stride=2 * TILES)
                err_tab[far, :] = (
                    matrix[pl.ds(start, count), pl.ds(tile * 128, 128)]
                    - product[:count, tile * 128 : (tile + 1) * 128]
                )
            reduced = outer_dot(part(sums, b, start, span), basis[b, :, own_cols])
            near = pl.ds(start * 2 + b - 2, count, stride=2)
            new = stepped(
                rate_tables[b - 2], tab_w[near, :], tab_m[near, :], tab_e[near, :], reduced[:count]
            )
            for out, value in zip((o_tab_w, o_tab_m, o_tab_e), new):
                out[near, :] = value

    @pl.loop(0, whole)
    def _(c):
        table_rows(pl.multiple_of(c * CHUNK, CHUNK), CHUNK)

    if vocab > whole * CHUNK:
        table_rows(whole * CHUNK, vocab - whole * CHUNK)

    layer_parts = (
        (m_in, err_in, (in_w, in_m, in_e), (o_in_w, o_in_m, o_in_e)),
        (m_back, err_back, (back_w, back_m, back_e), (o_back_w, o_back_m, o_back_e)),
    )
    for b, (matrix, err, olds, outs) in enumerate(layer_parts):
        for start in range(0, matrix.shape[0], CHUNK):
            count = min(CHUNK, matrix.shape[0] - start)
            at = pl.ds(start, count)
            lanes = pl.ds(places[b][1] + start, count)
            err[at, :] = matrix[at, :] - outer_dot(own[places[b][0], :, lanes], basis[b])
            reduced = outer_dot(sums[places[b][0], :, lanes], basis[b])
            new = stepped(rate_layer, *[old[at, :] for old in olds], reduced)
            for out, value in zip(outs, new):
                out[at, :] = value


def updated(vocab, rates, m_tables, m_in, m_back, basis, own, sums, params, err_shape):
    outs = [err_shape, m_in.shape, m_back.shape] + [a.shape for a in params]
    return kernel_call(
        functools.partial(update_body, vocab, rates[0], rates[1]),
        [jax.ShapeDtypeStruct(a, F32) for a in outs],
        (*m_tables, m_in, m_back, basis, own, sums, *params),
        [],
        None,
        56,
    )


def rotary_tables():
    half_rot = ROT // 2
    inverse = 10000.0 ** (-jnp.arange(half_rot, dtype=F32) * (2.0 / ROT))
    angles = jnp.arange(LENGTH, dtype=F32)[:, None] * inverse[None, :]
    return (jnp.cos(angles), jnp.sin(angles))


def rotate(heads, cosine, sine):
    half_rot = ROT // 2
    first = heads[..., :half_rot]
    second = heads[..., half_rot:ROT]
    return jnp.concatenate(
        [first * cosine - second * sine, second * cosine + first * sine, heads[..., ROT:]], -1
    )


ATT_BLOCK = 512


def causal(start, stop):
    rows = start + lax.broadcasted_iota(jnp.int32, (stop - start, stop), 0)
    return rows >= lax.broadcasted_iota(jnp.int32, (stop - start, stop), 1)


def attention_forward(q_rot, k_rot, v_val):
    outputs, all_lse = [], []
    for start in range(0, LENGTH, ATT_BLOCK):
        stop = start + ATT_BLOCK
        scores = dot_cols(q_rot[start:stop], k_rot[:stop]) * HEAD ** (-0.5)
        scores = jnp.where(causal(start, stop), scores, NEG_BIG)
        top = jnp.max(scores, -1, keepdims=True)
        expo = jnp.exp(scores - top)
        total = jnp.sum(expo, -1, keepdims=True)
        probs = (expo / total).astype(BF)
        outputs.append(dot_plain(probs, v_val[:stop]))
        all_lse.append(top + jnp.log(total))
    return (jnp.concatenate(outputs, 0), jnp.concatenate(all_lse, 0))


def attention_backward(q_rot, k_rot, v_val, lse, grad_out):
    scale = HEAD ** (-0.5)
    grad_query, grad_key, grad_value = [], 0.0, 0.0
    for start in range(0, LENGTH, ATT_BLOCK):
        stop = start + ATT_BLOCK
        spare = ((0, LENGTH - stop), (0, 0))
        scores = dot_cols(q_rot[start:stop], k_rot[:stop]) * scale
        probs = jnp.where(causal(start, stop), jnp.exp(scores - lse[start:stop]), 0.0)
        grad_probs = dot_cols(grad_out[start:stop], v_val[:stop])
        grad_scores = (
            probs * (grad_probs - jnp.sum(grad_probs * probs, -1, keepdims=True))
        ).astype(BF)
        grad_query.append(dot_plain(grad_scores, k_rot[:stop]) * scale)
        grad_key = grad_key + jnp.pad(dot_rows(grad_scores, q_rot[start:stop]), spare) * scale
        grad_value = grad_value + jnp.pad(
            dot_rows(probs.astype(BF), grad_out[start:stop]), spare
        )
    return (jnp.concatenate(grad_query, 0), grad_key, grad_value)


def block_forward(hat, weights, cosine, sine):
    w_all, bias, vector = weights
    w_cols, w_rows = w_all[: bias.shape[0]], w_all[bias.shape[0] :]
    wide = hat.astype(F32)
    first_in = (wide * vector[0] + vector[1]).astype(BF)
    second_in = (wide * vector[2] + vector[3]).astype(BF)
    qkv = dot_cols(first_in, w_cols[: 3 * HEAD]) + bias[: 3 * HEAD]
    up_val = dot_cols(second_in, w_cols[3 * HEAD :]) + bias[3 * HEAD :]
    q_rot = rotate(qkv[:, :HEAD], cosine, sine).astype(BF)
    k_rot = rotate(qkv[:, HEAD : 2 * HEAD], cosine, sine).astype(BF)
    v_val = qkv[:, 2 * HEAD :].astype(BF)
    attended, lse = attention_forward(q_rot, k_rot, v_val)
    attended = attended.astype(BF)
    hidden = jax.nn.gelu(up_val, approximate=False).astype(BF)
    branch = dot_plain(attended, w_rows[:HEAD]) + dot_plain(hidden, w_rows[HEAD:])
    return (
        branch.astype(BF),
        (hat, first_in, second_in, q_rot, k_rot, v_val, lse, attended, up_val, hidden),
    )


def gelu_exact(values):
    return jax.nn.gelu(values, approximate=False)


def block_backward(grad_low, kept, weights, cosine, sine):
    w_all, bias, vector = weights
    w_cols, w_rows = w_all[: bias.shape[0]], w_all[bias.shape[0] :]
    hat, first_in, second_in, q_rot, k_rot, v_val, lse, attended, up_val, hidden = kept
    grad_att = dot_cols(grad_low, w_rows[:HEAD]).astype(BF)
    grad_hidden = dot_cols(grad_low, w_rows[HEAD:])
    grad_up = jax.vjp(gelu_exact, up_val)[1](grad_hidden)[0].astype(BF)
    grad_query, grad_key, grad_value = attention_backward(q_rot, k_rot, v_val, lse, grad_att)
    grad_query = rotate(grad_query, cosine, -sine)
    grad_key = rotate(grad_key, cosine, -sine)
    grad_qkv = jnp.concatenate([grad_query, grad_key, grad_value], 1).astype(BF)
    grad_weights = jnp.concatenate(
        [
            dot_rows(grad_qkv, first_in).astype(BF),
            dot_rows(grad_up, second_in).astype(BF),
            dot_rows(attended, grad_low).astype(BF),
            dot_rows(hidden, grad_low).astype(BF),
        ]
    )
    grad_bias = jnp.concatenate(
        [jnp.sum(grad_qkv.astype(F32), 0), jnp.sum(grad_up.astype(F32), 0)]
    )
    grad_first = dot_plain(grad_qkv, w_cols[: 3 * HEAD])
    grad_second = dot_plain(grad_up, w_cols[3 * HEAD :])
    wide = hat.astype(F32)
    grad_norms = jnp.stack(
        [
            jnp.sum(grad_first * wide, 0),
            jnp.sum(grad_first, 0),
            jnp.sum(grad_second * wide, 0),
            jnp.sum(grad_second, 0),
        ]
    )
    grad_hat = grad_first * vector[0] + grad_second * vector[2]
    return (grad_hat.astype(BF), (grad_weights, grad_bias, grad_norms))


def on_device(
    tokens,
    groups,
    counts,
    domain,
    w_in,
    w_back,
    tables,
    b_in,
    vecs,
    final_norm,
    w_in_mom,
    w_back_mom,
    tables_mom,
    b_in_mom,
    vecs_mom,
    final_mom,
    w_in_ema,
    w_back_ema,
    tables_ema,
    b_in_ema,
    vecs_ema,
    final_ema,
    w_in_err,
    w_back_err,
    tables_err,
    w_in_fac,
    w_back_fac,
    tables_fac,
):
    y, core, z = where_am_i()
    replica = lax.axis_index("xx")
    section = lax.axis_index("yl") * 2 + core
    vocab_part = section * 8 + lax.axis_index("yh") * 4 + z
    shard = core * 4 + z
    seq_rep = tokens.shape[0]
    row_total = seq_rep * LENGTH
    vocab_shard = tables.shape[1]
    own_cols = tables.shape[2]
    cosine, sine = rotary_tables()

    seq_index = jnp.arange(groups.shape[0], dtype=jnp.int32)
    live = seq_index % seq_rep < counts[seq_index // seq_rep]
    domain_hit = groups[:, None] == jnp.arange(domain.shape[0], dtype=jnp.int32)[None, :]
    seq_weight = jnp.where(live, jnp.sum(jnp.where(domain_hit, domain[None, :], 0.0), 1), 0.0)
    weight_total = jnp.sum(seq_weight)
    own_weight = lax.dynamic_slice_in_dim(seq_weight, replica * seq_rep, seq_rep, 0)
    token_ids = tokens[:, :LENGTH].reshape(-1)
    target_ids = tokens[:, 1:].reshape(-1)

    pad_ids = -vocab_shard % 128
    tall = vocab_shard + pad_ids
    short = jnp.pad(
        jnp.transpose(tables.astype(BF), (0, 2, 1)), ((0, 0), (0, 0), (0, pad_ids))
    )
    small = jnp.concatenate(
        [
            jnp.pad(vecs[0], ((0, 2), (0, 0))),
            jnp.pad(b_in, ((0, 7), (0, D - b_in.shape[1]))),
        ]
    )
    sources = (jnp.concatenate([w_in[0].T.astype(BF), w_back[0].astype(BF)]), small)
    err = jnp.transpose(
        tables_err.reshape(2, vocab_shard, D // 128, 128), (1, 2, 0, 3)
    ).reshape(-1, 128)
    embed_t, *packs_0, err = all_features(short[0], 0, sources, err, vocab_shard, tall)
    packs = {0: packs_0}
    head_t = lax.all_gather(short[1], "xx", axis=0, tiled=True)

    def own_ids(ids):
        local = ids - vocab_part * vocab_shard
        inside = (local >= 0) & (local < vocab_shard)
        return jnp.where(inside, local, -1).reshape(16, 1, 2 * BLOCK)

    own_tokens, own_targets = own_ids(token_ids), own_ids(target_ids)
    x, hat = embedded(embed_t.reshape(D, tall), own_tokens)
    head = jnp.transpose(head_t)

    gains = jnp.pad(final_norm, ((0, 6), (0, 0)))
    weights, kept, before = [], [], []
    for index in range(LAYERS):
        w_all, rest = packs[index]
        weights.append((w_all, rest[8, : b_in.shape[1]], rest))
        shift = jnp.broadcast_to((rest[4] + rest[5])[None], (8, D))
        before.append(x)
        branch, keep = block_forward(hat.reshape(LENGTH, D), weights[index], cosine, sine)
        kept.append(keep)
        branch = branch.reshape(8, BLOCK, D)
        if index + 1 < LAYERS:
            hat, x, *packs[index + 1] = next_hat(branch, x, shift, index + 1, sources)

    x, normed, probs, stats, joined = last_and_lse(
        vocab_shard, branch, x, shift, gains, head, own_targets
    )
    losses = joined[:, :, 1, :].reshape(seq_rep, LENGTH)
    loss_part = jnp.sum(own_weight * jnp.mean(losses, 1))
    coefs = jnp.broadcast_to(
        jnp.repeat(own_weight / (weight_total * LENGTH), 4)[:, None, None], (16, 1, 2 * BLOCK)
    )
    steep, grad_all, grad, grad_gains = loss_back(
        probs, stats, joined, own_targets, coefs, head_t, x, gains
    )
    grad_gains = grad_gains[:2]
    vector_rows = [None] * LAYERS
    grad_table = None
    returned = [None] * LAYERS
    for index in reversed(range(LAYERS)):
        outbias = jnp.sum(grad, 0)[None]
        grad_hat, (w_grad, bias_row, norm_rows) = block_backward(
            grad_all.reshape(LENGTH, D), kept[index], weights[index], cosine, sine
        )
        vector_rows[index] = jnp.concatenate([norm_rows, outbias, outbias], 0)
        given = (w_grad, jnp.pad(bias_row[None], ((0, 7), (0, D - bias_row.shape[0]))))
        grad_hat = grad_hat.reshape(8, BLOCK, D)
        if index >= LAYERS - 2:
            parts = (0, 1) if index == LAYERS - 1 else (2, 3)
            grad_all, grad, *returned[index], grad_table = next_grad(
                index, grad_hat, before[index], grad, given, parts, steep, normed, grad_table
            )
        elif index:
            grad_all, grad, *returned[index] = next_grad(
                index, grad_hat, before[index], grad, given
            )
        else:
            grad_embed, *returned[index] = lowest_grad(
                index, grad_hat, before[index], grad, own_tokens, given, tall
            )

    def of_own_layer(n):
        picked = returned[LAYERS - 1][n]
        for index in range(LAYERS - 1):
            picked = jnp.where(section == index, returned[index][n], picked)
        return picked

    loss_row = jnp.zeros((1, D), F32).at[0, 0].set(jnp.where(shard + y * 8 == 0, loss_part, 0.0))
    vectors = jnp.concatenate(vector_rows + [grad_gains, loss_row], 0)
    vectors = jnp.pad(vectors, ((0, 32 - vectors.shape[0]), (0, 0))).reshape(32, D // 128, 128)
    vectors = jnp.pad(vectors, ((0, 0), (0, 8 - D // 128), (0, 0)))
    full = of_own_layer(0)
    n_in = b_in.shape[1]
    full_in = full[:n_in] + w_in_err[0, 0].T
    full_back = full[n_in:] + w_back_err[0, 0]
    facs = (
        w_in_fac[0].T,
        w_back_fac[0].T,
        jnp.pad(tables_fac[0].T, ((0, 0), (0, pad_ids))),
        jnp.pad(tables_fac[1].T, ((0, 0), (0, pad_ids))),
    )
    m_embed, m_head, basis, own, sums, bias_sum, vector_sums = compressed(
        vocab_shard, grad_embed, grad_table, err, full_in, full_back, facs, of_own_layer(1), vectors
    )
    bias_sum = bias_sum[:1, : b_in.shape[1]]
    vector_sums = vector_sums[:, : D // 128, :].reshape(32, D)
    vec_sum = lax.dynamic_slice_in_dim(vector_sums, section * 6, 6, 0)
    final_sum = vector_sums[6 * LAYERS : 6 * LAYERS + 2]
    loss_sum = vector_sums[6 * LAYERS + 2, 0]

    def of_tables(arrays):
        return [jnp.transpose(a, (1, 0, 2)).reshape(-1, 128) for a in arrays]

    token_count = lax.axis_size("xx") * seq_rep * LENGTH
    rate_layer = 2.0 * math.sqrt(token_count)
    rate_vector = 6.0 * math.sqrt(token_count)
    rate_tables = [rate * math.sqrt(token_count * VOCAB) for rate in (50.0, 0.5)]
    params = (
        [w_in[0].T, w_in_mom[0].T, w_in_ema[0].T, w_back[0], w_back_mom[0], w_back_ema[0]]
        + of_tables((tables, tables_mom, tables_ema))
    )
    err_tab, err_in, err_back, *new = updated(
        vocab_shard, (rate_layer, rate_tables), (m_embed, m_head), full_in, full_back,
        basis, own, sums, params, (vocab_shard * 8, 128),
    )
    err_tab = jnp.transpose(
        err_tab.reshape(vocab_shard, D // 128, 2, 128), (2, 0, 1, 3)
    ).reshape(tables_err.shape)
    in_w, in_m, in_e = [a.T[None] for a in new[:3]]
    back_w, back_m, back_e = [a[None] for a in new[3:6]]
    tab_w, tab_m, tab_e = [
        jnp.transpose(a.reshape(vocab_shard, 2, own_cols), (1, 0, 2)) for a in new[6:]
    ]
    _, places = factor_places(full_in.shape[0], full_back.shape[0], vocab_shard)
    fac_in, fac_back, fac_embed, fac_head = [
        sums[half, :, at : at + width].T for half, at, width in places
    ]
    bias_w, bias_m, bias_e = stepped(rate_layer, b_in, b_in_mom, b_in_ema, bias_sum)
    vec_w, vec_m, vec_e = stepped(rate_vector, vecs, vecs_mom, vecs_ema, vec_sum[None])
    fin_w, fin_m, fin_e = stepped(rate_layer, final_norm, final_mom, final_ema, final_sum)
    return (
        loss_sum,
        weight_total,
        in_w,
        back_w,
        tab_w,
        bias_w,
        vec_w,
        fin_w,
        in_m,
        back_m,
        tab_m,
        bias_m,
        vec_m,
        fin_m,
        in_e,
        back_e,
        tab_e,
        bias_e,
        vec_e,
        fin_e,
        err_in.T[None, None],
        err_back[None, None],
        err_tab,
        fac_in[None],
        fac_back[None],
        fac_embed,
        fac_head,
    )


def solution(mesh):
    fine = Mesh(
        np.asarray(mesh.devices).reshape(2, 2, 2, 4, 4), ("yl", "co", "yh", "zz", "xx")
    )
    names = {"section": ("yl", "co"), "tensor": ("yh", "zz"), "dp": ("xx",)}

    def spec(*axes):
        return P(*[None if a is None else sum((names[n] for n in a.split()), ()) for a in axes])

    layer_in, layer_back = spec("section", None, "tensor"), spec("section", "tensor", None)
    table, bias = spec(None, "section tensor", "dp"), spec("section", "tensor")
    vector = spec("section", None, None)
    params = (layer_in, layer_back, table, bias, vector, P())
    errors = (
        spec("dp", "section", None, "tensor"),
        spec("dp", "section", "tensor", None),
        spec("dp", None, "section tensor", None),
    )
    in_specs = (
        (spec("dp", None), P(), P(), P())
        + params * 3
        + errors
        + (layer_back, layer_back, spec(None, "section tensor", None))
    )
    out_specs = (
        (P(), P())
        + params * 3
        + errors
        + (layer_back, layer_back, spec("section tensor", None), spec("section tensor", None))
    )
    return jax.shard_map(
        on_device, mesh=fine, in_specs=in_specs, out_specs=out_specs, check_vma=False
    )
```

```python
import functools
import math

import jax
import jax.numpy as jnp
import numpy as np
from jax import lax
from jax.experimental import pallas as pl
from jax.experimental.pallas import tpu as pltpu
from jax.sharding import Mesh
from jax.sharding import PartitionSpec as P

D = 512
HEAD = 64
ROT = 16
VOCAB = 50304
LAYERS = 4
LENGTH = 1024
RANK = 8
STEP = 5
BLOCK = 128
CHUNK = 128
ROWS = 256
TILES = D // 128

EPS_NORM = 1e-05
MOMENTUM = 0.9
NEG_BIG = -1e30
HIGH = lax.Precision.HIGHEST
BF = jnp.bfloat16
F32 = jnp.float32
MESH_ID = pl.DeviceIdType.MESH
FAR = (2, 1, 3)


def where_am_i():
    core, z = lax.axis_index("co"), lax.axis_index("zz")
    y = lax.axis_index("yh") * 2 + lax.axis_index("yl")
    return y, core, z


def at_chip(y, z):
    return {"yh": y // 2, "yl": lax.rem(y, 2), "zz": z}


def send(src, dst, sems, at, device):
    copy = pltpu.make_async_remote_copy(
        src_ref=src,
        dst_ref=dst,
        send_sem=sems[0].at[at],
        recv_sem=sems[1].at[at],
        device_id=device,
        device_id_type=MESH_ID,
    )
    copy.start()
    return copy


def greet(devices):
    barrier = pltpu.get_barrier_semaphore()
    for device in devices:
        pl.semaphore_signal(barrier, inc=1, device_id=device, device_id_type=MESH_ID)
    pl.semaphore_wait(barrier, len(devices))


def sem_pairs(*counts):
    return [pltpu.SemaphoreType.DMA((n,)) for n in counts for _ in range(2)]


VMEM_SPEC = pl.BlockSpec(memory_space=pltpu.VMEM)


def kernel_call(
    body, out_shape, args, scratch, cid=None, limit=48, in_specs=None, out_specs=None
):
    many = isinstance(out_shape, (list, tuple))
    return pl.pallas_call(
        body,
        out_shape=out_shape,
        in_specs=in_specs or [VMEM_SPEC] * len(args),
        out_specs=out_specs or ([VMEM_SPEC] * len(out_shape) if many else VMEM_SPEC),
        scratch_shapes=scratch,
        compiler_params=pltpu.CompilerParams(
            collective_id=cid, has_side_effects=cid is not None, vmem_limit_bytes=limit * 2**20
        ),
    )(*args)


def dot_rows(left, right):
    return lax.dot_general(
        left, right, (((0,), (0,)), ((), ())), preferred_element_type=F32
    )


def dot_cols(left, right):
    return lax.dot_general(
        left, right, (((1,), (1,)), ((), ())), preferred_element_type=F32
    )


def dot_plain(left, right):
    return jnp.dot(left, right, preferred_element_type=F32)


def normed_rows(values):
    center = values - jnp.mean(values, -1, keepdims=True)
    spread = jnp.mean(center * center, -1, keepdims=True)
    scale = lax.rsqrt(spread + EPS_NORM)
    return center * scale, scale


def norm_back(values, grad):
    hat, scale = normed_rows(values)
    return scale * (
        grad
        - jnp.mean(grad, -1, keepdims=True)
        - hat * jnp.mean(grad * hat, -1, keepdims=True)
    )


def row_sum(part, r1, s, r2, sems1, sems2):
    y, core, z = where_am_i()
    first = []
    for i, k in enumerate(FAR + (0,)):
        zz = lax.rem(z + k, 4)
        first.append(send(part.at[zz * 2 + 1 - core], r1.at[i], sems1, i, {"co": 1 - core}))
    second = []
    for i, k in enumerate(FAR):
        zz = lax.rem(z + k, 4)
        first[i].wait_recv()
        s[i] = (part[zz * 2 + core].astype(F32) + r1[i].astype(F32)).astype(BF)
        second.append(send(s.at[i], r2.at[i], sems2, i, {"zz": zz}))
    first[3].wait_recv()
    total = part[z * 2 + core].astype(F32) + r1[3].astype(F32)
    for i in range(3):
        second[i].wait_recv()
        total = total + r2[i].astype(F32)
    for copy in first + second:
        copy.wait_send()
    return total


def row_gather(everyone, sems3, sems4):
    y, core, z = where_am_i()
    own = everyone.at[z * 2 + core]
    third = [
        send(own, own, sems3, i, {"zz": lax.rem(z + k, 4)}) for i, k in enumerate(FAR)
    ]
    fourth = [send(own, own, sems4, 3, {"co": 1 - core})]
    for i, k in enumerate(FAR):
        third[i].wait_recv()
        came = everyone.at[lax.rem(z + 4 - k, 4) * 2 + core]
        fourth.append(send(came, came, sems4, i, {"co": 1 - core}))
    for copy in third:
        copy.wait_send()
    for copy in fourth:
        copy.wait()


HALVES = [pl.ds(0, BLOCK // 2), pl.ds(BLOCK // 2, BLOCK // 2)]


def row_exchange(part, everyone, middle, r1, s, r2, sems, hooks):
    y, core, z = where_am_i()
    own = z * 2 + core
    first, second, third, fourth = [], [], [], []
    for h, rows in enumerate(HALVES):
        for i, k in enumerate(FAR + (0,)):
            block = part.at[lax.rem(z + k, 4) * 2 + 1 - core, rows]
            first.append(send(block, r1.at[i, rows], sems[0:2], 4 * h + i, {"co": 1 - core}))
    for h, rows in enumerate(HALVES):
        for i, k in enumerate(FAR):
            zz = lax.rem(z + k, 4)
            first[4 * h + i].wait_recv()
            s[i, rows] = (part[zz * 2 + core, rows].astype(F32) + r1[i, rows].astype(F32)).astype(BF)
            second.append(send(s.at[i, rows], r2.at[i, rows], sems[2:4], 3 * h + i, {"zz": zz}))
    hooks[0]()
    for h, rows in enumerate(HALVES):
        first[4 * h + 3].wait_recv()
        total = part[own, rows].astype(F32) + r1[3, rows].astype(F32)
        for i in range(3):
            second[3 * h + i].wait_recv()
            total = total + r2[i, rows].astype(F32)
        everyone[own, rows] = middle(rows, total).astype(BF)
        mine = everyone.at[own, rows]
        for i, k in enumerate(FAR):
            third.append(send(mine, mine, sems[4:6], 3 * h + i, {"zz": lax.rem(z + k, 4)}))
        fourth.append(send(mine, mine, sems[6:8], 6 + h, {"co": 1 - core}))
    hooks[1]()
    for h, rows in enumerate(HALVES):
        for i, k in enumerate(FAR):
            third[3 * h + i].wait_recv()
            came = everyone.at[lax.rem(z + 4 - k, 4) * 2 + core, rows]
            fourth.append(send(came, came, sems[6:8], 3 * h + i, {"co": 1 - core}))
    for copy in first + second + third:
        copy.wait_send()
    for copy in fourth:
        copy.wait()


def nothing():
    pass


def row_peers():
    y, core, z = where_am_i()
    return [{"co": 1 - core}] + [{"zz": lax.rem(z + k, 4)} for k in FAR]


SUM_SCRATCH = [
    pltpu.VMEM((4, BLOCK, D), BF),
    pltpu.VMEM((3, BLOCK, D), BF),
    pltpu.VMEM((3, BLOCK, D), BF),
] + sem_pairs(4, 3)
GATHER_SCRATCH = sem_pairs(3, 4)
EXCHANGE_SCRATCH = SUM_SCRATCH[:3] + sem_pairs(8, 6, 6, 8)


def pair_peer():
    return [{"co": 1 - lax.axis_index("co")}]


def column_peers():
    y, core, z = where_am_i()
    return [{**at_chip(lax.rem(y + dy, 4), z), "co": c} for dy in FAR for c in (0, 1)]


def column_others():
    y, core, z = where_am_i()
    return [{**at_chip(lax.rem(y + dy, 4), z), "co": 1 - core} for dy in FAR]


def home_and_layer():
    y, core, z = where_am_i()
    return y // 2 == core, lax.rem(y, 2) * 2 + core


def take_copies(sources, places, sems, dy):
    y, core, z = where_am_i()
    return [
        pltpu.make_async_remote_copy(
            src_ref=src,
            dst_ref=dst,
            send_sem=sems[2 * n].at[dy],
            recv_sem=sems[2 * n + 1].at[0],
            device_id={**at_chip(lax.rem(y + dy, 4), z), "co": y // 2},
            device_id_type=MESH_ID,
        )
        for n, (src, dst) in enumerate(zip(sources, places))
    ]


def take_local(sources, places, sems):
    return [
        pltpu.make_async_copy(src, dst, sems[2 * n + 1].at[0])
        for n, (src, dst) in enumerate(zip(sources, places))
    ]


def take_start(layer, sources, places, sems):
    home, own = home_and_layer()

    @pl.when(own == layer)
    def _():
        for dy in FAR:
            for copy in take_copies(sources, places, sems, dy):
                copy.start()

    @pl.when(jnp.logical_and(own == layer, home))
    def _():
        for copy in take_local(sources, places, sems):
            copy.start()

    @pl.when(jnp.logical_and(own == layer, jnp.logical_not(home)))
    def _():
        for copy in take_copies(sources, places, sems, 0):
            copy.start()


def take_finish(layer, sources, places, sems):
    home, own = home_and_layer()

    @pl.when(own == layer)
    def _():
        for dy in FAR:
            for copy in take_copies(sources, places, sems, dy):
                copy.wait_send()

    @pl.when(jnp.logical_and(own == layer, jnp.logical_not(home)))
    def _():
        for copy in take_copies(sources, places, sems, 0):
            copy.wait_send()

    for copy in take_local(sources, places, sems):
        copy.wait()


def take_scratch(count):
    return [pltpu.SemaphoreType.DMA((n,)) for _ in range(count) for n in (4, 1)]


def give_copies(layer, sources, landed, sems):
    y, core, z = where_am_i()
    return [
        pltpu.make_async_remote_copy(
            src_ref=src,
            dst_ref=dst.at[y],
            send_sem=sems[2 * n].at[0],
            recv_sem=sems[2 * n + 1].at[y],
            device_id={**at_chip(core * 2 + layer // 2, z), "co": layer % 2},
            device_id_type=MESH_ID,
        )
        for n, (src, dst) in enumerate(zip(sources, landed))
    ]


def give_start(layer, sources, landed, sems):
    y, core, z = where_am_i()
    home, own = home_and_layer()
    local = jnp.logical_and(home, own == layer)

    @pl.when(jnp.logical_not(local))
    def _():
        for copy in give_copies(layer, sources, landed, sems):
            copy.start()

    @pl.when(local)
    def _():
        for n, (src, dst) in enumerate(zip(sources, landed)):
            pltpu.make_async_copy(src, dst.at[y], sems[2 * n + 1].at[y]).start()


def give_finish(layer, sources, landed, sums, sems):
    home, own = home_and_layer()

    @pl.when(own == layer)
    def _():
        for n, (src, dst) in enumerate(zip(sources, landed)):
            for index in range(4):
                pltpu.make_async_copy(src, dst.at[index], sems[2 * n + 1].at[index]).wait()
            total = dst[0].astype(F32)
            for index in range(1, 4):
                total = total + dst[index].astype(F32)
            sums[n][...] = total

    @pl.when(jnp.logical_not(jnp.logical_and(home, own == layer)))
    def _():
        for copy in give_copies(layer, sources, landed, sems):
            copy.wait_send()


def give_scratch(grads):
    return [pltpu.VMEM((4, *g.shape), g.dtype) for g in grads] + [
        pltpu.SemaphoreType.DMA((n,)) for _ in grads for n in (1, 4)
    ]


def forward_body(layer, part, x, rest, *refs):
    sources, everyone, x_new, places, refs = refs[:2], refs[2], refs[3], refs[4:6], refs[6:]
    r1, s, r2, sems, side = refs[0], refs[1], refs[2], refs[3:11], refs[11:]
    greet(row_peers() + column_peers())
    take_start(layer, sources, places, side)

    def middle(rows, total):
        after = x[rows] + total + (rest[4:5] + rest[5:6])
        x_new[rows] = after
        return normed_rows(after)[0]

    row_exchange(part, everyone, middle, r1, s, r2, sems, (nothing, nothing))
    take_finish(layer, sources, places, side)


def next_hat(part, x, rest, layer, sources):
    return kernel_call(
        functools.partial(forward_body, layer),
        [jax.ShapeDtypeStruct((8, BLOCK, D), BF), jax.ShapeDtypeStruct((BLOCK, D), F32)]
        + [jax.ShapeDtypeStruct(a.shape, a.dtype) for a in sources],
        (part, x, rest, *sources),
        EXCHANGE_SCRATCH + take_scratch(len(sources)),
        10 + layer,
    )


def backward_body(layer, table_parts, finish, part, x, grad, *refs):
    sources, refs = refs[:2], refs[2:]
    begun, steep, tokens = (), None, None
    if table_parts:
        steep, tokens, refs = refs[0], refs[1], refs[2:]
        if table_parts[0]:
            begun, refs = refs[:1], refs[1:]
    if finish:
        begun, err, factor, refs = refs[0], refs[1], refs[2], refs[3:]
    everyone, g_new, sums, refs = refs[0], refs[1], refs[2:4], refs[4:]
    if table_parts:
        table_grad, refs = refs[0], refs[1:]
    if finish:
        matrix, left, refs = refs[0], refs[1], refs[2:]
    landed, give_sems, refs = refs[:2], refs[2:6], refs[6:]
    r1, s, r2, sems, refs = refs[0], refs[1], refs[2], refs[3:11], refs[11:]
    greet(row_peers() + column_peers())
    hooks = [nothing, nothing]
    if finish:
        errors, err_sem = refs
        load = pltpu.make_async_copy(err.at[1], errors, err_sem)
        load.start()

        def whole_matrix():
            load.wait()
            matrix[...] = begun[...] + errors[...]

        def left_factor():
            left[...] = short_dot(factor[...], matrix[...], ((1,), (0,)))

        hooks = [whole_matrix, left_factor]
    if table_parts:
        slopes, rows, sem_slopes, sem_rows = refs
        loads = []
        for n, q in enumerate(table_parts):
            loads.append(
                (
                    pltpu.make_async_copy(steep.at[q], slopes.at[n], sem_slopes.at[n]),
                    pltpu.make_async_copy(
                        tokens.at[pl.ds(q * 4, 4)], rows.at[pl.ds(n * 4, 4)], sem_rows.at[n]
                    ),
                )
            )
            for load in loads[n]:
                load.start()

        def table_step(n):
            for load in loads[n]:
                load.wait()
            product = dot_plain(slopes[n], rows[pl.ds(n * 4, 4)].reshape(8 * BLOCK, D))
            if n:
                table_grad[...] += product
            else:
                table_grad[...] = begun[0][...] + product if begun else product

        hooks = [lambda: table_step(0), lambda: table_step(1)]
    give_start(layer, sources, landed, give_sems)

    def middle(rows, total):
        after = grad[rows] + norm_back(x[rows], total)
        g_new[rows] = after
        return after

    row_exchange(part, everyone, middle, r1, s, r2, sems, hooks)
    give_finish(layer, sources, landed, sums, give_sems)


def next_grad(layer, part, x, grad, sources, table_parts=(), steep=None, tokens=None, begun=None,
              finish=None):
    some = pl.BlockSpec(memory_space=pl.ANY)
    args, specs, outs, scratch = [], [], [], []
    if table_parts:
        args = [steep, tokens] + ([] if begun is None else [begun])
        specs = [some, some] + ([] if begun is None else [VMEM_SPEC])
        outs = [jax.ShapeDtypeStruct((steep.shape[1], D), F32)]
        scratch = [
            pltpu.VMEM((2, *steep.shape[1:]), BF),
            pltpu.VMEM((8, *tokens.shape[1:]), BF),
            pltpu.SemaphoreType.DMA((2,)),
            pltpu.SemaphoreType.DMA((2,)),
        ]
    if finish:
        args, specs = [begun, *finish], [VMEM_SPEC, some, VMEM_SPEC]
        outs = [jax.ShapeDtypeStruct(begun.shape, F32), jax.ShapeDtypeStruct((RANK, D), F32)]
        scratch = [pltpu.VMEM(begun.shape, F32), pltpu.SemaphoreType.DMA]
    return kernel_call(
        functools.partial(backward_body, layer, table_parts, finish is not None),
        [jax.ShapeDtypeStruct((8, BLOCK, D), BF), jax.ShapeDtypeStruct((BLOCK, D), F32)]
        + [jax.ShapeDtypeStruct(a.shape, F32) for a in sources]
        + outs,
        (part, x, grad, *sources, *args),
        give_scratch(sources) + EXCHANGE_SCRATCH + scratch,
        20 + layer,
        in_specs=[VMEM_SPEC] * (3 + len(sources)) + specs,
    )


def offset(i):
    at = lax.rem(jnp.int32(i) * 5, 16)
    return lax.div(at, 4), lax.rem(at, 4)


def chip(i, sign):
    y, _, z = where_am_i()
    dy, dz = offset(i)
    return lax.rem(y + sign * dy + 4, 4), lax.rem(z + sign * dz + 4, 4)


def plane_peers(both_cores):
    y, core, z = where_am_i()
    found = [{"co": 1 - core}]
    for i in range(1, 16):
        for c in (core, 1 - core) if both_cores else (core,):
            found.append({**at_chip(*chip(i, 1)), "co": c})
    return found


def remote(src, dst, send_sem, recv_sem, device):
    return pltpu.make_async_remote_copy(
        src_ref=src,
        dst_ref=dst,
        send_sem=send_sem,
        recv_sem=recv_sem,
        device_id=device,
        device_id_type=MESH_ID,
    )


def core_rows(core):
    return pl.ds(pl.multiple_of(core * BLOCK, BLOCK), BLOCK)


AHEAD = 10


def plane_collect(everyone, sems, on_chip):
    y, core, z = where_am_i()
    a, b, c, d = sems
    own = everyone.at[y * 4 + z, core_rows(core)]

    def direct(i):
        return remote(own, own, a.at[i], b.at[i], at_chip(*chip(i, 1)))

    def across(i):
        yy, zz = chip(i, -1)
        came = everyone.at[yy * 4 + zz, core_rows(core)]
        return remote(came, came, c.at[i], d.at[i], {"co": 1 - core})

    def use(i):
        across(i).wait_recv()
        yy, zz = chip(i, -1)
        on_chip(i, yy * 4 + zz)

    across(0).start()
    for i in range(1, 1 + AHEAD):
        direct(i).start()
    use(0)
    direct(1 + AHEAD).start()
    direct(1).wait_recv()
    across(1).start()

    def step(i, more):
        if more:
            direct(i + AHEAD).start()
        direct(i).wait_recv()
        across(i).start()
        use(i - 1)

    @pl.loop(2, 16 - AHEAD)
    def _(i):
        step(i, True)

    @pl.loop(16 - AHEAD, 16)
    def _(i):
        step(i, False)

    use(15)

    @pl.loop(1, 16)
    def _(i):
        direct(i).wait_send()
        across(i).wait_send()

    across(0).wait_send()


COLLECT_SEMS = sem_pairs(16, 16)


def plane_total(group, between, keep, other, r1, s, r2, sems):
    y, core, z = where_am_i()
    a, b, c, d = sems

    def pair(i):
        return remote(other.at[i], r1.at[i], a.at[i], b.at[i], {"co": 1 - core})

    def away(i):
        return remote(s.at[i], r2.at[i], c.at[i], d.at[i], at_chip(*chip(i, 1)))

    def make(i):
        yy, zz = chip(i, 1)
        part = group(i, yy * 4 + zz)
        low, high = part[:, :BLOCK], part[:, BLOCK:]
        keep[i] = jnp.where(core == 0, low, high).astype(BF)
        other[i] = jnp.where(core == 0, high, low).astype(BF)
        pair(i).start()

    def forward(i):
        pair(i).wait_recv()
        s[i] = (keep[i].astype(F32) + r1[i].astype(F32)).astype(BF)
        away(i).start()

    make(1)

    @pl.loop(2, 16)
    def _(i):
        make(i)
        forward(i - 1)

    forward(15)
    make(0)
    between()
    pair(0).wait_recv()
    total = keep[0].astype(F32) + r1[0].astype(F32)

    def add(i, total):
        away(i).wait_recv()
        return total + r2[i].astype(F32)

    total = lax.fori_loop(1, 16, add, total)

    @pl.loop(1, 16)
    def _(i):
        pair(i).wait_send()
        away(i).wait_send()

    pair(0).wait_send()
    return total


TOTAL_SCRATCH = [pltpu.VMEM((16, D, BLOCK), BF) for _ in range(5)] + sem_pairs(16, 16)


def vocab_rows(v, rows):
    return v * rows + lax.broadcasted_iota(jnp.int32, (rows, 1), 0)


def onehot_into(place, ids):
    rows = place.shape[0]

    @pl.loop(0, rows // 128)
    def _(v):
        hit = vocab_rows(v, 128) == ids
        place[pl.ds(pl.multiple_of(v * 128, 128), 128), :] = jnp.where(hit, 1.0, 0.0).astype(BF)


def embed_body(table, ids, x, everyone, hot, keep, other, r1, s, r2, e, f, g, h, a, b, c, d):
    y, core, z = where_am_i()
    greet(plane_peers(False))

    def group(i, c):
        onehot_into(hot, ids[c])
        return jnp.dot(table[...], hot[...], preferred_element_type=F32)

    total = plane_total(group, lambda: None, keep, other, r1, s, r2, (e, f, g, h))
    rows = jnp.transpose(total)
    x[...] = rows
    everyone[z * 2 + core] = normed_rows(rows)[0].astype(BF)
    row_gather(everyone, (a, b), (c, d))


def embedded(table, ids):
    return kernel_call(
        embed_body,
        [jax.ShapeDtypeStruct((BLOCK, D), F32), jax.ShapeDtypeStruct((8, BLOCK, D), BF)],
        (table, ids),
        [pltpu.VMEM((table.shape[1], 2 * BLOCK), BF)] + TOTAL_SCRATCH + GATHER_SCRATCH,
        7,
    )


def lse_body(
    vocab, part, x, rest, gains, head, targets,
    x_new, tokens_out, probs_out, stats, joined,
    everyone, probs, out_sems, logits, came, r1, s, r2, *sems,
):
    y, core, z = where_am_i()
    greet(plane_peers(True))
    here = y * 4 + z
    a, b, c, d = sems[8:]
    shift = rest[4:5] + rest[5:6]
    after = x[...] + row_sum(part, r1, s, r2, sems[0:2], sems[2:4]) + shift
    x_new[...] = after
    everyone[here, core_rows(core)] = (
        normed_rows(after)[0] * gains[0:1] + gains[1:2]
    ).astype(BF)
    tall = head.shape[0]

    def stat_copy(i, flip, where):
        device = {**at_chip(*chip(i, -1)), "co": core if flip == 0 else 1 - core}
        to = core if flip == 0 else 1 - core
        return remote(
            stats.at[where, to], came.at[2 * i + flip], a.at[2 * i + flip], b.at[2 * i + flip], device
        )

    tokens_write = pltpu.make_async_copy(everyone, tokens_out, out_sems.at[16])

    def probs_write(i):
        yy, zz = chip(i, -1)
        return pltpu.make_async_copy(
            probs.at[yy * 4 + zz], probs_out.at[yy * 4 + zz], out_sems.at[i]
        )

    def on_chip(i, where):
        logits[...] = dot_cols(head[...], everyone[where])
        wanted = targets[where]

        whole = vocab // 128
        edge = pl.ds(whole * 128, tall - whole * 128)
        logits[edge, :] = jnp.where(
            vocab_rows(whole, tall - whole * 128) < vocab, logits[edge, :], NEG_BIG
        )

        def highest(v, top):
            value = logits[pl.ds(pl.multiple_of(v * 128, 128), 128), :]
            return jnp.maximum(top, jnp.max(value.reshape(16, 8, 2 * BLOCK), 0))

        top = lax.fori_loop(0, tall // 128, highest, jnp.full((8, 2 * BLOCK), NEG_BIG, F32))
        top = jnp.max(top, 0, keepdims=True)

        def summed(v, carry):
            rows = pl.ds(pl.multiple_of(v * 128, 128), 128)
            value = logits[rows, :]
            expo = jnp.exp(value - top)
            probs[where, rows, :] = expo.astype(BF)
            hit = jnp.where(vocab_rows(v, 128) == wanted, value, 0.0)
            return (
                carry[0] + jnp.sum(expo.reshape(16, 8, 2 * BLOCK), 0),
                carry[1] + jnp.sum(hit.reshape(16, 8, 2 * BLOCK), 0),
            )

        zero = jnp.zeros((8, 2 * BLOCK), F32)
        total, target = lax.fori_loop(0, tall // 128, summed, (zero, zero))
        found = jnp.concatenate(
            [
                top,
                jnp.sum(total, 0, keepdims=True),
                jnp.sum(target, 0, keepdims=True),
                jnp.zeros((5, 2 * BLOCK), F32),
            ],
            0,
        )
        stats[where, 0] = found[:, :BLOCK]
        stats[where, 1] = found[:, BLOCK:]
        probs_write(i).start()
        if isinstance(i, int) and i == 0:
            came[0] = stats[where, core]
        else:
            stat_copy(i, 0, where).start()
        stat_copy(i, 1, where).start()

    plane_collect(everyone, sems[4:8], on_chip)
    tokens_write.start()

    @pl.loop(1, 16)
    def _(i):
        stat_copy(i, 0, here).wait()
        stat_copy(i, 1, here).wait()

    stat_copy(0, 1, here).wait()
    top = jnp.max(came[:, 0, :], 0, keepdims=True)
    total = jnp.sum(came[:, 1, :] * jnp.exp(came[:, 0, :] - top), 0, keepdims=True)
    target = jnp.sum(came[:, 2, :], 0, keepdims=True)
    lse = top + jnp.log(total)
    joined[here, core] = jnp.concatenate([lse, lse - target, jnp.zeros((6, BLOCK), F32)], 0)
    mine = joined.at[here, core]

    def lse_copy(i, flip):
        device = {**at_chip(*chip(i, 1)), "co": core if flip == 0 else 1 - core}
        return remote(mine, mine, c.at[2 * i + flip], d.at[2 * i + flip], device)

    lse_copy(0, 1).start()

    @pl.loop(1, 16)
    def _(i):
        lse_copy(i, 0).start()
        lse_copy(i, 1).start()

    @pl.loop(1, 16)
    def _(i):
        lse_copy(i, 0).wait()
        lse_copy(i, 1).wait()

    lse_copy(0, 1).wait()
    tokens_write.wait()

    @pl.loop(0, 16)
    def _(i):
        probs_write(i).wait()


def last_and_lse(vocab, part, x, rest, gains, head, targets):
    tall = head.shape[0]
    return kernel_call(
        functools.partial(lse_body, vocab),
        [
            jax.ShapeDtypeStruct((BLOCK, D), F32),
            jax.ShapeDtypeStruct((16, 2 * BLOCK, D), BF),
            jax.ShapeDtypeStruct((16, tall, 2 * BLOCK), BF),
            jax.ShapeDtypeStruct((16, 2, 8, BLOCK), F32),
            jax.ShapeDtypeStruct((16, 2, 8, BLOCK), F32),
        ],
        (part, x, rest, gains, head, targets),
        [
            pltpu.VMEM((16, 2 * BLOCK, D), BF),
            pltpu.VMEM((16, tall, 2 * BLOCK), BF),
            pltpu.SemaphoreType.DMA((17,)),
            pltpu.VMEM((tall, 2 * BLOCK), F32),
            pltpu.VMEM((32, 8, BLOCK), F32),
        ]
        + SUM_SCRATCH
        + COLLECT_SEMS
        + sem_pairs(32, 32),
        8,
        56,
        out_specs=[VMEM_SPEC] + [pl.BlockSpec(memory_space=pl.ANY)] * 2 + [VMEM_SPEC] * 2,
    )


def loss_back_body(
    probs_in, stats, joined, targets, coefs, head_t, x, gains,
    steep, row_all, grad, grad_gains, slopes, probs, in_sems, keep, other, r1, s, r2, *sems,
):
    y, core, z = where_am_i()

    def read(i):
        yy, zz = chip(i, 1)
        return pltpu.make_async_copy(
            probs_in.at[yy * 4 + zz], probs.at[yy * 4 + zz], in_sems.at[i]
        )

    @pl.loop(1, 16)
    def _(i):
        read(i).start()

    read(0).start()
    greet(plane_peers(False))
    tall = head_t.shape[1]
    written = pltpu.make_async_copy(slopes, steep, sems[8])

    def group(i, c):
        read(i).wait()

        def row(ref):
            return jnp.concatenate([ref[c, 0, 0:1, :], ref[c, 1, 0:1, :]], 1)

        coef, wanted = coefs[c], targets[c]
        scale = jnp.exp(row(stats) - row(joined)) * coef
        lanes = pl.ds(pl.multiple_of(lax.rem(c, 4) * (2 * BLOCK), 2 * BLOCK), 2 * BLOCK)

        @pl.loop(0, tall // 128)
        def _(v):
            rows = pl.ds(pl.multiple_of(v * 128, 128), 128)
            hit = jnp.where(vocab_rows(v, 128) == wanted, coef, 0.0)
            slopes[lax.div(c, 4), rows, lanes] = (
                probs[c, rows, :].astype(F32) * scale - hit
            ).astype(BF)

        return jnp.dot(
            head_t[...], slopes[lax.div(c, 4), :, lanes], preferred_element_type=F32
        )

    total = plane_total(group, lambda: written.start(), keep, other, r1, s, r2, sems[:4])
    normed_grad = jnp.transpose(total)
    hat, _ = normed_rows(x[...])
    grad_gains[...] = jnp.concatenate(
        [
            jnp.sum(normed_grad * hat, 0, keepdims=True),
            jnp.sum(normed_grad, 0, keepdims=True),
            jnp.zeros((6, D), F32),
        ],
        0,
    )
    after = norm_back(x[...], normed_grad * gains[0:1])
    grad[...] = after
    row_all[z * 2 + core] = after.astype(BF)
    row_gather(row_all, sems[4:6], sems[6:8])
    written.wait()


def loss_back(probs, stats, joined, targets, coefs, head_t, x, gains):
    tall = head_t.shape[1]
    return kernel_call(
        loss_back_body,
        [
            jax.ShapeDtypeStruct((4, tall, 8 * BLOCK), BF),
            jax.ShapeDtypeStruct((8, BLOCK, D), BF),
            jax.ShapeDtypeStruct((BLOCK, D), F32),
            jax.ShapeDtypeStruct((8, D), F32),
        ],
        (probs, stats, joined, targets, coefs, head_t, x, gains),
        [
            pltpu.VMEM((4, tall, 8 * BLOCK), BF),
            pltpu.VMEM((16, tall, 2 * BLOCK), BF),
            pltpu.SemaphoreType.DMA((16,)),
        ]
        + TOTAL_SCRATCH
        + GATHER_SCRATCH
        + [pltpu.SemaphoreType.DMA],
        9,
        56,
        in_specs=[pl.BlockSpec(memory_space=pl.ANY)] + [VMEM_SPEC] * 7,
        out_specs=[pl.BlockSpec(memory_space=pl.ANY)] + [VMEM_SPEC] * 3,
    )


def lowest_body(layer, part, x, grad, ids, *refs):
    sources, grad_embed, sums, landed, give_sems = (
        refs[:2], refs[2], refs[3:5], refs[5:7], refs[7:11],
    )
    r1, s, r2, e, f, g, h, everyone, hot = refs[11:20]
    y, core, z = where_am_i()
    greet(plane_peers(False) + column_others())
    give_start(layer, sources, landed, give_sems)
    after = grad[...] + norm_back(x[...], row_sum(part, r1, s, r2, (e, f), (g, h)))
    everyone[y * 4 + z, core_rows(core)] = after.astype(BF)
    grad_embed[...] = jnp.zeros(grad_embed.shape, F32)

    def on_chip(i, where):
        onehot_into(hot, ids[where])
        grad_embed[...] += jnp.dot(hot[...], everyone[where], preferred_element_type=F32)

    plane_collect(everyone, refs[20:], on_chip)
    give_finish(layer, sources, landed, sums, give_sems)


def lowest_grad(layer, part, x, grad, ids, sources, tall):
    return kernel_call(
        functools.partial(lowest_body, layer),
        [jax.ShapeDtypeStruct((tall, D), F32)]
        + [jax.ShapeDtypeStruct(a.shape, F32) for a in sources],
        (part, x, grad, ids, *sources),
        give_scratch(sources)
        + SUM_SCRATCH
        + [pltpu.VMEM((16, 2 * BLOCK, D), BF), pltpu.VMEM((tall, 2 * BLOCK), BF)]
        + COLLECT_SEMS,
        6,
        56,
    )


def replicas_peers():
    x = lax.axis_index("xx")
    return [(lax.rem(x + k, 4), {"xx": lax.rem(x + k, 4)}) for k in FAR]


def replicas_exchange(block, everyone, a, b):
    x = lax.axis_index("xx")
    copies = [
        send(block, everyone.at[x], (a, b), i, device)
        for i, (_, device) in enumerate(replicas_peers())
    ]
    return copies


def features_body(layer, vocab, block, err, *refs):
    sources, everyone, places, ordered = refs[:2], refs[2], refs[3:5], refs[5]
    mixed, own_sem, err_sem, sems = refs[6], refs[7], refs[8], refs[9:]
    load = pltpu.make_async_copy(err, mixed, err_sem)
    load.start()
    greet([device for _, device in replicas_peers()] + pair_peer() + column_peers())
    copies = replicas_exchange(block, everyone, *sems[:2])
    own = pltpu.make_async_copy(block, everyone.at[lax.axis_index("xx")], own_sem)
    own.start()
    take_start(layer, sources, places, sems[2:])
    load.wait()

    def put_rows(start, count):
        for b in range(2):
            for tile in range(TILES):
                far = pl.ds(start * (2 * TILES) + 2 * tile + b, count, stride=2 * TILES)
                ordered[b, pl.ds(start, count), pl.ds(tile * 128, 128)] = mixed[far, :]

    whole = vocab // CHUNK * CHUNK
    ordered[:, pl.ds(whole, ordered.shape[1] - whole), :] = jnp.zeros(
        (2, ordered.shape[1] - whole, D), F32
    )

    @pl.loop(0, vocab // CHUNK)
    def _(c):
        put_rows(pl.multiple_of(c * CHUNK, CHUNK), CHUNK)

    put_rows(whole, vocab - whole)
    own.wait()
    for copy in copies:
        copy.wait()
    take_finish(layer, sources, places, sems[2:])


def all_features(block, layer, sources, err, vocab, tall):
    some = pl.BlockSpec(memory_space=pl.ANY)
    return kernel_call(
        functools.partial(features_body, layer, vocab),
        [jax.ShapeDtypeStruct((4, *block.shape), block.dtype)]
        + [jax.ShapeDtypeStruct(a.shape, a.dtype) for a in sources]
        + [jax.ShapeDtypeStruct((2, tall, D), F32)],
        (block, err, *sources),
        [pltpu.VMEM(err.shape, F32), pltpu.SemaphoreType.DMA, pltpu.SemaphoreType.DMA]
        + sem_pairs(3)
        + take_scratch(2),
        31,
        in_specs=[some] * 4,
        out_specs=[some] * 3 + [VMEM_SPEC],
    )


def halves(values):
    high = values.astype(BF)
    return high, (values - high.astype(F32)).astype(BF)


def short_dot(short, tall, contract):
    high, low = halves(tall)
    both = jnp.concatenate(halves(short), 0)
    first = lax.dot_general(both, high, (contract, ((), ())), preferred_element_type=F32)
    second = lax.dot_general(both, low, (contract, ((), ())), preferred_element_type=F32)
    return first[:RANK] + first[RANK:] + second[:RANK]


def outer_dot(left, right):
    (a, b), (c, d) = halves(left), halves(right)
    return dot_rows(jnp.concatenate([a, b, a], 0), jnp.concatenate([c, c, d], 0))


def factor_places(cols, rows, vocab):
    def up(n):
        return -(-n // 128) * 128

    half = up(cols) + -(-vocab // ROWS) * ROWS
    return half, ((0, 0, cols), (1, 0, rows), (0, up(cols), vocab), (1, up(rows), vocab))


def compress_body(
    vocab, g_embed_in, m_head_in, left_head, err, err_in, err_back, q_in, q_back, q_embed,
    ret0, ret1, ret2, ret3, bias0, bias1, bias2, bias3, out_rows, vectors,
    m_embed, m_layer, basis, own, sums, bias_sum, vector_sum,
    g_embed, m_head, errors, came, landed, out_sum, load_sems, give_send, give_recv,
    bias, left, left_came, bias_came, joint, joint_came, work, vec_came, vec_mine, vec_sums, vec_all,
    *sems,
):
    y, core, z = where_am_i()
    x = lax.axis_index("xx")
    me = y * 8 + core * 4 + z
    peers = []
    for k in range(1, 32):
        p = lax.rem(me + k, 32)
        peers.append((p, {**at_chip(p // 8, lax.rem(p, 4)), "co": lax.rem(p // 4, 2)}))
    own_layer = home_and_layer()[1]
    rets = (ret0, ret1, ret2, ret3)

    def load(index):
        size = rets[index].shape[0]
        return pltpu.make_async_copy(rets[index], came.at[pl.ds(0, size)], load_sems.at[0])

    def load_own(act):
        for index in range(LAYERS):

            @pl.when(own_layer == index)
            def _():
                act(load(index))

    load_err = pltpu.make_async_copy(err.at[0], errors, load_sems.at[1])
    load_embed = pltpu.make_async_copy(g_embed_in, g_embed, load_sems.at[2])
    load_head = pltpu.make_async_copy(m_head_in, m_head, load_sems.at[3])
    load_embed.start()
    load_err.start()
    load_own(lambda copy: copy.start())
    load_head.start()
    greet([device for _, device in peers] + [device for _, device in replicas_peers()])
    pairs = [(sems[2 * n], sems[2 * n + 1]) for n in range(len(sems) // 2)]
    vec_first = [
        send(vectors.at[p], vec_came.at[me], pairs[0], k, device)
        for k, (p, device) in enumerate(peers)
    ]
    vec_came[me] = vectors[me]

    cols, rows = err_in.shape[0], err_back.shape[0]
    half, places = factor_places(cols, rows, vocab)
    of_in, of_back = pl.ds(0, cols), pl.ds(cols, rows)
    give = (0, (out_rows,), (landed,))
    give_start(*give, (give_send, give_recv))
    for index, bias_part in enumerate((bias0, bias1, bias2, bias3)):

        @pl.when(own_layer == index)
        def _():
            bias[...] = bias_part[...]

    load_embed.wait()
    load_err.wait()
    m_embed[...] = g_embed[...] + errors[...]
    left[2] = short_dot(q_embed[...], m_embed[...], ((1,), (0,)))
    load_own(lambda copy: copy.wait())
    m_layer[of_in, :] = came[of_in, :] + err_in[...]
    left[0] = short_dot(q_in[...], m_layer[of_in, :], ((1,), (0,)))
    give_finish(*give, (out_sum,), (give_send, give_recv))

    @pl.when(own_layer == 0)
    def _():
        m_layer[of_back, :] = out_sum[...] + err_back[...]

    @pl.when(own_layer != 0)
    def _():
        m_layer[of_back, :] = came[of_back, :] + err_back[...]

    left[1] = short_dot(q_back[...], m_layer[of_back, :], ((1,), (0,)))
    load_head.wait()
    blocks = (m_layer.at[of_in], m_layer.at[of_back], m_embed, m_head)
    left[3] = left_head[...]

    for copy in vec_first:
        copy.wait_recv()
    vec_mine[...] = jnp.sum(vec_came[...], 0)
    second = []
    for n, (src, dst) in enumerate(
        ((left, left_came), (bias, bias_came), (vec_mine, vec_sums))
    ):
        second += replicas_exchange(src, dst, *pairs[1 + n])
    left_came[x] = left[...]
    bias_came[x] = bias[...]
    vec_sums[x] = vec_mine[...]
    for copy in second:
        copy.wait()
    bias_sum[...] = jnp.sum(bias_came[...], 0)
    vec_all[me] = jnp.sum(vec_sums[...], 0)
    mine = vec_all.at[me]
    third = [send(mine, mine, pairs[4], k, device) for k, (_, device) in enumerate(peers)]
    work[...] = jnp.sum(left_came[...], 0)
    order = lax.broadcasted_iota(jnp.int32, (1, RANK, 1), 1)
    for index in range(RANK):
        columns = work[...]
        one = columns[:, index : index + 1, :]
        one = one * lax.rsqrt(jnp.sum(one * one, -1, keepdims=True) + 1e-30)
        shares = jnp.sum(columns * one, -1, keepdims=True)
        work[...] = jnp.where(order > index, columns - shares * one, columns)
        basis[:, index : index + 1, :] = one

    own[...] = jnp.zeros(own.shape, F32)
    for b, block in enumerate(blocks):
        at = pl.ds(places[b][1], block.shape[0])
        own[places[b][0], :, at] = short_dot(basis[b], block[...], ((1,), (1,)))

    joint[...] = own[...].reshape(joint.shape).astype(BF)
    fourth = replicas_exchange(joint, joint_came, *pairs[5])
    joint_came[x] = joint[...]
    for copy in fourth:
        copy.wait()
    total = jnp.sum(joint_came[...].astype(F32), 0)
    sums[...] = total.reshape(sums.shape)
    for copy in vec_first:
        copy.wait_send()
    for copy in third:
        copy.wait()
    vector_sum[...] = vec_all[...]


def compressed(vocab, g_embed, m_head, left_head, err, errs, facs, returned, out_rows, vectors):
    half, _ = factor_places(errs[0].shape[0], errs[1].shape[0], vocab)
    tall = g_embed.shape
    layers = [r[0] for r in returned]
    rows = (errs[0].shape[0] + errs[1].shape[0], D)
    some = pl.BlockSpec(memory_space=pl.ANY)
    biases = [r[1] for r in returned]
    bias = biases[0]
    return kernel_call(
        functools.partial(compress_body, vocab),
        [
            jax.ShapeDtypeStruct(s, F32)
            for s in (
                tall, rows, (4, 8, D), (2, 8, half), (2, 8, half), bias.shape,
                vectors.shape,
            )
        ],
        (g_embed, m_head, left_head, err, *errs, *facs, *layers, *biases, out_rows, vectors),
        [
            pltpu.VMEM(tall, F32),
            pltpu.VMEM(tall, F32),
            pltpu.VMEM(tall, F32),
            pltpu.VMEM(rows, F32),
            pltpu.VMEM((4, *out_rows.shape), BF),
            pltpu.VMEM(out_rows.shape, F32),
            pltpu.SemaphoreType.DMA((4,)),
            pltpu.SemaphoreType.DMA((1,)),
            pltpu.SemaphoreType.DMA((4,)),
            pltpu.VMEM(bias.shape, F32),
            pltpu.VMEM((4, 8, D), F32),
            pltpu.VMEM((4, 4, 8, D), F32),
            pltpu.VMEM((4, *bias.shape), F32),
            pltpu.VMEM((16, half), BF),
            pltpu.VMEM((4, 16, half), BF),
            pltpu.VMEM((4, 8, D), F32),
            pltpu.VMEM(vectors.shape, F32),
            pltpu.VMEM(vectors.shape[1:], F32),
            pltpu.VMEM((4, *vectors.shape[1:]), F32),
            pltpu.VMEM(vectors.shape, F32),
        ]
        + sem_pairs(31, 3, 3, 3, 31, 3),
        30,
        56,
        in_specs=[some, some, VMEM_SPEC, some] + [VMEM_SPEC] * 5 + [some] * 4 + [VMEM_SPEC] * 6,
    )


def ema_decay():
    return min(0.999, (1.0 + STEP) / (10.0 + STEP))


def stepped(rate, weight, moment, average, grad):
    decay = ema_decay()
    new_moment = MOMENTUM * moment + (1.0 - MOMENTUM) * grad
    new_weight = weight - rate * new_moment
    return new_weight, new_moment, decay * average + (1.0 - decay) * new_weight


def update_body(
    vocab, rates, m_embed, m_head, m_layer, basis, own, sums, bias_sum, vector_sum, *refs
):
    rate_layer, rate_vector, rate_tables = rates
    olds, new = refs[:18], refs[18:36]
    (err_tab, err_in, err_back, *factors) = refs[36:]
    x = lax.axis_index("xx")
    cols, rows = err_in.shape[0], err_back.shape[0]
    half, places = factor_places(cols, rows, vocab)
    own_cols = pl.ds(pl.multiple_of(x * 128, 128), 128)
    step = pl.program_id(0)
    start = pl.multiple_of(step * ROWS, ROWS)

    def change(rate, group, at, reduced):
        values = stepped(rate, *[old[at] for old in olds[group : group + 3]], reduced)
        for out, value in zip(new[group : group + 3], values):
            out[at] = value

    for b, matrix in ((2, m_embed), (3, m_head)):
        lanes = pl.ds(pl.multiple_of(places[b][1] + start, 128), ROWS)
        product = outer_dot(own[places[b][0], :, lanes], basis[b])
        for tile in range(TILES):
            far = pl.ds(2 * tile + b - 2, ROWS, stride=2 * TILES)
            lane = slice(tile * 128, (tile + 1) * 128)
            err_tab[far, :] = matrix[:, lane] - product[:, lane]
        reduced = outer_dot(sums[places[b][0], :, lanes], basis[b, :, own_cols])
        change(rate_tables[b - 2], 6, (pl.ds(b - 2, ROWS, stride=2), slice(None)), reduced)

    @pl.when(step == 0)
    def _():
        for b, (first, count, err) in enumerate(((0, cols, err_in), (cols, rows, err_back))):
            for begin in range(0, count, CHUNK):
                size = min(CHUNK, count - begin)
                at = (pl.ds(begin, size), slice(None))
                lanes = pl.ds(places[b][1] + begin, size)
                err[at] = m_layer[pl.ds(first + begin, size), :] - outer_dot(
                    own[places[b][0], :, lanes], basis[b]
                )
                reduced = outer_dot(sums[places[b][0], :, lanes], basis[b])
                change(rate_layer, 3 * b, at, reduced)
        for factor, (group, at, width) in zip(factors, places):
            factor[...] = sums[group, :, pl.ds(at, width)]
        change(rate_layer, 9, (slice(None), slice(None)), bias_sum[0:1, :cols])
        section = home_and_layer()[1]
        for tile in range(TILES):
            lanes = (slice(None), pl.ds(tile * 128, 128))
            change(rate_vector, 12, lanes, vector_sum[pl.ds(section * 6, 6), tile, :])
            final = vector_sum[6 * LAYERS : 6 * LAYERS + 2, tile, :]
            change(rate_layer, 15, lanes, final)


def updated(vocab, rates, m_tables, m_layer, basis, own, sums, bias_sum, vector_sum, params):
    cols, rows = params[0].shape[0], params[3].shape[0]

    def whole(shape):
        return pl.BlockSpec(shape, lambda step: (0,) * len(shape))

    def spec(index, array):
        if 6 <= index < 9:
            return pl.BlockSpec((2 * ROWS, 128), lambda step: (step, 0))
        return whole(array.shape)

    before = (*m_tables, m_layer, basis, own, sums, bias_sum, vector_sum)
    factors = [(RANK, cols), (RANK, rows), (RANK, vocab), (RANK, vocab)]
    outs = [a.shape for a in params] + [(vocab * 8, 128), (cols, D), (rows, D)] + factors
    param_specs = [spec(n, a) for n, a in enumerate(params)]
    return pl.pallas_call(
        functools.partial(update_body, vocab, rates),
        grid=(-(-vocab // ROWS),),
        out_shape=[jax.ShapeDtypeStruct(a, F32) for a in outs],
        in_specs=[pl.BlockSpec((ROWS, D), lambda step: (step, 0))] * 2
        + [whole(a.shape) for a in before[2:]]
        + param_specs,
        out_specs=param_specs
        + [pl.BlockSpec((8 * ROWS, 128), lambda step: (step, 0))]
        + [whole(a) for a in outs[19:]],
        compiler_params=pltpu.CompilerParams(vmem_limit_bytes=56 * 2**20),
    )(*before, *params)


def rotary_tables():
    half_rot = ROT // 2
    inverse = 10000.0 ** (-jnp.arange(half_rot, dtype=F32) * (2.0 / ROT))
    angles = jnp.arange(LENGTH, dtype=F32)[:, None] * inverse[None, :]
    return (jnp.cos(angles), jnp.sin(angles))


def rotate(heads, cosine, sine):
    half_rot = ROT // 2
    first = heads[..., :half_rot]
    second = heads[..., half_rot:ROT]
    return jnp.concatenate(
        [first * cosine - second * sine, second * cosine + first * sine, heads[..., ROT:]], -1
    )


ATT_BLOCK = 512


def causal(start, stop):
    rows = start + lax.broadcasted_iota(jnp.int32, (stop - start, stop), 0)
    return rows >= lax.broadcasted_iota(jnp.int32, (stop - start, stop), 1)


def attention_forward(q_rot, k_rot, v_val):
    outputs, all_lse = [], []
    for start in range(0, LENGTH, ATT_BLOCK):
        stop = start + ATT_BLOCK
        scores = dot_cols(q_rot[start:stop], k_rot[:stop]) * HEAD ** (-0.5)
        scores = jnp.where(causal(start, stop), scores, NEG_BIG)
        top = jnp.max(scores, -1, keepdims=True)
        expo = jnp.exp(scores - top)
        total = jnp.sum(expo, -1, keepdims=True)
        probs = (expo / total).astype(BF)
        outputs.append(dot_plain(probs, v_val[:stop]))
        all_lse.append(top + jnp.log(total))
    return (jnp.concatenate(outputs, 0), jnp.concatenate(all_lse, 0))


def attention_backward(q_rot, k_rot, v_val, lse, grad_out):
    scale = HEAD ** (-0.5)
    grad_query, grad_key, grad_value = [], 0.0, 0.0
    for start in range(0, LENGTH, ATT_BLOCK):
        stop = start + ATT_BLOCK
        spare = ((0, LENGTH - stop), (0, 0))
        scores = dot_cols(q_rot[start:stop], k_rot[:stop]) * scale
        probs = jnp.where(causal(start, stop), jnp.exp(scores - lse[start:stop]), 0.0)
        grad_probs = dot_cols(grad_out[start:stop], v_val[:stop])
        grad_scores = (
            probs * (grad_probs - jnp.sum(grad_probs * probs, -1, keepdims=True))
        ).astype(BF)
        grad_query.append(dot_plain(grad_scores, k_rot[:stop]) * scale)
        grad_key = grad_key + jnp.pad(dot_rows(grad_scores, q_rot[start:stop]), spare) * scale
        grad_value = grad_value + jnp.pad(
            dot_rows(probs.astype(BF), grad_out[start:stop]), spare
        )
    return (jnp.concatenate(grad_query, 0), grad_key, grad_value)


def block_forward(hat, weights, cosine, sine):
    w_all, bias, vector = weights
    w_cols, w_rows = w_all[: bias.shape[0]], w_all[bias.shape[0] :]
    wide = hat.astype(F32)
    first_in = (wide * vector[0] + vector[1]).astype(BF)
    second_in = (wide * vector[2] + vector[3]).astype(BF)
    qkv = dot_cols(first_in, w_cols[: 3 * HEAD]) + bias[: 3 * HEAD]
    up_val = dot_cols(second_in, w_cols[3 * HEAD :]) + bias[3 * HEAD :]
    q_rot = rotate(qkv[:, :HEAD], cosine, sine).astype(BF)
    k_rot = rotate(qkv[:, HEAD : 2 * HEAD], cosine, sine).astype(BF)
    v_val = qkv[:, 2 * HEAD :].astype(BF)
    attended, lse = attention_forward(q_rot, k_rot, v_val)
    attended = attended.astype(BF)
    hidden = jax.nn.gelu(up_val, approximate=False).astype(BF)
    branch = dot_plain(attended, w_rows[:HEAD]) + dot_plain(hidden, w_rows[HEAD:])
    return (
        branch.astype(BF),
        (hat, first_in, second_in, q_rot, k_rot, v_val, lse, attended, up_val, hidden),
    )


def gelu_exact(values):
    return jax.nn.gelu(values, approximate=False)


def block_backward(grad_low, kept, weights, cosine, sine):
    w_all, bias, vector = weights
    w_cols, w_rows = w_all[: bias.shape[0]], w_all[bias.shape[0] :]
    hat, first_in, second_in, q_rot, k_rot, v_val, lse, attended, up_val, hidden = kept
    grad_att = dot_cols(grad_low, w_rows[:HEAD]).astype(BF)
    grad_hidden = dot_cols(grad_low, w_rows[HEAD:])
    grad_up = jax.vjp(gelu_exact, up_val)[1](grad_hidden)[0].astype(BF)
    grad_query, grad_key, grad_value = attention_backward(q_rot, k_rot, v_val, lse, grad_att)
    grad_query = rotate(grad_query, cosine, -sine)
    grad_key = rotate(grad_key, cosine, -sine)
    grad_qkv = jnp.concatenate([grad_query, grad_key, grad_value], 1).astype(BF)
    grad_weights = (
        dot_rows(grad_qkv, first_in).astype(BF),
        dot_rows(grad_up, second_in).astype(BF),
        dot_rows(attended, grad_low).astype(BF),
        dot_rows(hidden, grad_low).astype(BF),
    )
    grad_bias = jnp.concatenate(
        [jnp.sum(grad_qkv.astype(F32), 0), jnp.sum(grad_up.astype(F32), 0)]
    )
    grad_first = dot_plain(grad_qkv, w_cols[: 3 * HEAD])
    grad_second = dot_plain(grad_up, w_cols[3 * HEAD :])
    wide = hat.astype(F32)
    grad_norms = jnp.stack(
        [
            jnp.sum(grad_first * wide, 0),
            jnp.sum(grad_first, 0),
            jnp.sum(grad_second * wide, 0),
            jnp.sum(grad_second, 0),
        ]
    )
    grad_hat = grad_first * vector[0] + grad_second * vector[2]
    return (grad_hat.astype(BF), (grad_weights, grad_bias, grad_norms))


def on_device(
    tokens,
    groups,
    counts,
    domain,
    w_in,
    w_back,
    tables,
    b_in,
    vecs,
    final_norm,
    w_in_mom,
    w_back_mom,
    tables_mom,
    b_in_mom,
    vecs_mom,
    final_mom,
    w_in_ema,
    w_back_ema,
    tables_ema,
    b_in_ema,
    vecs_ema,
    final_ema,
    w_in_err,
    w_back_err,
    tables_err,
    w_in_fac,
    w_back_fac,
    tables_fac,
):
    y, core, z = where_am_i()
    replica = lax.axis_index("xx")
    section = lax.axis_index("yl") * 2 + core
    vocab_part = section * 8 + lax.axis_index("yh") * 4 + z
    shard = core * 4 + z
    seq_rep = tokens.shape[0]
    row_total = seq_rep * LENGTH
    vocab_shard = tables.shape[1]
    own_cols = tables.shape[2]
    cosine, sine = rotary_tables()

    seq_index = jnp.arange(groups.shape[0], dtype=jnp.int32)
    live = seq_index % seq_rep < counts[seq_index // seq_rep]
    domain_hit = groups[:, None] == jnp.arange(domain.shape[0], dtype=jnp.int32)[None, :]
    seq_weight = jnp.where(live, jnp.sum(jnp.where(domain_hit, domain[None, :], 0.0), 1), 0.0)
    weight_total = jnp.sum(seq_weight)
    own_weight = lax.dynamic_slice_in_dim(seq_weight, replica * seq_rep, seq_rep, 0)
    token_ids = tokens[:, :LENGTH].reshape(-1)
    target_ids = tokens[:, 1:].reshape(-1)

    pad_ids = -vocab_shard % 128
    tall = vocab_shard + pad_ids
    short = jnp.pad(
        jnp.transpose(tables.astype(BF), (0, 2, 1)), ((0, 0), (0, 0), (0, pad_ids))
    )
    small = jnp.concatenate(
        [
            jnp.pad(vecs[0], ((0, 2), (0, 0))),
            jnp.pad(b_in, ((0, 7), (0, D - b_in.shape[1]))),
        ]
    )
    sources = (jnp.concatenate([w_in[0].T.astype(BF), w_back[0].astype(BF)]), small)
    err = jnp.transpose(
        tables_err.reshape(2, vocab_shard, D // 128, 128), (1, 2, 0, 3)
    ).reshape(-1, 128)
    embed_t, *packs_0, err = all_features(short[0], 0, sources, err, vocab_shard, tall)
    packs = {0: packs_0}
    head_t = lax.all_gather(short[1], "xx", axis=0, tiled=True)

    def own_ids(ids):
        local = ids - vocab_part * vocab_shard
        inside = (local >= 0) & (local < vocab_shard)
        return jnp.where(inside, local, -1).reshape(16, 1, 2 * BLOCK)

    own_tokens, own_targets = own_ids(token_ids), own_ids(target_ids)
    x, hat = embedded(embed_t.reshape(D, tall), own_tokens)
    head = jnp.transpose(head_t)

    weights, kept, before = [], [], []
    for index in range(LAYERS):
        w_all, rest = packs[index]
        weights.append((w_all, rest[8, : b_in.shape[1]], rest))
        before.append(x)
        branch, keep = block_forward(hat.reshape(LENGTH, D), weights[index], cosine, sine)
        kept.append(keep)
        branch = branch.reshape(8, BLOCK, D)
        if index + 1 < LAYERS:
            hat, x, *packs[index + 1] = next_hat(branch, x, rest, index + 1, sources)

    x, normed, probs, stats, joined = last_and_lse(
        vocab_shard, branch, x, rest, final_norm, head, own_targets
    )
    losses = joined[:, :, 1, :].reshape(seq_rep, LENGTH)
    loss_part = jnp.sum(own_weight * jnp.mean(losses, 1))
    coefs = jnp.broadcast_to(
        jnp.repeat(own_weight / (weight_total * LENGTH), 4)[:, None, None], (16, 1, 2 * BLOCK)
    )
    steep, grad_all, grad, grad_gains = loss_back(
        probs, stats, joined, own_targets, coefs, head_t, x, final_norm
    )
    grad_gains = grad_gains[:2]
    vector_rows = [None] * LAYERS
    grad_table = None
    returned = [None] * LAYERS
    for index in reversed(range(LAYERS)):
        outbias = jnp.sum(grad, 0)[None]
        grad_hat, (w_grad, bias_row, norm_rows) = block_backward(
            grad_all.reshape(LENGTH, D), kept[index], weights[index], cosine, sine
        )
        vector_rows[index] = jnp.concatenate([norm_rows, outbias, outbias], 0)
        w_grad_in, w_grad_out = w_grad[:2], w_grad[2:]
        w_grad = jnp.concatenate(w_grad if index else w_grad_in)
        given = (w_grad, jnp.pad(bias_row[None], ((0, 7), (0, D - bias_row.shape[0]))))
        grad_hat = grad_hat.reshape(8, BLOCK, D)
        if index >= LAYERS - 2:
            parts = (0, 1) if index == LAYERS - 1 else (2, 3)
            grad_all, grad, *returned[index], grad_table = next_grad(
                index, grad_hat, before[index], grad, given, parts, steep, normed, grad_table
            )
        elif index:
            *most, m_head, left_head = next_grad(
                index, grad_hat, before[index], grad, given, begun=grad_table,
                finish=(err, jnp.pad(tables_fac[1].T, ((0, 0), (0, pad_ids)))),
            )
            grad_all, grad, *returned[index] = most
        else:
            grad_embed, *returned[index] = lowest_grad(
                index, grad_hat, before[index], grad, own_tokens, given, tall
            )

    loss_row = jnp.zeros((1, D), F32).at[0, 0].set(jnp.where(shard + y * 8 == 0, loss_part, 0.0))
    vectors = jnp.concatenate(vector_rows + [grad_gains, loss_row], 0)
    vectors = jnp.pad(vectors, ((0, 32 - vectors.shape[0]), (0, 0))).reshape(32, D // 128, 128)
    vectors = jnp.pad(vectors, ((0, 0), (0, 8 - D // 128), (0, 0)))
    facs = (
        w_in_fac[0].T,
        w_back_fac[0].T,
        jnp.pad(tables_fac[0].T, ((0, 0), (0, pad_ids))),
    )
    errs = (w_in_err[0, 0].T, w_back_err[0, 0])
    m_embed, m_layer, basis, own, sums, bias_sum, vector_sums = compressed(
        vocab_shard, grad_embed, m_head, left_head, err, errs, facs, returned,
        jnp.concatenate(w_grad_out), vectors,
    )
    loss_sum = vector_sums[6 * LAYERS + 2, 0, 0]

    def of_tables(arrays):
        return [jnp.transpose(a, (1, 0, 2)).reshape(-1, 128) for a in arrays]

    token_count = lax.axis_size("xx") * seq_rep * LENGTH
    rate_layer = 2.0 * math.sqrt(token_count)
    rate_vector = 6.0 * math.sqrt(token_count)
    rate_tables = [rate * math.sqrt(token_count * VOCAB) for rate in (50.0, 0.5)]
    params = (
        [w_in[0].T, w_in_mom[0].T, w_in_ema[0].T, w_back[0], w_back_mom[0], w_back_ema[0]]
        + of_tables((tables, tables_mom, tables_ema))
        + [b_in, b_in_mom, b_in_ema, vecs[0], vecs_mom[0], vecs_ema[0]]
        + [final_norm, final_mom, final_ema]
    )
    new = updated(
        vocab_shard, (rate_layer, rate_vector, rate_tables), (m_embed, m_head), m_layer,
        basis, own, sums, bias_sum, vector_sums, params,
    )
    err_tab, err_in, err_back, fac_in, fac_back, fac_embed, fac_head = new[18:]
    err_tab = jnp.transpose(
        err_tab.reshape(vocab_shard, D // 128, 2, 128), (2, 0, 1, 3)
    ).reshape(tables_err.shape)
    in_w, in_m, in_e = [a.T[None] for a in new[:3]]
    back_w, back_m, back_e = [a[None] for a in new[3:6]]
    tab_w, tab_m, tab_e = [
        jnp.transpose(a.reshape(vocab_shard, 2, own_cols), (1, 0, 2)) for a in new[6:9]
    ]
    bias_w, bias_m, bias_e = new[9:12]
    vec_w, vec_m, vec_e = [a[None] for a in new[12:15]]
    fin_w, fin_m, fin_e = new[15:18]
    return (
        loss_sum,
        weight_total,
        in_w,
        back_w,
        tab_w,
        bias_w,
        vec_w,
        fin_w,
        in_m,
        back_m,
        tab_m,
        bias_m,
        vec_m,
        fin_m,
        in_e,
        back_e,
        tab_e,
        bias_e,
        vec_e,
        fin_e,
        err_in.T[None, None],
        err_back[None, None],
        err_tab,
        fac_in.T[None],
        fac_back.T[None],
        fac_embed.T,
        fac_head.T,
    )


def solution(mesh):
    fine = Mesh(
        np.asarray(mesh.devices).reshape(2, 2, 2, 4, 4), ("yl", "co", "yh", "zz", "xx")
    )
    names = {"section": ("yl", "co"), "tensor": ("yh", "zz"), "dp": ("xx",)}

    def spec(*axes):
        return P(*[None if a is None else sum((names[n] for n in a.split()), ()) for a in axes])

    layer_in, layer_back = spec("section", None, "tensor"), spec("section", "tensor", None)
    table, bias = spec(None, "section tensor", "dp"), spec("section", "tensor")
    vector = spec("section", None, None)
    params = (layer_in, layer_back, table, bias, vector, P())
    errors = (
        spec("dp", "section", None, "tensor"),
        spec("dp", "section", "tensor", None),
        spec("dp", None, "section tensor", None),
    )
    in_specs = (
        (spec("dp", None), P(), P(), P())
        + params * 3
        + errors
        + (layer_back, layer_back, spec(None, "section tensor", None))
    )
    out_specs = (
        (P(), P())
        + params * 3
        + errors
        + (layer_back, layer_back, spec("section tensor", None), spec("section tensor", None))
    )
    return jax.shard_map(
        on_device, mesh=fine, in_specs=in_specs, out_specs=out_specs, check_vma=False
    )
```

```python
import functools
import math

import jax
import jax.numpy as jnp
import numpy as np
from jax import lax
from jax.experimental import pallas as pl
from jax.experimental.pallas import tpu as pltpu
from jax.sharding import Mesh
from jax.sharding import PartitionSpec as P

D = 512
HEAD = 64
ROT = 16
VOCAB = 50304
LAYERS = 4
LENGTH = 1024
RANK = 8
STEP = 5
BLOCK = 128
CHUNK = 128
ROWS = 256
TILES = D // 128

EPS_NORM = 1e-05
MOMENTUM = 0.9
NEG_BIG = -1e30
HIGH = lax.Precision.HIGHEST
BF = jnp.bfloat16
F32 = jnp.float32
MESH_ID = pl.DeviceIdType.MESH
FAR = (2, 1, 3)


def where_am_i():
    core, z = lax.axis_index("co"), lax.axis_index("zz")
    y = lax.axis_index("yh") * 2 + lax.axis_index("yl")
    return y, core, z


def at_chip(y, z):
    return {"yh": y // 2, "yl": lax.rem(y, 2), "zz": z}


def send(src, dst, sems, at, device):
    copy = pltpu.make_async_remote_copy(
        src_ref=src,
        dst_ref=dst,
        send_sem=sems[0].at[at],
        recv_sem=sems[1].at[at],
        device_id=device,
        device_id_type=MESH_ID,
    )
    copy.start()
    return copy


def greet(devices):
    barrier = pltpu.get_barrier_semaphore()
    for device in devices:
        pl.semaphore_signal(barrier, inc=1, device_id=device, device_id_type=MESH_ID)
    pl.semaphore_wait(barrier, len(devices))


def sem_pairs(*counts):
    return [pltpu.SemaphoreType.DMA((n,)) for n in counts for _ in range(2)]


VMEM_SPEC = pl.BlockSpec(memory_space=pltpu.VMEM)


def kernel_call(
    body, out_shape, args, scratch, cid=None, limit=48, in_specs=None, out_specs=None
):
    many = isinstance(out_shape, (list, tuple))
    return pl.pallas_call(
        body,
        out_shape=out_shape,
        in_specs=in_specs or [VMEM_SPEC] * len(args),
        out_specs=out_specs or ([VMEM_SPEC] * len(out_shape) if many else VMEM_SPEC),
        scratch_shapes=scratch,
        compiler_params=pltpu.CompilerParams(
            collective_id=cid, has_side_effects=cid is not None, vmem_limit_bytes=limit * 2**20
        ),
    )(*args)


def dot_rows(left, right):
    return lax.dot_general(
        left, right, (((0,), (0,)), ((), ())), preferred_element_type=F32
    )


def dot_cols(left, right):
    return lax.dot_general(
        left, right, (((1,), (1,)), ((), ())), preferred_element_type=F32
    )


def dot_plain(left, right):
    return jnp.dot(left, right, preferred_element_type=F32)


def normed_rows(values):
    center = values - jnp.mean(values, -1, keepdims=True)
    spread = jnp.mean(center * center, -1, keepdims=True)
    scale = lax.rsqrt(spread + EPS_NORM)
    return center * scale, scale


def norm_back(values, grad):
    hat, scale = normed_rows(values)
    return scale * (
        grad
        - jnp.mean(grad, -1, keepdims=True)
        - hat * jnp.mean(grad * hat, -1, keepdims=True)
    )


def row_sum(part, r1, s, r2, sems1, sems2):
    y, core, z = where_am_i()
    first = []
    for i, k in enumerate(FAR + (0,)):
        zz = lax.rem(z + k, 4)
        first.append(send(part.at[zz * 2 + 1 - core], r1.at[i], sems1, i, {"co": 1 - core}))
    second = []
    for i, k in enumerate(FAR):
        zz = lax.rem(z + k, 4)
        first[i].wait_recv()
        s[i] = (part[zz * 2 + core].astype(F32) + r1[i].astype(F32)).astype(BF)
        second.append(send(s.at[i], r2.at[i], sems2, i, {"zz": zz}))
    first[3].wait_recv()
    total = part[z * 2 + core].astype(F32) + r1[3].astype(F32)
    for i in range(3):
        second[i].wait_recv()
        total = total + r2[i].astype(F32)
    for copy in first + second:
        copy.wait_send()
    return total


def row_gather(everyone, sems3, sems4):
    y, core, z = where_am_i()
    own = everyone.at[z * 2 + core]
    third = [
        send(own, own, sems3, i, {"zz": lax.rem(z + k, 4)}) for i, k in enumerate(FAR)
    ]
    fourth = [send(own, own, sems4, 3, {"co": 1 - core})]
    for i, k in enumerate(FAR):
        third[i].wait_recv()
        came = everyone.at[lax.rem(z + 4 - k, 4) * 2 + core]
        fourth.append(send(came, came, sems4, i, {"co": 1 - core}))
    for copy in third:
        copy.wait_send()
    for copy in fourth:
        copy.wait()


HALVES = [pl.ds(0, BLOCK // 2), pl.ds(BLOCK // 2, BLOCK // 2)]


def row_exchange(part, everyone, middle, r1, s, r2, sems, hooks):
    y, core, z = where_am_i()
    own = z * 2 + core
    first, second, third, fourth = [], [], [], []
    for h, rows in enumerate(HALVES):
        for i, k in enumerate(FAR + (0,)):
            block = part.at[lax.rem(z + k, 4) * 2 + 1 - core, rows]
            first.append(send(block, r1.at[i, rows], sems[0:2], 4 * h + i, {"co": 1 - core}))
    for h, rows in enumerate(HALVES):
        for i, k in enumerate(FAR):
            zz = lax.rem(z + k, 4)
            first[4 * h + i].wait_recv()
            s[i, rows] = (part[zz * 2 + core, rows].astype(F32) + r1[i, rows].astype(F32)).astype(BF)
            second.append(send(s.at[i, rows], r2.at[i, rows], sems[2:4], 3 * h + i, {"zz": zz}))
    hooks[0]()
    for h, rows in enumerate(HALVES):
        first[4 * h + 3].wait_recv()
        total = part[own, rows].astype(F32) + r1[3, rows].astype(F32)
        for i in range(3):
            second[3 * h + i].wait_recv()
            total = total + r2[i, rows].astype(F32)
        everyone[own, rows] = middle(rows, total).astype(BF)
        mine = everyone.at[own, rows]
        for i, k in enumerate(FAR):
            third.append(send(mine, mine, sems[4:6], 3 * h + i, {"zz": lax.rem(z + k, 4)}))
        fourth.append(send(mine, mine, sems[6:8], 6 + h, {"co": 1 - core}))
    hooks[1]()
    for h, rows in enumerate(HALVES):
        for i, k in enumerate(FAR):
            third[3 * h + i].wait_recv()
            came = everyone.at[lax.rem(z + 4 - k, 4) * 2 + core, rows]
            fourth.append(send(came, came, sems[6:8], 3 * h + i, {"co": 1 - core}))
    for copy in first + second + third:
        copy.wait_send()
    for copy in fourth:
        copy.wait()


def nothing():
    pass


def row_peers():
    y, core, z = where_am_i()
    return [{"co": 1 - core}] + [{"zz": lax.rem(z + k, 4)} for k in FAR]


SUM_SCRATCH = [
    pltpu.VMEM((4, BLOCK, D), BF),
    pltpu.VMEM((3, BLOCK, D), BF),
    pltpu.VMEM((3, BLOCK, D), BF),
] + sem_pairs(4, 3)
GATHER_SCRATCH = sem_pairs(3, 4)
EXCHANGE_SCRATCH = SUM_SCRATCH[:3] + sem_pairs(8, 6, 6, 8)


def pair_peer():
    return [{"co": 1 - lax.axis_index("co")}]


def column_peers():
    y, core, z = where_am_i()
    return [{**at_chip(lax.rem(y + dy, 4), z), "co": c} for dy in FAR for c in (0, 1)]


def column_others():
    y, core, z = where_am_i()
    return [{**at_chip(lax.rem(y + dy, 4), z), "co": 1 - core} for dy in FAR]


def home_and_layer():
    y, core, z = where_am_i()
    return y // 2 == core, lax.rem(y, 2) * 2 + core


def take_copies(sources, places, sems, dy):
    y, core, z = where_am_i()
    return [
        pltpu.make_async_remote_copy(
            src_ref=src,
            dst_ref=dst,
            send_sem=sems[2 * n].at[dy],
            recv_sem=sems[2 * n + 1].at[0],
            device_id={**at_chip(lax.rem(y + dy, 4), z), "co": y // 2},
            device_id_type=MESH_ID,
        )
        for n, (src, dst) in enumerate(zip(sources, places))
    ]


def take_local(sources, places, sems):
    return [
        pltpu.make_async_copy(src, dst, sems[2 * n + 1].at[0])
        for n, (src, dst) in enumerate(zip(sources, places))
    ]


def take_start(layer, sources, places, sems):
    home, own = home_and_layer()

    @pl.when(own == layer)
    def _():
        for dy in FAR:
            for copy in take_copies(sources, places, sems, dy):
                copy.start()

    @pl.when(jnp.logical_and(own == layer, home))
    def _():
        for copy in take_local(sources, places, sems):
            copy.start()

    @pl.when(jnp.logical_and(own == layer, jnp.logical_not(home)))
    def _():
        for copy in take_copies(sources, places, sems, 0):
            copy.start()


def take_finish(layer, sources, places, sems):
    home, own = home_and_layer()

    @pl.when(own == layer)
    def _():
        for dy in FAR:
            for copy in take_copies(sources, places, sems, dy):
                copy.wait_send()

    @pl.when(jnp.logical_and(own == layer, jnp.logical_not(home)))
    def _():
        for copy in take_copies(sources, places, sems, 0):
            copy.wait_send()

    for copy in take_local(sources, places, sems):
        copy.wait()


def take_scratch(count):
    return [pltpu.SemaphoreType.DMA((n,)) for _ in range(count) for n in (4, 1)]


def give_copies(layer, sources, landed, sems):
    y, core, z = where_am_i()
    return [
        pltpu.make_async_remote_copy(
            src_ref=src,
            dst_ref=dst.at[y],
            send_sem=sems[2 * n].at[0],
            recv_sem=sems[2 * n + 1].at[y],
            device_id={**at_chip(core * 2 + layer // 2, z), "co": layer % 2},
            device_id_type=MESH_ID,
        )
        for n, (src, dst) in enumerate(zip(sources, landed))
    ]


def give_start(layer, sources, landed, sems):
    y, core, z = where_am_i()
    home, own = home_and_layer()
    local = jnp.logical_and(home, own == layer)

    @pl.when(jnp.logical_not(local))
    def _():
        for copy in give_copies(layer, sources, landed, sems):
            copy.start()

    @pl.when(local)
    def _():
        for n, (src, dst) in enumerate(zip(sources, landed)):
            pltpu.make_async_copy(src, dst.at[y], sems[2 * n + 1].at[y]).start()


def give_finish(layer, sources, landed, sums, sems):
    home, own = home_and_layer()

    @pl.when(own == layer)
    def _():
        for n, (src, dst) in enumerate(zip(sources, landed)):
            for index in range(4):
                pltpu.make_async_copy(src, dst.at[index], sems[2 * n + 1].at[index]).wait()
            total = dst[0].astype(F32)
            for index in range(1, 4):
                total = total + dst[index].astype(F32)
            sums[n][...] = total

    @pl.when(jnp.logical_not(jnp.logical_and(home, own == layer)))
    def _():
        for copy in give_copies(layer, sources, landed, sems):
            copy.wait_send()


def give_scratch(grads):
    return [pltpu.VMEM((4, *g.shape), g.dtype) for g in grads] + [
        pltpu.SemaphoreType.DMA((n,)) for _ in grads for n in (1, 4)
    ]


def forward_body(layer, part, x, rest, *refs):
    sources, everyone, x_new, places, refs = refs[:2], refs[2], refs[3], refs[4:6], refs[6:]
    r1, s, r2, sems, side = refs[0], refs[1], refs[2], refs[3:11], refs[11:]
    greet(row_peers() + column_peers())
    take_start(layer, sources, places, side)

    def middle(rows, total):
        after = x[rows] + total + (rest[4:5] + rest[5:6])
        x_new[rows] = after
        return normed_rows(after)[0]

    row_exchange(part, everyone, middle, r1, s, r2, sems, (nothing, nothing))
    take_finish(layer, sources, places, side)


def next_hat(part, x, rest, layer, sources):
    return kernel_call(
        functools.partial(forward_body, layer),
        [jax.ShapeDtypeStruct((8, BLOCK, D), BF), jax.ShapeDtypeStruct((BLOCK, D), F32)]
        + [jax.ShapeDtypeStruct(a.shape, a.dtype) for a in sources],
        (part, x, rest, *sources),
        EXCHANGE_SCRATCH + take_scratch(len(sources)),
        10 + layer,
    )


def backward_body(layer, table_parts, finish, part, x, grad, *refs):
    sources, refs = refs[:2], refs[2:]
    begun, steep, tokens = (), None, None
    if table_parts:
        steep, tokens, refs = refs[0], refs[1], refs[2:]
        if table_parts[0]:
            begun, refs = refs[:1], refs[1:]
    if finish:
        begun, err, factor, refs = refs[0], refs[1], refs[2], refs[3:]
    everyone, g_new, sums, refs = refs[0], refs[1], refs[2:4], refs[4:]
    if table_parts:
        table_grad, refs = refs[0], refs[1:]
    if finish:
        matrix, left, refs = refs[0], refs[1], refs[2:]
    landed, give_sems, refs = refs[:2], refs[2:6], refs[6:]
    r1, s, r2, sems, refs = refs[0], refs[1], refs[2], refs[3:11], refs[11:]
    greet(row_peers() + column_peers())
    hooks = [nothing, nothing]
    if finish:
        errors, err_sem = refs
        load = pltpu.make_async_copy(err.at[1], errors, err_sem)
        load.start()

        def whole_matrix():
            load.wait()
            matrix[...] = begun[...] + errors[...]

        def left_factor():
            left[...] = short_dot(factor[...], matrix[...], ((1,), (0,)))

        hooks = [whole_matrix, left_factor]
    if table_parts:
        slopes, rows, sem_slopes, sem_rows = refs
        loads = []
        for n, q in enumerate(table_parts):
            loads.append(
                (
                    pltpu.make_async_copy(steep.at[q], slopes.at[n], sem_slopes.at[n]),
                    pltpu.make_async_copy(
                        tokens.at[pl.ds(q * 4, 4)], rows.at[pl.ds(n * 4, 4)], sem_rows.at[n]
                    ),
                )
            )
            for load in loads[n]:
                load.start()

        def table_step(n):
            for load in loads[n]:
                load.wait()
            product = dot_plain(slopes[n], rows[pl.ds(n * 4, 4)].reshape(8 * BLOCK, D))
            if n:
                table_grad[...] += product
            else:
                table_grad[...] = begun[0][...] + product if begun else product

        hooks = [lambda: table_step(0), lambda: table_step(1)]
    give_start(layer, sources, landed, give_sems)

    def middle(rows, total):
        after = grad[rows] + norm_back(x[rows], total)
        g_new[rows] = after
        return after

    row_exchange(part, everyone, middle, r1, s, r2, sems, hooks)
    give_finish(layer, sources, landed, sums, give_sems)


def next_grad(layer, part, x, grad, sources, table_parts=(), steep=None, tokens=None, begun=None,
              finish=None):
    some = pl.BlockSpec(memory_space=pl.ANY)
    args, specs, outs, scratch = [], [], [], []
    if table_parts:
        args = [steep, tokens] + ([] if begun is None else [begun])
        specs = [some, some] + ([] if begun is None else [VMEM_SPEC])
        outs = [jax.ShapeDtypeStruct((steep.shape[1], D), F32)]
        scratch = [
            pltpu.VMEM((2, *steep.shape[1:]), BF),
            pltpu.VMEM((8, *tokens.shape[1:]), BF),
            pltpu.SemaphoreType.DMA((2,)),
            pltpu.SemaphoreType.DMA((2,)),
        ]
    if finish:
        args, specs = [begun, *finish], [VMEM_SPEC, some, VMEM_SPEC]
        outs = [jax.ShapeDtypeStruct(begun.shape, F32), jax.ShapeDtypeStruct((RANK, D), F32)]
        scratch = [pltpu.VMEM(begun.shape, F32), pltpu.SemaphoreType.DMA]
    return kernel_call(
        functools.partial(backward_body, layer, table_parts, finish is not None),
        [jax.ShapeDtypeStruct((8, BLOCK, D), BF), jax.ShapeDtypeStruct((BLOCK, D), F32)]
        + [jax.ShapeDtypeStruct(a.shape, F32) for a in sources]
        + outs,
        (part, x, grad, *sources, *args),
        give_scratch(sources) + EXCHANGE_SCRATCH + scratch,
        20 + layer,
        in_specs=[VMEM_SPEC] * (3 + len(sources)) + specs,
    )


def offset(i):
    at = lax.rem(jnp.int32(i) * 5, 16)
    return lax.div(at, 4), lax.rem(at, 4)


def chip(i, sign):
    y, _, z = where_am_i()
    dy, dz = offset(i)
    return lax.rem(y + sign * dy + 4, 4), lax.rem(z + sign * dz + 4, 4)


def plane_peers(both_cores):
    y, core, z = where_am_i()
    found = [{"co": 1 - core}]
    for i in range(1, 16):
        for c in (core, 1 - core) if both_cores else (core,):
            found.append({**at_chip(*chip(i, 1)), "co": c})
    return found


def remote(src, dst, send_sem, recv_sem, device):
    return pltpu.make_async_remote_copy(
        src_ref=src,
        dst_ref=dst,
        send_sem=send_sem,
        recv_sem=recv_sem,
        device_id=device,
        device_id_type=MESH_ID,
    )


def core_rows(core):
    return pl.ds(pl.multiple_of(core * BLOCK, BLOCK), BLOCK)


AHEAD = 10


def plane_collect(everyone, sems, on_chip):
    y, core, z = where_am_i()
    a, b, c, d = sems
    own = everyone.at[y * 4 + z, core_rows(core)]

    def direct(i):
        return remote(own, own, a.at[i], b.at[i], at_chip(*chip(i, 1)))

    def across(i):
        yy, zz = chip(i, -1)
        came = everyone.at[yy * 4 + zz, core_rows(core)]
        return remote(came, came, c.at[i], d.at[i], {"co": 1 - core})

    def use(i):
        across(i).wait_recv()
        yy, zz = chip(i, -1)
        on_chip(i, yy * 4 + zz)

    across(0).start()
    for i in range(1, 1 + AHEAD):
        direct(i).start()
    use(0)
    direct(1 + AHEAD).start()
    direct(1).wait_recv()
    across(1).start()

    def step(i, more):
        if more:
            direct(i + AHEAD).start()
        direct(i).wait_recv()
        across(i).start()
        use(i - 1)

    @pl.loop(2, 16 - AHEAD)
    def _(i):
        step(i, True)

    @pl.loop(16 - AHEAD, 16)
    def _(i):
        step(i, False)

    use(15)

    @pl.loop(1, 16)
    def _(i):
        direct(i).wait_send()
        across(i).wait_send()

    across(0).wait_send()


COLLECT_SEMS = sem_pairs(16, 16)


def plane_total(group, between, keep, other, r1, s, r2, sems):
    y, core, z = where_am_i()
    a, b, c, d = sems

    def pair(i):
        return remote(other.at[i], r1.at[i], a.at[i], b.at[i], {"co": 1 - core})

    def away(i):
        return remote(s.at[i], r2.at[i], c.at[i], d.at[i], at_chip(*chip(i, 1)))

    def make(i):
        yy, zz = chip(i, 1)
        part = group(i, yy * 4 + zz)
        low, high = part[:, :BLOCK], part[:, BLOCK:]
        keep[i] = jnp.where(core == 0, low, high).astype(BF)
        other[i] = jnp.where(core == 0, high, low).astype(BF)
        pair(i).start()

    def forward(i):
        pair(i).wait_recv()
        s[i] = (keep[i].astype(F32) + r1[i].astype(F32)).astype(BF)
        away(i).start()

    make(1)

    @pl.loop(2, 16)
    def _(i):
        make(i)
        forward(i - 1)

    forward(15)
    make(0)
    between()
    pair(0).wait_recv()
    total = keep[0].astype(F32) + r1[0].astype(F32)

    def add(i, total):
        away(i).wait_recv()
        return total + r2[i].astype(F32)

    total = lax.fori_loop(1, 16, add, total)

    @pl.loop(1, 16)
    def _(i):
        pair(i).wait_send()
        away(i).wait_send()

    pair(0).wait_send()
    return total


TOTAL_SCRATCH = [pltpu.VMEM((16, D, BLOCK), BF) for _ in range(5)] + sem_pairs(16, 16)


def vocab_rows(v, rows):
    return v * rows + lax.broadcasted_iota(jnp.int32, (rows, 1), 0)


def onehot_into(place, ids):
    rows = place.shape[0]

    @pl.loop(0, rows // 128)
    def _(v):
        hit = vocab_rows(v, 128) == ids
        place[pl.ds(pl.multiple_of(v * 128, 128), 128), :] = jnp.where(hit, 1.0, 0.0).astype(BF)


def embed_body(table, ids, x, everyone, hot, keep, other, r1, s, r2, e, f, g, h, a, b, c, d):
    y, core, z = where_am_i()
    greet(plane_peers(False))

    def group(i, c):
        onehot_into(hot, ids[c])
        return jnp.dot(table[...], hot[...], preferred_element_type=F32)

    total = plane_total(group, lambda: None, keep, other, r1, s, r2, (e, f, g, h))
    rows = jnp.transpose(total)
    x[...] = rows
    everyone[z * 2 + core] = normed_rows(rows)[0].astype(BF)
    row_gather(everyone, (a, b), (c, d))


def embedded(table, ids):
    return kernel_call(
        embed_body,
        [jax.ShapeDtypeStruct((BLOCK, D), F32), jax.ShapeDtypeStruct((8, BLOCK, D), BF)],
        (table, ids),
        [pltpu.VMEM((table.shape[1], 2 * BLOCK), BF)] + TOTAL_SCRATCH + GATHER_SCRATCH,
        7,
    )


def lse_body(
    vocab, part, x, rest, gains, head, targets,
    x_new, tokens_out, probs_out, stats, joined,
    everyone, probs, out_sems, logits, came, r1, s, r2, *sems,
):
    y, core, z = where_am_i()
    greet(plane_peers(True))
    here = y * 4 + z
    a, b, c, d = sems[8:]
    shift = rest[4:5] + rest[5:6]
    after = x[...] + row_sum(part, r1, s, r2, sems[0:2], sems[2:4]) + shift
    x_new[...] = after
    everyone[here, core_rows(core)] = (
        normed_rows(after)[0] * gains[0:1] + gains[1:2]
    ).astype(BF)
    tall = head.shape[0]

    def stat_copy(i, flip, where):
        device = {**at_chip(*chip(i, -1)), "co": core if flip == 0 else 1 - core}
        to = core if flip == 0 else 1 - core
        return remote(
            stats.at[where, to], came.at[2 * i + flip], a.at[2 * i + flip], b.at[2 * i + flip], device
        )

    tokens_write = pltpu.make_async_copy(everyone, tokens_out, out_sems.at[16])

    def probs_write(i):
        yy, zz = chip(i, -1)
        return pltpu.make_async_copy(
            probs.at[yy * 4 + zz], probs_out.at[yy * 4 + zz], out_sems.at[i]
        )

    def on_chip(i, where):
        logits[...] = dot_cols(head[...], everyone[where])
        wanted = targets[where]

        whole = vocab // 128
        edge = pl.ds(whole * 128, tall - whole * 128)
        logits[edge, :] = jnp.where(
            vocab_rows(whole, tall - whole * 128) < vocab, logits[edge, :], NEG_BIG
        )

        def highest(v, top):
            value = logits[pl.ds(pl.multiple_of(v * 128, 128), 128), :]
            return jnp.maximum(top, jnp.max(value.reshape(16, 8, 2 * BLOCK), 0))

        top = lax.fori_loop(0, tall // 128, highest, jnp.full((8, 2 * BLOCK), NEG_BIG, F32))
        top = jnp.max(top, 0, keepdims=True)

        def summed(v, carry):
            rows = pl.ds(pl.multiple_of(v * 128, 128), 128)
            value = logits[rows, :]
            expo = jnp.exp(value - top)
            probs[where, rows, :] = expo.astype(BF)
            hit = jnp.where(vocab_rows(v, 128) == wanted, value, 0.0)
            return (
                carry[0] + jnp.sum(expo.reshape(16, 8, 2 * BLOCK), 0),
                carry[1] + jnp.sum(hit.reshape(16, 8, 2 * BLOCK), 0),
            )

        zero = jnp.zeros((8, 2 * BLOCK), F32)
        total, target = lax.fori_loop(0, tall // 128, summed, (zero, zero))
        found = jnp.concatenate(
            [
                top,
                jnp.sum(total, 0, keepdims=True),
                jnp.sum(target, 0, keepdims=True),
                jnp.zeros((5, 2 * BLOCK), F32),
            ],
            0,
        )
        stats[where, 0] = found[:, :BLOCK]
        stats[where, 1] = found[:, BLOCK:]
        probs_write(i).start()
        if isinstance(i, int) and i == 0:
            came[0] = stats[where, core]
        else:
            stat_copy(i, 0, where).start()
        stat_copy(i, 1, where).start()

    plane_collect(everyone, sems[4:8], on_chip)
    tokens_write.start()

    @pl.loop(1, 16)
    def _(i):
        stat_copy(i, 0, here).wait()
        stat_copy(i, 1, here).wait()

    stat_copy(0, 1, here).wait()
    top = jnp.max(came[:, 0, :], 0, keepdims=True)
    total = jnp.sum(came[:, 1, :] * jnp.exp(came[:, 0, :] - top), 0, keepdims=True)
    target = jnp.sum(came[:, 2, :], 0, keepdims=True)
    lse = top + jnp.log(total)
    joined[here, core] = jnp.concatenate([lse, lse - target, jnp.zeros((6, BLOCK), F32)], 0)
    mine = joined.at[here, core]

    def lse_copy(i, flip):
        device = {**at_chip(*chip(i, 1)), "co": core if flip == 0 else 1 - core}
        return remote(mine, mine, c.at[2 * i + flip], d.at[2 * i + flip], device)

    lse_copy(0, 1).start()

    @pl.loop(1, 16)
    def _(i):
        lse_copy(i, 0).start()
        lse_copy(i, 1).start()

    @pl.loop(1, 16)
    def _(i):
        lse_copy(i, 0).wait()
        lse_copy(i, 1).wait()

    lse_copy(0, 1).wait()
    tokens_write.wait()

    @pl.loop(0, 16)
    def _(i):
        probs_write(i).wait()


def last_and_lse(vocab, part, x, rest, gains, head, targets):
    tall = head.shape[0]
    return kernel_call(
        functools.partial(lse_body, vocab),
        [
            jax.ShapeDtypeStruct((BLOCK, D), F32),
            jax.ShapeDtypeStruct((16, 2 * BLOCK, D), BF),
            jax.ShapeDtypeStruct((16, tall, 2 * BLOCK), BF),
            jax.ShapeDtypeStruct((16, 2, 8, BLOCK), F32),
            jax.ShapeDtypeStruct((16, 2, 8, BLOCK), F32),
        ],
        (part, x, rest, gains, head, targets),
        [
            pltpu.VMEM((16, 2 * BLOCK, D), BF),
            pltpu.VMEM((16, tall, 2 * BLOCK), BF),
            pltpu.SemaphoreType.DMA((17,)),
            pltpu.VMEM((tall, 2 * BLOCK), F32),
            pltpu.VMEM((32, 8, BLOCK), F32),
        ]
        + SUM_SCRATCH
        + COLLECT_SEMS
        + sem_pairs(32, 32),
        8,
        56,
        out_specs=[VMEM_SPEC] + [pl.BlockSpec(memory_space=pl.ANY)] * 2 + [VMEM_SPEC] * 2,
    )


def loss_back_body(
    probs_in, stats, joined, targets, coefs, head_t, x, gains,
    steep, row_all, grad, grad_gains, slopes, probs, in_sems, keep, other, r1, s, r2, *sems,
):
    y, core, z = where_am_i()

    def read(i):
        yy, zz = chip(i, 1)
        return pltpu.make_async_copy(
            probs_in.at[yy * 4 + zz], probs.at[yy * 4 + zz], in_sems.at[i]
        )

    @pl.loop(1, 16)
    def _(i):
        read(i).start()

    read(0).start()
    greet(plane_peers(False))
    tall = head_t.shape[1]
    written = pltpu.make_async_copy(slopes, steep, sems[8])

    def group(i, c):
        read(i).wait()

        def row(ref):
            return jnp.concatenate([ref[c, 0, 0:1, :], ref[c, 1, 0:1, :]], 1)

        coef, wanted = coefs[lax.div(c, 4)], targets[c]
        scale = jnp.exp(row(stats) - row(joined)) * coef
        lanes = pl.ds(pl.multiple_of(lax.rem(c, 4) * (2 * BLOCK), 2 * BLOCK), 2 * BLOCK)

        @pl.loop(0, tall // 128)
        def _(v):
            rows = pl.ds(pl.multiple_of(v * 128, 128), 128)
            hit = jnp.where(vocab_rows(v, 128) == wanted, coef, 0.0)
            slopes[lax.div(c, 4), rows, lanes] = (
                probs[c, rows, :].astype(F32) * scale - hit
            ).astype(BF)

        return jnp.dot(
            head_t[...], slopes[lax.div(c, 4), :, lanes], preferred_element_type=F32
        )

    total = plane_total(group, lambda: written.start(), keep, other, r1, s, r2, sems[:4])
    normed_grad = jnp.transpose(total)
    hat, _ = normed_rows(x[...])
    grad_gains[...] = jnp.concatenate(
        [
            jnp.sum(normed_grad * hat, 0, keepdims=True),
            jnp.sum(normed_grad, 0, keepdims=True),
            jnp.zeros((6, D), F32),
        ],
        0,
    )
    after = norm_back(x[...], normed_grad * gains[0:1])
    grad[...] = after
    row_all[z * 2 + core] = after.astype(BF)
    row_gather(row_all, sems[4:6], sems[6:8])
    written.wait()


def loss_back(probs, stats, joined, targets, coefs, head_t, x, gains):
    tall = head_t.shape[1]
    return kernel_call(
        loss_back_body,
        [
            jax.ShapeDtypeStruct((4, tall, 8 * BLOCK), BF),
            jax.ShapeDtypeStruct((8, BLOCK, D), BF),
            jax.ShapeDtypeStruct((BLOCK, D), F32),
            jax.ShapeDtypeStruct((8, D), F32),
        ],
        (probs, stats, joined, targets, coefs, head_t, x, gains),
        [
            pltpu.VMEM((4, tall, 8 * BLOCK), BF),
            pltpu.VMEM((16, tall, 2 * BLOCK), BF),
            pltpu.SemaphoreType.DMA((16,)),
        ]
        + TOTAL_SCRATCH
        + GATHER_SCRATCH
        + [pltpu.SemaphoreType.DMA],
        9,
        56,
        in_specs=[pl.BlockSpec(memory_space=pl.ANY)] + [VMEM_SPEC] * 7,
        out_specs=[pl.BlockSpec(memory_space=pl.ANY)] + [VMEM_SPEC] * 3,
    )


def lowest_body(layer, part, x, grad, ids, *refs):
    sources, grad_embed, sums, landed, give_sems = (
        refs[:2], refs[2], refs[3:5], refs[5:7], refs[7:11],
    )
    r1, s, r2, e, f, g, h, everyone, hot = refs[11:20]
    y, core, z = where_am_i()
    greet(plane_peers(False) + column_others())
    give_start(layer, sources, landed, give_sems)
    after = grad[...] + norm_back(x[...], row_sum(part, r1, s, r2, (e, f), (g, h)))
    everyone[y * 4 + z, core_rows(core)] = after.astype(BF)
    grad_embed[...] = jnp.zeros(grad_embed.shape, F32)

    def on_chip(i, where):
        onehot_into(hot, ids[where])
        grad_embed[...] += jnp.dot(hot[...], everyone[where], preferred_element_type=F32)

    plane_collect(everyone, refs[20:], on_chip)
    give_finish(layer, sources, landed, sums, give_sems)


def lowest_grad(layer, part, x, grad, ids, sources, tall):
    return kernel_call(
        functools.partial(lowest_body, layer),
        [jax.ShapeDtypeStruct((tall, D), F32)]
        + [jax.ShapeDtypeStruct(a.shape, F32) for a in sources],
        (part, x, grad, ids, *sources),
        give_scratch(sources)
        + SUM_SCRATCH
        + [pltpu.VMEM((16, 2 * BLOCK, D), BF), pltpu.VMEM((tall, 2 * BLOCK), BF)]
        + COLLECT_SEMS,
        6,
        56,
    )


def replicas_peers():
    x = lax.axis_index("xx")
    return [(lax.rem(x + k, 4), {"xx": lax.rem(x + k, 4)}) for k in FAR]


def replicas_exchange(block, everyone, a, b):
    x = lax.axis_index("xx")
    copies = [
        send(block, everyone.at[x], (a, b), i, device)
        for i, (_, device) in enumerate(replicas_peers())
    ]
    return copies


def features_body(layer, vocab, block, err, *refs):
    sources, everyone, places, ordered = refs[:2], refs[2], refs[3:5], refs[5]
    mixed, own_sem, err_sem, sems = refs[6], refs[7], refs[8], refs[9:]
    load = pltpu.make_async_copy(err, mixed, err_sem)
    load.start()
    greet([device for _, device in replicas_peers()] + pair_peer() + column_peers())
    copies = replicas_exchange(block, everyone, *sems[:2])
    own = pltpu.make_async_copy(block, everyone.at[lax.axis_index("xx")], own_sem)
    own.start()
    take_start(layer, sources, places, sems[2:])
    load.wait()

    def put_rows(start, count):
        for b in range(2):
            for tile in range(TILES):
                far = pl.ds(start * (2 * TILES) + 2 * tile + b, count, stride=2 * TILES)
                ordered[b, pl.ds(start, count), pl.ds(tile * 128, 128)] = mixed[far, :]

    whole = vocab // CHUNK * CHUNK
    ordered[:, pl.ds(whole, ordered.shape[1] - whole), :] = jnp.zeros(
        (2, ordered.shape[1] - whole, D), F32
    )

    @pl.loop(0, vocab // CHUNK)
    def _(c):
        put_rows(pl.multiple_of(c * CHUNK, CHUNK), CHUNK)

    put_rows(whole, vocab - whole)
    own.wait()
    for copy in copies:
        copy.wait()
    take_finish(layer, sources, places, sems[2:])


def all_features(block, layer, sources, err, vocab, tall):
    some = pl.BlockSpec(memory_space=pl.ANY)
    return kernel_call(
        functools.partial(features_body, layer, vocab),
        [jax.ShapeDtypeStruct((4, *block.shape), block.dtype)]
        + [jax.ShapeDtypeStruct(a.shape, a.dtype) for a in sources]
        + [jax.ShapeDtypeStruct((2, tall, D), F32)],
        (block, err, *sources),
        [pltpu.VMEM(err.shape, F32), pltpu.SemaphoreType.DMA, pltpu.SemaphoreType.DMA]
        + sem_pairs(3)
        + take_scratch(2),
        31,
        in_specs=[some] * 4,
        out_specs=[some] * 3 + [VMEM_SPEC],
    )


def halves(values):
    high = values.astype(BF)
    return high, (values - high.astype(F32)).astype(BF)


def short_dot(short, tall, contract):
    high, low = halves(tall)
    both = jnp.concatenate(halves(short), 0)
    first = lax.dot_general(both, high, (contract, ((), ())), preferred_element_type=F32)
    second = lax.dot_general(both, low, (contract, ((), ())), preferred_element_type=F32)
    return first[:RANK] + first[RANK:] + second[:RANK]


def outer_dot(left, right):
    (a, b), (c, d) = halves(left), halves(right)
    return dot_rows(jnp.concatenate([a, b, a], 0), jnp.concatenate([c, c, d], 0))


def factor_places(cols, rows, vocab):
    def up(n):
        return -(-n // 128) * 128

    half = up(cols) + -(-vocab // ROWS) * ROWS
    return half, ((0, 0, cols), (1, 0, rows), (0, up(cols), vocab), (1, up(rows), vocab))


def compress_body(
    vocab, g_embed_in, m_head_in, left_head, err, err_in, err_back, q_in, q_back, q_embed,
    ret0, ret1, ret2, ret3, bias0, bias1, bias2, bias3, out_rows, vectors,
    m_embed_out, m_layer_out, basis, own, sums, bias_sum, vector_sum,
    m_embed, m_layer, g_embed, m_head, errors, came, landed, out_sum, load_sems, give_send, give_recv,
    bias, left, left_came, bias_came, joint, joint_came, work, vec_came, vec_mine, vec_sums, vec_all,
    *sems,
):
    y, core, z = where_am_i()
    x = lax.axis_index("xx")
    me = y * 8 + core * 4 + z
    peers = []
    for k in range(1, 32):
        p = lax.rem(me + k, 32)
        peers.append((p, {**at_chip(p // 8, lax.rem(p, 4)), "co": lax.rem(p // 4, 2)}))
    own_layer = home_and_layer()[1]
    rets = (ret0, ret1, ret2, ret3)

    def load(index):
        size = rets[index].shape[0]
        return pltpu.make_async_copy(rets[index], came.at[pl.ds(0, size)], load_sems.at[0])

    def load_own(act):
        for index in range(LAYERS):

            @pl.when(own_layer == index)
            def _():
                act(load(index))

    load_err = pltpu.make_async_copy(err.at[0], errors, load_sems.at[1])
    load_embed = pltpu.make_async_copy(g_embed_in, g_embed, load_sems.at[2])
    load_head = pltpu.make_async_copy(m_head_in, m_head, load_sems.at[3])
    load_embed.start()
    load_err.start()
    m_embed_write = pltpu.make_async_copy(m_embed, m_embed_out, load_sems.at[4])
    m_layer_write = pltpu.make_async_copy(m_layer, m_layer_out, load_sems.at[5])
    load_own(lambda copy: copy.start())
    load_head.start()
    greet([device for _, device in peers] + [device for _, device in replicas_peers()])
    give = (0, (out_rows,), (landed,))
    give_start(*give, (give_send, give_recv))
    pairs = [(sems[2 * n], sems[2 * n + 1]) for n in range(len(sems) // 2)]
    vec_first = [
        send(vectors.at[p], vec_came.at[me], pairs[0], k, device)
        for k, (p, device) in enumerate(peers)
    ]
    vec_came[me] = vectors[me]

    cols, rows = err_in.shape[0], err_back.shape[0]
    half, places = factor_places(cols, rows, vocab)
    of_in, of_back = pl.ds(0, cols), pl.ds(cols, rows)
    for index, bias_part in enumerate((bias0, bias1, bias2, bias3)):

        @pl.when(own_layer == index)
        def _():
            bias[...] = bias_part[...]

    load_embed.wait()
    load_err.wait()
    m_embed[...] = g_embed[...] + errors[...]
    left[2] = short_dot(q_embed[...], m_embed[...], ((1,), (0,)))
    load_own(lambda copy: copy.wait())
    m_layer[of_in, :] = came[of_in, :] + err_in[...]
    left[0] = short_dot(q_in[...], m_layer[of_in, :], ((1,), (0,)))
    give_finish(*give, (out_sum,), (give_send, give_recv))

    @pl.when(own_layer == 0)
    def _():
        m_layer[of_back, :] = out_sum[...] + err_back[...]

    @pl.when(own_layer != 0)
    def _():
        m_layer[of_back, :] = came[of_back, :] + err_back[...]

    left[1] = short_dot(q_back[...], m_layer[of_back, :], ((1,), (0,)))
    load_head.wait()
    blocks = (m_layer.at[of_in], m_layer.at[of_back], m_embed, m_head)
    left[3] = left_head[...]

    second = replicas_exchange(left, left_came, *pairs[1])
    second += replicas_exchange(bias, bias_came, *pairs[2])
    left_came[x] = left[...]
    bias_came[x] = bias[...]
    m_embed_write.start()
    m_layer_write.start()
    for copy in vec_first:
        copy.wait_recv()
    vec_mine[...] = jnp.sum(vec_came[...], 0)
    vec_second = replicas_exchange(vec_mine, vec_sums, *pairs[3])
    vec_sums[x] = vec_mine[...]
    for copy in second:
        copy.wait()
    bias_sum[...] = jnp.sum(bias_came[...], 0)
    work[...] = jnp.sum(left_came[...], 0)
    order = lax.broadcasted_iota(jnp.int32, (1, RANK, 1), 1)
    for index in range(RANK):
        columns = work[...]
        one = columns[:, index : index + 1, :]
        one = one * lax.rsqrt(jnp.sum(one * one, -1, keepdims=True) + 1e-30)
        shares = jnp.sum(columns * one, -1, keepdims=True)
        work[...] = jnp.where(order > index, columns - shares * one, columns)
        basis[:, index : index + 1, :] = one

    own[...] = jnp.zeros(own.shape, F32)
    for b, block in enumerate(blocks):
        at = pl.ds(places[b][1], block.shape[0])
        own[places[b][0], :, at] = short_dot(basis[b], block[...], ((1,), (1,)))

    joint[...] = own[...].reshape(joint.shape).astype(BF)
    fourth = replicas_exchange(joint, joint_came, *pairs[5])
    joint_came[x] = joint[...]
    for copy in vec_second:
        copy.wait()
    vec_all[me] = jnp.sum(vec_sums[...], 0)
    mine = vec_all.at[me]
    third = [send(mine, mine, pairs[4], k, device) for k, (_, device) in enumerate(peers)]
    for copy in fourth:
        copy.wait()
    total = jnp.sum(joint_came[...].astype(F32), 0)
    sums[...] = total.reshape(sums.shape)
    for copy in vec_first:
        copy.wait_send()
    for copy in third:
        copy.wait()
    vector_sum[...] = vec_all[...]
    m_embed_write.wait()
    m_layer_write.wait()


def compressed(vocab, g_embed, m_head, left_head, err, errs, facs, returned, out_rows, vectors):
    half, _ = factor_places(errs[0].shape[0], errs[1].shape[0], vocab)
    tall = g_embed.shape
    layers = [r[0] for r in returned]
    rows = (errs[0].shape[0] + errs[1].shape[0], D)
    some = pl.BlockSpec(memory_space=pl.ANY)
    biases = [r[1] for r in returned]
    bias = biases[0]
    return kernel_call(
        functools.partial(compress_body, vocab),
        [
            jax.ShapeDtypeStruct(s, F32)
            for s in (
                tall, rows, (4, 8, D), (2, 8, half), (2, 8, half), bias.shape,
                vectors.shape,
            )
        ],
        (g_embed, m_head, left_head, err, *errs, *facs, *layers, *biases, out_rows, vectors),
        [
            pltpu.VMEM(tall, F32),
            pltpu.VMEM(rows, F32),
            pltpu.VMEM(tall, F32),
            pltpu.VMEM(tall, F32),
            pltpu.VMEM(tall, F32),
            pltpu.VMEM(rows, F32),
            pltpu.VMEM((4, *out_rows.shape), BF),
            pltpu.VMEM(out_rows.shape, F32),
            pltpu.SemaphoreType.DMA((6,)),
            pltpu.SemaphoreType.DMA((1,)),
            pltpu.SemaphoreType.DMA((4,)),
            pltpu.VMEM(bias.shape, F32),
            pltpu.VMEM((4, 8, D), F32),
            pltpu.VMEM((4, 4, 8, D), F32),
            pltpu.VMEM((4, *bias.shape), F32),
            pltpu.VMEM((16, half), BF),
            pltpu.VMEM((4, 16, half), BF),
            pltpu.VMEM((4, 8, D), F32),
            pltpu.VMEM(vectors.shape, F32),
            pltpu.VMEM(vectors.shape[1:], F32),
            pltpu.VMEM((4, *vectors.shape[1:]), F32),
            pltpu.VMEM(vectors.shape, F32),
        ]
        + sem_pairs(31, 3, 3, 3, 31, 3),
        30,
        56,
        in_specs=[some, some, VMEM_SPEC, some] + [VMEM_SPEC] * 5 + [some] * 4 + [VMEM_SPEC] * 6,
        out_specs=[some, some] + [VMEM_SPEC] * 5,
    )


def ema_decay():
    return min(0.999, (1.0 + STEP) / (10.0 + STEP))


def stepped(rate, weight, moment, average, grad):
    decay = ema_decay()
    new_moment = MOMENTUM * moment + (1.0 - MOMENTUM) * grad
    new_weight = weight - rate * new_moment
    return new_weight, new_moment, decay * average + (1.0 - decay) * new_weight


def update_body(
    vocab, rates, m_embed, m_head, m_layer, basis, own, sums, bias_sum, vector_sum, *refs
):
    rate_layer, rate_vector, rate_tables = rates
    olds, new = refs[:18], refs[18:36]
    (err_tab, err_in, err_back, *factors) = refs[36:]
    x = lax.axis_index("xx")
    cols, rows = err_in.shape[0], err_back.shape[0]
    half, places = factor_places(cols, rows, vocab)
    own_cols = pl.ds(pl.multiple_of(x * 128, 128), 128)
    step = pl.program_id(0)
    start = pl.multiple_of(step * ROWS, ROWS)

    def change(rate, group, at, reduced):
        values = stepped(rate, *[old[at] for old in olds[group : group + 3]], reduced)
        for out, value in zip(new[group : group + 3], values):
            out[at] = value

    for b, matrix in ((2, m_embed), (3, m_head)):
        lanes = pl.ds(pl.multiple_of(places[b][1] + start, 128), ROWS)
        product = outer_dot(own[places[b][0], :, lanes], basis[b])
        for tile in range(TILES):
            far = pl.ds(2 * tile + b - 2, ROWS, stride=2 * TILES)
            lane = slice(tile * 128, (tile + 1) * 128)
            err_tab[far, :] = matrix[:, lane] - product[:, lane]
        reduced = outer_dot(sums[places[b][0], :, lanes], basis[b, :, own_cols])
        change(rate_tables[b - 2], 6, (pl.ds(b - 2, ROWS, stride=2), slice(None)), reduced)

    @pl.when(step == 0)
    def _():
        for b, (first, count, err) in enumerate(((0, cols, err_in), (cols, rows, err_back))):
            for begin in range(0, count, CHUNK):
                size = min(CHUNK, count - begin)
                at = (pl.ds(begin, size), slice(None))
                lanes = pl.ds(places[b][1] + begin, size)
                err[at] = m_layer[pl.ds(first + begin, size), :] - outer_dot(
                    own[places[b][0], :, lanes], basis[b]
                )
                reduced = outer_dot(sums[places[b][0], :, lanes], basis[b])
                change(rate_layer, 3 * b, at, reduced)
        for factor, (group, at, width) in zip(factors, places):
            factor[...] = sums[group, :, pl.ds(at, width)]
        change(rate_layer, 9, (slice(None), slice(None)), bias_sum[0:1, :cols])
        section = home_and_layer()[1]
        for tile in range(TILES):
            lanes = (slice(None), pl.ds(tile * 128, 128))
            change(rate_vector, 12, lanes, vector_sum[pl.ds(section * 6, 6), tile, :])
            final = vector_sum[6 * LAYERS : 6 * LAYERS + 2, tile, :]
            change(rate_layer, 15, lanes, final)


def updated(vocab, rates, m_tables, m_layer, basis, own, sums, bias_sum, vector_sum, params):
    cols, rows = params[0].shape[0], params[3].shape[0]

    def whole(shape):
        return pl.BlockSpec(shape, lambda step: (0,) * len(shape))

    def spec(index, array):
        if 6 <= index < 9:
            return pl.BlockSpec((2 * ROWS, 128), lambda step: (step, 0))
        return whole(array.shape)

    before = (*m_tables, m_layer, basis, own, sums, bias_sum, vector_sum)
    factors = [(RANK, cols), (RANK, rows), (RANK, vocab), (RANK, vocab)]
    outs = [a.shape for a in params] + [(vocab * 8, 128), (cols, D), (rows, D)] + factors
    param_specs = [spec(n, a) for n, a in enumerate(params)]
    return pl.pallas_call(
        functools.partial(update_body, vocab, rates),
        grid=(-(-vocab // ROWS),),
        out_shape=[jax.ShapeDtypeStruct(a, F32) for a in outs],
        in_specs=[pl.BlockSpec((ROWS, D), lambda step: (step, 0))] * 2
        + [whole(a.shape) for a in before[2:]]
        + param_specs,
        out_specs=param_specs
        + [pl.BlockSpec((8 * ROWS, 128), lambda step: (step, 0))]
        + [whole(a) for a in outs[19:]],
        compiler_params=pltpu.CompilerParams(vmem_limit_bytes=56 * 2**20),
    )(*before, *params)


def rotary_tables():
    half_rot = ROT // 2
    inverse = 10000.0 ** (-jnp.arange(half_rot, dtype=F32) * (2.0 / ROT))
    angles = jnp.arange(LENGTH, dtype=F32)[:, None] * inverse[None, :]
    return (jnp.cos(angles), jnp.sin(angles))


def rotate(heads, cosine, sine):
    half_rot = ROT // 2
    first = heads[..., :half_rot]
    second = heads[..., half_rot:ROT]
    return jnp.concatenate(
        [first * cosine - second * sine, second * cosine + first * sine, heads[..., ROT:]], -1
    )


ATT_BLOCK = 512


def causal(start, stop):
    rows = start + lax.broadcasted_iota(jnp.int32, (stop - start, stop), 0)
    return rows >= lax.broadcasted_iota(jnp.int32, (stop - start, stop), 1)


def attention_forward(q_rot, k_rot, v_val):
    outputs, all_lse = [], []
    for start in range(0, LENGTH, ATT_BLOCK):
        stop = start + ATT_BLOCK
        scores = dot_cols(q_rot[start:stop], k_rot[:stop]) * HEAD ** (-0.5)
        scores = jnp.where(causal(start, stop), scores, NEG_BIG)
        top = jnp.max(scores, -1, keepdims=True)
        expo = jnp.exp(scores - top)
        total = jnp.sum(expo, -1, keepdims=True)
        probs = (expo / total).astype(BF)
        outputs.append(dot_plain(probs, v_val[:stop]))
        all_lse.append(top + jnp.log(total))
    return (jnp.concatenate(outputs, 0), jnp.concatenate(all_lse, 0))


def attention_backward(q_rot, k_rot, v_val, lse, grad_out):
    scale = HEAD ** (-0.5)
    grad_query, grad_key, grad_value = [], 0.0, 0.0
    for start in range(0, LENGTH, ATT_BLOCK):
        stop = start + ATT_BLOCK
        spare = ((0, LENGTH - stop), (0, 0))
        scores = dot_cols(q_rot[start:stop], k_rot[:stop]) * scale
        probs = jnp.where(causal(start, stop), jnp.exp(scores - lse[start:stop]), 0.0)
        grad_probs = dot_cols(grad_out[start:stop], v_val[:stop])
        grad_scores = (
            probs * (grad_probs - jnp.sum(grad_probs * probs, -1, keepdims=True))
        ).astype(BF)
        grad_query.append(dot_plain(grad_scores, k_rot[:stop]) * scale)
        grad_key = grad_key + jnp.pad(dot_rows(grad_scores, q_rot[start:stop]), spare) * scale
        grad_value = grad_value + jnp.pad(
            dot_rows(probs.astype(BF), grad_out[start:stop]), spare
        )
    return (jnp.concatenate(grad_query, 0), grad_key, grad_value)


def block_forward(hat, weights, cosine, sine):
    w_all, bias, vector = weights
    w_cols, w_rows = w_all[: bias.shape[0]], w_all[bias.shape[0] :]
    wide = hat.astype(F32)
    first_in = (wide * vector[0] + vector[1]).astype(BF)
    second_in = (wide * vector[2] + vector[3]).astype(BF)
    qkv = dot_cols(first_in, w_cols[: 3 * HEAD]) + bias[: 3 * HEAD]
    up_val = dot_cols(second_in, w_cols[3 * HEAD :]) + bias[3 * HEAD :]
    q_rot = rotate(qkv[:, :HEAD], cosine, sine).astype(BF)
    k_rot = rotate(qkv[:, HEAD : 2 * HEAD], cosine, sine).astype(BF)
    v_val = qkv[:, 2 * HEAD :].astype(BF)
    attended, lse = attention_forward(q_rot, k_rot, v_val)
    attended = attended.astype(BF)
    hidden = jax.nn.gelu(up_val, approximate=False).astype(BF)
    branch = dot_plain(attended, w_rows[:HEAD]) + dot_plain(hidden, w_rows[HEAD:])
    return (
        branch.astype(BF),
        (hat, first_in, second_in, q_rot, k_rot, v_val, lse, attended, up_val, hidden),
    )


def gelu_exact(values):
    return jax.nn.gelu(values, approximate=False)


def block_backward(grad_low, kept, weights, cosine, sine):
    w_all, bias, vector = weights
    w_cols, w_rows = w_all[: bias.shape[0]], w_all[bias.shape[0] :]
    hat, first_in, second_in, q_rot, k_rot, v_val, lse, attended, up_val, hidden = kept
    grad_att = dot_cols(grad_low, w_rows[:HEAD]).astype(BF)
    grad_hidden = dot_cols(grad_low, w_rows[HEAD:])
    grad_up = jax.vjp(gelu_exact, up_val)[1](grad_hidden)[0].astype(BF)
    grad_query, grad_key, grad_value = attention_backward(q_rot, k_rot, v_val, lse, grad_att)
    grad_query = rotate(grad_query, cosine, -sine)
    grad_key = rotate(grad_key, cosine, -sine)
    grad_qkv = jnp.concatenate([grad_query, grad_key, grad_value], 1).astype(BF)
    grad_weights = (
        dot_rows(grad_qkv, first_in).astype(BF),
        dot_rows(grad_up, second_in).astype(BF),
        dot_rows(attended, grad_low).astype(BF),
        dot_rows(hidden, grad_low).astype(BF),
    )
    grad_bias = jnp.concatenate(
        [jnp.sum(grad_qkv.astype(F32), 0), jnp.sum(grad_up.astype(F32), 0)]
    )
    grad_first = dot_plain(grad_qkv, w_cols[: 3 * HEAD])
    grad_second = dot_plain(grad_up, w_cols[3 * HEAD :])
    wide = hat.astype(F32)
    grad_norms = jnp.stack(
        [
            jnp.sum(grad_first * wide, 0),
            jnp.sum(grad_first, 0),
            jnp.sum(grad_second * wide, 0),
            jnp.sum(grad_second, 0),
        ]
    )
    grad_hat = grad_first * vector[0] + grad_second * vector[2]
    return (grad_hat.astype(BF), (grad_weights, grad_bias, grad_norms))


def on_device(
    tokens,
    groups,
    counts,
    domain,
    w_in,
    w_back,
    tables,
    b_in,
    vecs,
    final_norm,
    w_in_mom,
    w_back_mom,
    tables_mom,
    b_in_mom,
    vecs_mom,
    final_mom,
    w_in_ema,
    w_back_ema,
    tables_ema,
    b_in_ema,
    vecs_ema,
    final_ema,
    w_in_err,
    w_back_err,
    tables_err,
    w_in_fac,
    w_back_fac,
    tables_fac,
):
    y, core, z = where_am_i()
    replica = lax.axis_index("xx")
    section = lax.axis_index("yl") * 2 + core
    vocab_part = section * 8 + lax.axis_index("yh") * 4 + z
    shard = core * 4 + z
    seq_rep = tokens.shape[0]
    row_total = seq_rep * LENGTH
    vocab_shard = tables.shape[1]
    own_cols = tables.shape[2]
    cosine, sine = rotary_tables()

    seq_index = jnp.arange(groups.shape[0], dtype=jnp.int32)
    live = seq_index % seq_rep < counts[seq_index // seq_rep]
    domain_hit = groups[:, None] == jnp.arange(domain.shape[0], dtype=jnp.int32)[None, :]
    seq_weight = jnp.where(live, jnp.sum(jnp.where(domain_hit, domain[None, :], 0.0), 1), 0.0)
    weight_total = jnp.sum(seq_weight)
    own_weight = lax.dynamic_slice_in_dim(seq_weight, replica * seq_rep, seq_rep, 0)
    token_ids = tokens[:, :LENGTH].reshape(-1)
    target_ids = tokens[:, 1:].reshape(-1)

    pad_ids = -vocab_shard % 128
    tall = vocab_shard + pad_ids
    short = jnp.pad(
        jnp.transpose(tables.astype(BF), (0, 2, 1)), ((0, 0), (0, 0), (0, pad_ids))
    )
    small = jnp.concatenate(
        [
            jnp.pad(vecs[0], ((0, 2), (0, 0))),
            jnp.pad(b_in, ((0, 7), (0, D - b_in.shape[1]))),
        ]
    )
    sources = (jnp.concatenate([w_in[0].T.astype(BF), w_back[0].astype(BF)]), small)
    err = jnp.transpose(
        tables_err.reshape(2, vocab_shard, D // 128, 128), (1, 2, 0, 3)
    ).reshape(-1, 128)
    embed_t, *packs_0, err = all_features(short[0], 0, sources, err, vocab_shard, tall)
    packs = {0: packs_0}
    head_t = lax.all_gather(short[1], "xx", axis=0, tiled=True)

    def own_ids(ids):
        local = ids - vocab_part * vocab_shard
        inside = (local >= 0) & (local < vocab_shard)
        return jnp.where(inside, local, -1).reshape(16, 1, 2 * BLOCK)

    own_tokens, own_targets = own_ids(token_ids), own_ids(target_ids)
    x, hat = embedded(embed_t.reshape(D, tall), own_tokens)
    head = jnp.transpose(head_t)

    weights, kept, before = [], [], []
    for index in range(LAYERS):
        w_all, rest = packs[index]
        weights.append((w_all, rest[8, : b_in.shape[1]], rest))
        before.append(x)
        branch, keep = block_forward(hat.reshape(LENGTH, D), weights[index], cosine, sine)
        kept.append(keep)
        branch = branch.reshape(8, BLOCK, D)
        if index + 1 < LAYERS:
            hat, x, *packs[index + 1] = next_hat(branch, x, rest, index + 1, sources)

    x, normed, probs, stats, joined = last_and_lse(
        vocab_shard, branch, x, rest, final_norm, head, own_targets
    )
    losses = joined[:, :, 1, :].reshape(seq_rep, LENGTH)
    loss_part = jnp.sum(own_weight * jnp.mean(losses, 1))
    coefs = jnp.broadcast_to(
        (own_weight / (weight_total * LENGTH))[:, None, None], (seq_rep, 1, 2 * BLOCK)
    )
    steep, grad_all, grad, grad_gains = loss_back(
        probs, stats, joined, own_targets, coefs, head_t, x, final_norm
    )
    grad_gains = grad_gains[:2]
    vector_rows = [None] * LAYERS
    grad_table = None
    returned = [None] * LAYERS
    for index in reversed(range(LAYERS)):
        outbias = jnp.sum(grad, 0)[None]
        grad_hat, (w_grad, bias_row, norm_rows) = block_backward(
            grad_all.reshape(LENGTH, D), kept[index], weights[index], cosine, sine
        )
        vector_rows[index] = jnp.concatenate([norm_rows, outbias, outbias], 0)
        w_grad_in, w_grad_out = w_grad[:2], w_grad[2:]
        w_grad = jnp.concatenate(w_grad if index else w_grad_in)
        given = (w_grad, jnp.pad(bias_row[None], ((0, 7), (0, D - bias_row.shape[0]))))
        grad_hat = grad_hat.reshape(8, BLOCK, D)
        if index >= LAYERS - 2:
            parts = (0, 1) if index == LAYERS - 1 else (2, 3)
            grad_all, grad, *returned[index], grad_table = next_grad(
                index, grad_hat, before[index], grad, given, parts, steep, normed, grad_table
            )
        elif index:
            *most, m_head, left_head = next_grad(
                index, grad_hat, before[index], grad, given, begun=grad_table,
                finish=(err, jnp.pad(tables_fac[1].T, ((0, 0), (0, pad_ids)))),
            )
            grad_all, grad, *returned[index] = most
        else:
            grad_embed, *returned[index] = lowest_grad(
                index, grad_hat, before[index], grad, own_tokens, given, tall
            )

    loss_row = jnp.zeros((1, D), F32).at[0, 0].set(jnp.where(shard + y * 8 == 0, loss_part, 0.0))
    vectors = jnp.concatenate(vector_rows + [grad_gains, loss_row], 0)
    vectors = jnp.pad(vectors, ((0, 32 - vectors.shape[0]), (0, 0))).reshape(32, D // 128, 128)
    vectors = jnp.pad(vectors, ((0, 0), (0, 8 - D // 128), (0, 0)))
    facs = (
        w_in_fac[0].T,
        w_back_fac[0].T,
        jnp.pad(tables_fac[0].T, ((0, 0), (0, pad_ids))),
    )
    errs = (w_in_err[0, 0].T, w_back_err[0, 0])
    m_embed, m_layer, basis, own, sums, bias_sum, vector_sums = compressed(
        vocab_shard, grad_embed, m_head, left_head, err, errs, facs, returned,
        jnp.concatenate(w_grad_out), vectors,
    )
    loss_sum = vector_sums[6 * LAYERS + 2, 0, 0]

    def of_tables(arrays):
        return [jnp.transpose(a, (1, 0, 2)).reshape(-1, 128) for a in arrays]

    token_count = lax.axis_size("xx") * seq_rep * LENGTH
    rate_layer = 2.0 * math.sqrt(token_count)
    rate_vector = 6.0 * math.sqrt(token_count)
    rate_tables = [rate * math.sqrt(token_count * VOCAB) for rate in (50.0, 0.5)]
    params = (
        [w_in[0].T, w_in_mom[0].T, w_in_ema[0].T, w_back[0], w_back_mom[0], w_back_ema[0]]
        + of_tables((tables, tables_mom, tables_ema))
        + [b_in, b_in_mom, b_in_ema, vecs[0], vecs_mom[0], vecs_ema[0]]
        + [final_norm, final_mom, final_ema]
    )
    new = updated(
        vocab_shard, (rate_layer, rate_vector, rate_tables), (m_embed, m_head), m_layer,
        basis, own, sums, bias_sum, vector_sums, params,
    )
    err_tab, err_in, err_back, fac_in, fac_back, fac_embed, fac_head = new[18:]
    err_tab = jnp.transpose(
        err_tab.reshape(vocab_shard, D // 128, 2, 128), (2, 0, 1, 3)
    ).reshape(tables_err.shape)
    in_w, in_m, in_e = [a.T[None] for a in new[:3]]
    back_w, back_m, back_e = [a[None] for a in new[3:6]]
    tab_w, tab_m, tab_e = [
        jnp.transpose(a.reshape(vocab_shard, 2, own_cols), (1, 0, 2)) for a in new[6:9]
    ]
    bias_w, bias_m, bias_e = new[9:12]
    vec_w, vec_m, vec_e = [a[None] for a in new[12:15]]
    fin_w, fin_m, fin_e = new[15:18]
    return (
        loss_sum,
        weight_total,
        in_w,
        back_w,
        tab_w,
        bias_w,
        vec_w,
        fin_w,
        in_m,
        back_m,
        tab_m,
        bias_m,
        vec_m,
        fin_m,
        in_e,
        back_e,
        tab_e,
        bias_e,
        vec_e,
        fin_e,
        err_in.T[None, None],
        err_back[None, None],
        err_tab,
        fac_in.T[None],
        fac_back.T[None],
        fac_embed.T,
        fac_head.T,
    )


def solution(mesh):
    fine = Mesh(
        np.asarray(mesh.devices).reshape(2, 2, 2, 4, 4), ("yl", "co", "yh", "zz", "xx")
    )
    names = {"section": ("yl", "co"), "tensor": ("yh", "zz"), "dp": ("xx",)}

    def spec(*axes):
        return P(*[None if a is None else sum((names[n] for n in a.split()), ()) for a in axes])

    layer_in, layer_back = spec("section", None, "tensor"), spec("section", "tensor", None)
    table, bias = spec(None, "section tensor", "dp"), spec("section", "tensor")
    vector = spec("section", None, None)
    params = (layer_in, layer_back, table, bias, vector, P())
    errors = (
        spec("dp", "section", None, "tensor"),
        spec("dp", "section", "tensor", None),
        spec("dp", None, "section tensor", None),
    )
    in_specs = (
        (spec("dp", None), P(), P(), P())
        + params * 3
        + errors
        + (layer_back, layer_back, spec(None, "section tensor", None))
    )
    out_specs = (
        (P(), P())
        + params * 3
        + errors
        + (layer_back, layer_back, spec("section tensor", None), spec("section tensor", None))
    )
    return jax.shard_map(
        on_device, mesh=fine, in_specs=in_specs, out_specs=out_specs, check_vma=False
    )
```
